128 devices in a mesh: dp: 16 (over y_hi, x, core), tensor: 8 (over z, y_lo).
Axes of the slice: x: 4, y: 4 (y_hi: 2, y_lo: 2; y = y_hi * 2 + y_lo), z: 4, core: 2. Of those that a mesh axis runs over, the one named last changes fastest.
Arguments:
- tokens: bfloat16 [32768, 1536], P('dp'), may hold values from -6 to 6
- w_in: bfloat16 [1536, 6144], P(None, 'tensor'), may hold values from -0.15625 to 0.15625
- w_out: bfloat16 [6144, 1536], P('tensor'), may hold values from -0.078125 to 0.078125
- text_emb: bfloat16 [128, 1536], P('dp'), may hold values from -6 to 6
- labels: int32 [128], P('dp'), may hold values from 0 to 127, each once
- logit_scale: float32 [1], replicated, may hold values from 2 to 8
- logit_bias: float32 [1], replicated, may hold values from -1.5 to 0.5
Outputs:
- token_grad: bfloat16 [32768, 1536], P('dp', 'tensor')
- w_in_grad: bfloat16 [1536, 6144], P('dp', 'tensor')
- w_out_grad: bfloat16 [6144, 1536], P('tensor', 'dp')
- text_grad: bfloat16 [128, 1536], P('dp')
The draws below stay inside these ranges and needn't reach their ends.
Inputs may be any that keep to these rules, and one draw needn't show every extreme that they name: `labels`: each text index appears exactly once.
All inputs are finite; a program needn't handle non-finite values.
Results may differ from the reference program's by a relative error of at most 0.015.
Values may be sent and summed in bfloat16 or wider, within the bound.
A program may use at most 128 MiB of HBM per device.

```python
import math
import jax
import jax.numpy as jnp
from jax import lax

D = 1536
FF = 6144
TOKS = 256
IMG_DEV = 8
IMAGES = 128
ALL_ROWS = 32768
N_TENSOR = 8


def spiked(array, rng, source, target, blocks, factor):
    owner, partner = [(jnp.arange(array.shape[dim]) // (array.shape[dim] // blocks)).reshape([-1 if axis == dim else 1 for axis in range(array.ndim)]) for dim in (source, target)]
    chosen = jax.random.permutation(rng, blocks)[partner]
    strong = (owner == chosen) | (owner == (partner + blocks // 2) % blocks)
    return jnp.where(strong, factor * array, array)


def level_of(stream_key, shape, cuts, least, top_value):
    level, own = 1.0, jax.random.fold_in(stream_key, 6)
    for dim, shards_of in cuts:
        draws = jnp.exp(jax.random.uniform(jax.random.fold_in(own, dim), (shards_of,), jnp.float32, least / len(cuts), top_value / len(cuts)))
        level = level * jnp.repeat(draws, shape[dim] // shards_of).reshape([-1 if axis == dim else 1 for axis in range(len(shape))])
    return level


def gaussian(own_key, dims, scale, bound, cuts=(), kind=jnp.bfloat16):
    drawn = scale * jax.random.normal(own_key, dims, jnp.float32)
    if cuts:
        drawn = drawn * level_of(own_key, dims, cuts, -0.22, 0.18)
    return jnp.clip(drawn, -bound, bound).astype(kind)


def heavy_noise(key, extent, scale, limit, shards, heavy, kind=jnp.bfloat16):
    drawn = scale * jax.random.normal(key, extent, jnp.float32)
    if shards:
        drawn = drawn * level_of(key, extent, shards, -0.22, 0.18)
    return jnp.clip(spiked(drawn, jax.random.fold_in(key, 3), *heavy), -limit, limit).astype(kind)


def setup_inputs(seed: int = 0) -> dict:
    keys = jax.random.split(jax.random.key(seed), 8)
    tokens = heavy_noise(keys[0], (ALL_ROWS, D), 1.0, 6.0, ((0, 16),), (0, 1, 16, 2.0))
    w_in = gaussian(keys[1], (D, FF), D ** -0.5, 0.15625, ((1, 8),))
    w_out = gaussian(keys[2], (FF, D), FF ** -0.5, 0.078125, ((0, 8),))
    text_emb = gaussian(keys[3], (IMAGES, D), 1.0, 6.0, ((0, 16),))
    labels = jax.random.permutation(keys[4], IMAGES).astype(jnp.int32)
    logit_scale = jnp.clip(jnp.exp(jax.random.uniform(keys[5], (1,), jnp.float32, math.log(2.0), math.log(8.0))), 2.0, 8.0)
    logit_bias = jnp.clip(jax.random.uniform(keys[6], (1,), jnp.float32, -1.5, 0.5), -1.5, 0.5)
    return dict(tokens=tokens, w_in=w_in, w_out=w_out, text_emb=text_emb, labels=labels, logit_scale=logit_scale, logit_bias=logit_bias)


loss_scale = 8192.0
norm_eps = 1e-06

def layer_stats(block):
    values = block.astype(jnp.float32)
    center = values - lax.optimization_barrier(jnp.mean(values, axis=1, keepdims=True))
    inv_std = lax.rsqrt(lax.optimization_barrier(jnp.mean(center * center, axis=1, keepdims=True)) + norm_eps)
    return (center * inv_std, inv_std)

def pooled_hidden(block, w_in):
    normed, inv_std = layer_stats(block)
    normed_bf = normed.astype(jnp.bfloat16)
    hidden_pre = jnp.dot(normed_bf, w_in, preferred_element_type=jnp.float32)
    return lax.optimization_barrier(jnp.mean(jax.nn.gelu(hidden_pre).reshape(-1, TOKS, hidden_pre.shape[1]), axis=1))

def sig_grads(image_bf, text_bf, match, logit_scale, logit_bias, count):
    logits = logit_scale[0] * jnp.dot(image_bf, text_bf.T, preferred_element_type=jnp.float32) + logit_bias[0]
    signs = jnp.where(match, 1.0, -1.0).astype(logits.dtype)
    grad_logit = -signs * jax.nn.sigmoid(-signs * logits) * (loss_scale / count)
    return grad_logit.astype(jnp.bfloat16)

def reference(tokens, w_in, w_out, text_emb, labels, logit_scale, logit_bias):
    groups = IMAGES // IMG_DEV
    block_rows = IMG_DEV * TOKS
    token_blocks = tokens.reshape(groups, block_rows, D)
    pooled = lax.map(lambda blk: pooled_hidden(blk, w_in), token_blocks).reshape(IMAGES, FF)
    pooled_bf = pooled.astype(jnp.bfloat16)
    token_mean = lax.optimization_barrier(jnp.mean(tokens.astype(jnp.float32).reshape(IMAGES, TOKS, D), axis=1))
    embedding = token_mean + jnp.dot(pooled_bf, w_out, preferred_element_type=jnp.float32)
    emb_inv = lax.rsqrt(lax.optimization_barrier(jnp.sum(embedding * embedding, axis=1, keepdims=True)) + norm_eps)
    image_bf = (embedding * emb_inv).astype(jnp.bfloat16)
    text_vals = text_emb.astype(jnp.float32)
    text_inv = lax.rsqrt(lax.optimization_barrier(jnp.sum(text_vals * text_vals, axis=1, keepdims=True)) + norm_eps)
    text_bf = (text_vals * text_inv).astype(jnp.bfloat16)
    match = labels[:, None] == jnp.arange(IMAGES, dtype=jnp.int32)[None, :]
    grad_bf = sig_grads(image_bf, text_bf, match, logit_scale, logit_bias, IMAGES)
    image_dir = logit_scale[0] * jnp.dot(grad_bf, text_bf, preferred_element_type=jnp.float32)
    text_dir = logit_scale[0] * jnp.dot(grad_bf.T, image_bf, preferred_element_type=jnp.float32)
    emb_grad = emb_inv * image_dir - emb_inv ** 3 * embedding * lax.optimization_barrier(jnp.sum(embedding * image_dir, axis=1, keepdims=True))
    text_grad = (text_inv * text_dir - text_inv ** 3 * text_vals * lax.optimization_barrier(jnp.sum(text_vals * text_dir, axis=1, keepdims=True))).astype(jnp.bfloat16)
    emb_grad_bf = emb_grad.astype(jnp.bfloat16)
    pooled_grad = jnp.dot(emb_grad_bf, w_out.T, preferred_element_type=jnp.float32)
    w_out_grad = jnp.dot(pooled_bf.T, emb_grad_bf, preferred_element_type=jnp.float32).astype(jnp.bfloat16)
    group_width = FF // N_TENSOR

    def backward(carry, inputs):
        block, pool_grad_blk, emb_grad_blk = inputs
        normed, inv_std = layer_stats(block)
        normed_bf = normed.astype(jnp.bfloat16)
        hidden_pre = jnp.dot(normed_bf, w_in, preferred_element_type=jnp.float32)
        spread = jnp.broadcast_to((pool_grad_blk / TOKS)[:, None, :], (IMG_DEV, TOKS, FF)).reshape(block_rows, FF)
        hidden_grad = jax.vjp(jax.nn.gelu, hidden_pre)[1](spread)[0].astype(jnp.bfloat16)
        carry = carry + jnp.dot(normed_bf.T, hidden_grad, preferred_element_type=jnp.float32)
        pieces = jnp.einsum('rkf,dkf->rkd', hidden_grad.reshape(block_rows, N_TENSOR, group_width).astype(jnp.float32), w_in.reshape(D, N_TENSOR, group_width).astype(jnp.float32))
        pieces = lax.optimization_barrier(pieces.astype(jnp.bfloat16)).astype(jnp.float32)
        normed_grad = lax.optimization_barrier(jnp.sum(pieces, axis=1))
        token_grad = inv_std * (normed_grad - lax.optimization_barrier(jnp.mean(normed_grad, axis=1, keepdims=True)) - normed * lax.optimization_barrier(jnp.mean(normed_grad * normed, axis=1, keepdims=True)))
        token_grad = token_grad + jnp.broadcast_to((emb_grad_blk / TOKS)[:, None, :], (IMG_DEV, TOKS, D)).reshape(block_rows, D)
        return (carry, token_grad.astype(jnp.bfloat16))
    w_acc, token_grads = lax.scan(backward, jnp.zeros((D, FF), jnp.float32), (token_blocks, pooled_grad.reshape(groups, IMG_DEV, FF), emb_grad.reshape(groups, IMG_DEV, D)))
    return (token_grads.reshape(IMAGES * TOKS, D), w_acc.astype(jnp.bfloat16), w_out_grad, text_grad)
```

```python
import math

import jax
import jax.numpy as jnp
from jax import lax
from jax.experimental import pallas as pl
from jax.experimental.pallas import tpu as pltpu
from jax.sharding import PartitionSpec as P

F32 = jnp.float32
BF16 = jnp.bfloat16

D = 1536
HALF = D // 2
HID = 768
ROWS = 2048
TOKS = 256
IMGS = 8
LOSS_SCALE = 64.0
EPS = 1e-06
GELU_A = math.sqrt(2.0 / math.pi)
GELU_B = 0.044715

PAIR_FIRST = 3
CHUNKS = 8

NN = (((1,), (0,)), ((), ()))
NT = (((1,), (1,)), ((), ()))
TN = (((0,), (0,)), ((), ()))


def dot(a, b, dims=NN):
    return lax.dot_general(a, b, dims, preferred_element_type=F32)


def kernel(
    tokens_hbm, w_in_hbm, w_out_hbm, text_ref, labels_ref, scale_ref, bias_ref,
    out_ref, win_ref, wout_ref, tgrad_ref,
    tok, inv, hpre, hg, nt, w_in, w_out,
    tmean, pooled, pgs, egs, ones_cs, part, part2, tdir,
    texts, ebuf, msgs,
    q, ra, rb, sa, sb, yr, yq,
    g, gc, gx, gra, grb, gsa, gsb, gyr,
    tok_sem, w_sem,
    text_ss, text_rs, emb_ss, emb_rs, msg_ss, msg_rs,
    q_ss, q_rs, g_ss, g_rs,
):
    dp = lax.axis_index("dp")
    tp = lax.axis_index("tensor")
    yh, local = dp // 8, dp % 8
    x, core = local // 2, dp % 2
    z, y = tp // 2, tp % 2

    def mesh_z(step):
        return (dp, ((z + step) % 4) * 2 + y)

    def mesh_x(step):
        return (yh * 8 + ((x + step) % 4) * 2 + core, tp)

    y_pair = (dp, z * 2 + (1 - y))
    core_pair = (dp - core + (1 - core), tp)
    y_far = ((1 - yh) * 8 + local, tp)

    def octet(k):
        return (yh * 8 + (local + k) % 8, tp)

    def remote(src, dst, ssem, rsem, dev):
        return pltpu.make_async_remote_copy(
            src_ref=src, dst_ref=dst, send_sem=ssem, recv_sem=rsem,
            device_id=dev, device_id_type=pl.DeviceIdType.MESH,
        )

    def tok_copy(c):
        rows = pl.ds(c * TOKS, TOKS)
        return pltpu.make_async_copy(tokens_hbm.at[rows], tok.at[rows], tok_sem.at[c])

    tok_copy(0).start()
    w_in_copy = pltpu.make_async_copy(w_in_hbm, w_in, w_sem.at[0])
    w_out_copy = pltpu.make_async_copy(w_out_hbm, w_out, w_sem.at[1])
    w_in_copy.start()

    @pl.loop(1, CHUNKS)
    def _(c):
        tok_copy(c).start()

    w_out_copy.start()

    barrier = pltpu.get_barrier_semaphore()

    def greet(dev):
        pl.semaphore_signal(barrier, inc=1, device_id=dev, device_id_type=pl.DeviceIdType.MESH)

    greet(y_far)
    for k in range(1, 8):
        greet(octet(k))
        greet((dp, (tp + k) % 8))

    text_vals = text_ref[...].astype(F32)
    text_inv = lax.rsqrt(jnp.sum(text_vals * text_vals, axis=1, keepdims=True) + EPS)
    text_nrm = text_vals * text_inv
    texts[dp] = jnp.concatenate([text_nrm[:, :HALF], text_nrm[:, HALF:]], axis=0).astype(BF16)

    pl.semaphore_wait(barrier, 15)

    def gather_send(buf, slot, ss, rs, row):
        @pl.loop(1, 8)
        def _(k):
            remote(buf.at[slot], buf.at[slot], ss.at[row, k], rs.at[slot], octet(k)).start()

    def gather_far(buf, ss, rs):
        return remote(buf.at[dp], buf.at[dp], ss.at[0, 0], rs.at[dp], y_far)

    def gather_recv(buf, slot, ss, rs):
        remote(buf.at[slot], buf.at[slot], ss.at[0, 0], rs.at[slot], y_far).wait_recv()

    def gather_first(buf, ss, rs):
        gather_far(buf, ss, rs).start()
        gather_send(buf, dp, ss, rs, 0)

    far_slot = (1 - yh) * 8 + local

    def gather_relay(buf, ss, rs):
        gather_recv(buf, far_slot, ss, rs)
        gather_send(buf, far_slot, ss, rs, 1)

    def gather_rest(buf, ss, rs):
        @pl.loop(1, 8)
        def _(k):
            gather_recv(buf, yh * 8 + (local + k) % 8, ss, rs)
            gather_recv(buf, (1 - yh) * 8 + (local + k) % 8, ss, rs)

    def gather_sent(buf, ss, rs):
        gather_far(buf, ss, rs).wait_send()

        @pl.loop(1, 8)
        def _(k):
            for row in range(2):
                remote(buf.at[dp], buf.at[dp], ss.at[row, k], rs.at[dp], octet(k)).wait_send()

    gather_first(texts, text_ss, text_rs)

    w_in_copy.wait()

    @pl.loop(0, CHUNKS)
    def _(c):
        tok_copy(c).wait()

        def norm_rows(b, acc):
            rows = pl.ds(pl.multiple_of(c * TOKS + b * 32, 32), 32)
            vals = tok[rows, :].astype(F32)
            mean = jnp.sum(vals, axis=1, keepdims=True) * (1.0 / D)
            center = vals - mean
            var = jnp.sum(center * center, axis=1, keepdims=True) * (1.0 / D)
            scale = lax.rsqrt(var + EPS)
            tok[rows, :] = (center * scale).astype(BF16)
            inv[rows, :] = scale
            return acc + jnp.sum(vals.reshape(4, 8, D), axis=0)

        acc = lax.fori_loop(0, 8, norm_rows, jnp.zeros((8, D), F32))
        tmean[pl.ds(c, 1), :] = jnp.sum(acc, axis=0, keepdims=True) * (1.0 / TOKS)
        rows = pl.ds(pl.multiple_of(c * TOKS, TOKS), TOKS)
        hpre[rows, :] = dot(tok[rows, :], w_in[...])

        def pool_rows(b, acc):
            h = hpre[pl.ds(pl.multiple_of(c * TOKS + b * 32, 32), 32), :]
            t = jnp.tanh(GELU_A * (h + GELU_B * (h * h * h)))
            return acc + jnp.sum((0.5 * h * (1.0 + t)).reshape(4, 8, HID), axis=0)

        acc = lax.fori_loop(0, 8, pool_rows, jnp.zeros((8, HID), F32))
        pooled[pl.ds(c, 1), :] = jnp.sum(acc, axis=0, keepdims=True) * (1.0 / TOKS)

    w_out_copy.wait()
    pooled_bf = pooled[...].astype(BF16)
    part_emb = dot(pooled_bf, w_out[...])
    ebuf[tp] = jnp.concatenate([part_emb[:, :HALF], part_emb[:, HALF:]], axis=0).astype(BF16)

    def emb_copy(k):
        return remote(ebuf.at[tp], ebuf.at[tp], emb_ss.at[k], emb_rs.at[tp], (dp, (tp + k) % 8))

    @pl.loop(1, 8)
    def _(k):
        emb_copy(k).start()

    gather_relay(texts, text_ss, text_rs)

    @pl.loop(0, CHUNKS)
    def _(c):
        rows = pl.ds(pl.multiple_of(c * TOKS, TOKS), TOKS)
        nt[:, rows] = tok[rows, :].T

    def col_sum(b, acc):
        vals = w_in[pl.ds(pl.multiple_of(b * 32, 32), 32), :].astype(F32)
        return acc + jnp.sum(vals.reshape(4, 8, HID), axis=0)

    acc = lax.fori_loop(0, D // 32, col_sum, jnp.zeros((8, HID), F32))
    ones_cs[...] = jnp.sum(acc, axis=0, keepdims=True) * (1.0 / D)

    @pl.loop(1, 8)
    def _(k):
        src = (tp + k) % 8
        remote(ebuf.at[src], ebuf.at[src], emb_ss.at[k], emb_rs.at[src], (dp, src)).wait_recv()

    tm = tmean[...]
    emb = jnp.concatenate([tm[:, :HALF], tm[:, HALF:]], axis=0)
    for k in range(8):
        emb = emb + ebuf[k].astype(F32)

    def both(sums):
        total = sums[:IMGS] + sums[IMGS:]
        return jnp.concatenate([total, total], axis=0)

    emb_inv = lax.rsqrt(both(jnp.sum(emb * emb, axis=1, keepdims=True)) + EPS)
    image_bf = (emb * emb_inv).astype(BF16)

    gather_rest(texts, text_ss, text_rs)
    text_all = texts[...].reshape(256, HALF)
    prod = dot(image_bf, text_all, NT)
    scale = scale_ref[0]
    logits = scale * (prod[:IMGS] + pltpu.roll(prod[IMGS:], 256 - IMGS, 1)) + bias_ref[0]
    lane = lax.broadcasted_iota(jnp.int32, (IMGS, 256), 1)
    row = lax.broadcasted_iota(jnp.int32, (IMGS, 256), 0)
    valid = (lane % 16) < 8
    text_id = (lane // 16) * 8 + lane % 16
    label = jnp.zeros((IMGS, 256), jnp.int32)
    for k in range(IMGS):
        label = jnp.where(row == k, labels_ref[k], label)
    signs = jnp.where(label == text_id, 1.0, -1.0)
    grad = -signs * jax.nn.sigmoid(-signs * logits) * LOSS_SCALE
    grad = jnp.where(valid, grad, 0.0)
    grad = jnp.concatenate([grad, pltpu.roll(grad, IMGS, 1)], axis=0).astype(BF16)
    image_dir = scale * dot(grad, text_all)
    emb_grad = emb_inv * image_dir - (emb_inv * emb_inv * emb_inv) * emb * both(
        jnp.sum(emb * image_dir, axis=1, keepdims=True)
    )
    egs[...] = emb_grad * (1.0 / TOKS)
    eg_bf = emb_grad.astype(BF16)
    pgs[...] = (
        dot(eg_bf[:IMGS], w_out[:, :HALF], NT) + dot(eg_bf[IMGS:], w_out[:, HALF:], NT)
    ) * (1.0 / TOKS)

    msgs[dp, :, 0:HALF] = image_bf
    msgs[dp, :, HALF:D] = eg_bf
    pooled_f = pooled[...]
    msgs[dp, :, D:D + HID] = jnp.concatenate([pooled_f, pooled_f], axis=0).astype(BF16)
    msgs[dp, :, D + HID:D + HID + 256] = grad

    def hidden_chunk(c):
        pg = pgs[pl.ds(c, 1), :]
        cs = ones_cs[...]

        @pl.loop(0, 8)
        def _(b):
            rows = pl.ds(pl.multiple_of(c * TOKS + b * 32, 32), 32)
            h = hpre[rows, :]
            h2 = h * h
            t = jnp.tanh(GELU_A * (h + GELU_B * (h2 * h)))
            slope = 0.5 * (1.0 + t) + (0.5 * GELU_A) * h * (1.0 - t * t) * (
                1.0 + (3.0 * GELU_B) * h2
            )
            grad_bf = (slope * pg).astype(BF16)
            hg[rows, :] = grad_bf
            grad_h = grad_bf.astype(F32)
            p1 = grad_h * cs
            p2 = grad_h * h
            s1 = p1[:, 0:128]
            s2 = p2[:, 0:128]
            for i in range(1, HID // 128):
                s1 = s1 + p1[:, i * 128:(i + 1) * 128]
                s2 = s2 + p2[:, i * 128:(i + 1) * 128]
            own = pl.ds(pl.multiple_of(b * 32, 32), 32)
            part[own, :] = s1
            part2[own, :] = s2

        m1 = jnp.sum(part[...].T, axis=0, keepdims=True)
        m2 = jnp.sum(part2[...].T, axis=0, keepdims=True) * (1.0 / D)
        rows = pl.ds(pl.multiple_of(c * TOKS, TOKS), TOKS)
        hgc = hg[rows, :]

        @pl.loop(0, 4)
        def _(zb):
            feats = pl.ds(pl.multiple_of(zb * 384, 384), 384)
            block = dot(w_in[feats, :], hgc, NT) - m1 - nt[feats, rows].astype(F32) * m2
            block = block.astype(BF16)
            q[c, zb, 0] = block[:192]
            q[c, zb, 1] = block[192:]

    zp, zn, zo = (z + 1) % 4, (z + 3) % 4, (z + 2) % 4
    up, down = mesh_z(1), mesh_z(3)
    lo, hi = pl.ds(0, 96), pl.ds(96, 96)

    def pair_copy(c):
        return remote(q.at[c, :, 1 - y], yq.at[c], q_ss.at[c, 0], q_rs.at[c, 0], y_pair)

    def pair_ring1(c):
        return (
            remote(q.at[c, zo, y, lo], ra.at[c, lo], q_ss.at[c, 1], q_rs.at[c, 1], up),
            remote(q.at[c, zo, y, hi], rb.at[c, lo], q_ss.at[c, 2], q_rs.at[c, 2], down),
            remote(q.at[c, zp, y, hi], sa.at[c, 0, hi], q_ss.at[c, 3], q_rs.at[c, 3], up),
            remote(q.at[c, zn, y, lo], sb.at[c, 0, lo], q_ss.at[c, 4], q_rs.at[c, 4], down),
        )

    def pair_ring2(c):
        return (
            remote(q.at[c, zp, y, lo], sa.at[c, 0, lo], q_ss.at[c, 5], q_rs.at[c, 5], up),
            remote(q.at[c, zn, y, hi], sb.at[c, 0, hi], q_ss.at[c, 6], q_rs.at[c, 6], down),
        )

    def ring1(c):
        return (
            remote(q.at[c, zo, 0], ra.at[c], q_ss.at[c, 1], q_rs.at[c, 1], up),
            remote(q.at[c, zo, 1], rb.at[c], q_ss.at[c, 2], q_rs.at[c, 2], down),
            remote(q.at[c, zp, 1], sa.at[c, 1], q_ss.at[c, 3], q_rs.at[c, 3], up),
            remote(q.at[c, zn, 0], sb.at[c, 0], q_ss.at[c, 4], q_rs.at[c, 4], down),
        )

    def ring2(c):
        return (
            remote(q.at[c, zp, 0], sa.at[c, 0], q_ss.at[c, 5], q_rs.at[c, 5], up),
            remote(q.at[c, zn, 1], sb.at[c, 1], q_ss.at[c, 6], q_rs.at[c, 6], down),
        )

    def ring_pair(c):
        return remote(q.at[c, z, 1 - y], yr.at[c], q_ss.at[c, 0], q_rs.at[c, 0], y_pair)

    @pl.loop(0, PAIR_FIRST)
    def _(c):
        hidden_chunk(c)
        pair_copy(c).start()

    @pl.loop(PAIR_FIRST, CHUNKS)
    def _(c):
        hidden_chunk(c)
        for copy in ring1(c):
            copy.start()

    gather_first(msgs, msg_ss, msg_rs)

    @pl.loop(0, 4)
    def _(i):
        feats = pl.ds(pl.multiple_of(i * 384, 384), 384)
        block = dot(nt[feats, :], hg[...]).astype(BF16)
        for k in range(4):
            g[i, k // 2, k % 2] = block[k * 96:(k + 1) * 96]

    core_copy = remote(g.at[:, :, 1 - core], gc, g_ss.at[0], g_rs.at[0], core_pair)
    core_copy.start()

    def add_into(dst, a, b):
        dst[...] = (a[...].astype(F32) + b[...].astype(F32)).astype(BF16)

    @pl.loop(0, PAIR_FIRST)
    def _(c):
        pair_copy(c).wait_recv()
        for zb in range(4):
            blk = q.at[c, zb, y]
            add_into(blk, blk, yq.at[c, zb])
        for copy in pair_ring1(c):
            copy.start()

    core_copy.wait_recv()

    @pl.loop(0, 8)
    def _(k):
        xb, yb = k // 2, k % 2
        i, j = yb * 2 + xb // 2, xb % 2
        add_into(gx.at[xb, yb], g.at[i, j, core], gc.at[i, j])

    xp, xn, xo = (x + 1) % 4, (x + 3) % 4, (x + 2) % 4
    right, left = mesh_x(1), mesh_x(3)
    g1a = remote(gx.at[xo, 0], gra, g_ss.at[1], g_rs.at[1], right)
    g1b = remote(gx.at[xo, 1], grb, g_ss.at[2], g_rs.at[2], left)
    g2a = remote(gx.at[xp], gsa, g_ss.at[3], g_rs.at[3], right)
    g2b = remote(gx.at[xn], gsb, g_ss.at[4], g_rs.at[4], left)
    g3 = remote(gx.at[x, 1 - yh], gyr, g_ss.at[5], g_rs.at[5], y_far)
    g1a.start()
    g1b.start()

    gather_relay(msgs, msg_ss, msg_rs)

    @pl.loop(PAIR_FIRST, CHUNKS)
    def _(c):
        first, second = ring1(c)[:2]
        first.wait_recv()
        blk = q.at[c, zp, 0]
        add_into(blk, blk, ra.at[c])
        second.wait_recv()
        blk = q.at[c, zn, 1]
        add_into(blk, blk, rb.at[c])
        for copy in ring2(c):
            copy.start()

    g1a.wait_recv()
    add_into(gx.at[xp, 0], gx.at[xp, 0], gra)
    g1b.wait_recv()
    add_into(gx.at[xn, 1], gx.at[xn, 1], grb)
    g2a.start()
    g2b.start()

    @pl.loop(0, PAIR_FIRST)
    def _(c):
        first, second = pair_ring1(c)[:2]
        first.wait_recv()
        blk = q.at[c, zp, y, lo]
        add_into(blk, blk, ra.at[c, lo])
        second.wait_recv()
        blk = q.at[c, zn, y, hi]
        add_into(blk, blk, rb.at[c, lo])
        for copy in pair_ring2(c):
            copy.start()

    gather_rest(msgs, msg_ss, msg_rs)
    all_msgs = msgs[...].reshape(256, D + HID + 256)
    tdir[...] = dot(all_msgs[:, D + HID:], all_msgs[:, :HALF], TN)
    text_dir = scale * tdir[pl.ds(pl.multiple_of(dp * 16, 16), 16), :]
    text_dir = jnp.concatenate([text_dir[:IMGS], text_dir[IMGS:]], axis=1)
    tgrad_ref[...] = (
        text_inv * text_dir
        - (text_inv * text_inv * text_inv) * text_vals
        * jnp.sum(text_vals * text_dir, axis=1, keepdims=True)
    ).astype(BF16)
    feat = lax.broadcasted_iota(jnp.int32, (HALF, 128), 0)
    col = lax.broadcasted_iota(jnp.int32, (HALF, 128), 1)
    pick = jnp.where(feat == col + local * 96, 1.0, 0.0).astype(BF16)
    emb_cols = dot(all_msgs[:, HALF:D], pick)
    slot_row = lax.broadcasted_iota(jnp.int32, (256, 128), 0)
    emb_cols = jnp.where((slot_row // 8) % 2 == yh, emb_cols, 0.0).astype(BF16)
    wout_ref[...] = dot(all_msgs[:, D:D + HID], emb_cols, TN)[:, :96].astype(BF16)

    @pl.loop(PAIR_FIRST, CHUNKS)
    def _(c):
        for copy in ring1(c)[2:] + ring2(c):
            copy.wait_recv()
        for half in range(2):
            blk = q.at[c, z, half]
            blk[...] = (
                blk[...].astype(F32) + sa[c, half].astype(F32) + sb[c, half].astype(F32)
            ).astype(BF16)
        ring_pair(c).start()

    g2a.wait_recv()
    g2b.wait_recv()
    for half in range(2):
        blk = gx.at[x, half]
        blk[...] = (
            blk[...].astype(F32) + gsa[half].astype(F32) + gsb[half].astype(F32)
        ).astype(BF16)
    g3.start()

    eg_cols = egs[pl.ds(pl.multiple_of((z // 2) * 8, 8), 8),
                  pl.ds(pl.multiple_of((z % 2) * 384, 128), 384)]
    eg_cols = jnp.where(y == 0, eg_cols[:, :192], eg_cols[:, 192:])
    tdir[0:8, 0:192] = eg_cols

    def finish(c, total):
        rows = pl.ds(pl.multiple_of(c * TOKS, TOKS), TOKS)
        square = jnp.concatenate([total, jnp.zeros((64, 256), F32)], axis=0).T
        out_ref[rows, :] = (
            inv[rows, :] * square[:, :192] + tdir[pl.ds(c, 1), 0:192]
        ).astype(BF16)

    @pl.loop(0, PAIR_FIRST)
    def _(c):
        for copy in pair_ring1(c)[2:] + pair_ring2(c):
            copy.wait_recv()
        finish(c, q[c, z, y].astype(F32) + sa[c, 0].astype(F32) + sb[c, 0].astype(F32))

    @pl.loop(PAIR_FIRST, CHUNKS)
    def _(c):
        ring_pair(c).wait_recv()
        finish(c, q[c, z, y].astype(F32) + yr[c].astype(F32))

    g3.wait_recv()
    win_ref[...] = (gx[x, yh].astype(F32) + gyr[...].astype(F32)).astype(BF16)

    @pl.loop(0, PAIR_FIRST)
    def _(c):
        pair_copy(c).wait_send()
        for copy in pair_ring1(c) + pair_ring2(c):
            copy.wait_send()

    @pl.loop(PAIR_FIRST, CHUNKS)
    def _(c):
        ring_pair(c).wait_send()
        for copy in ring1(c) + ring2(c):
            copy.wait_send()

    for copy in (core_copy, g1a, g1b, g2a, g2b, g3):
        copy.wait_send()

    @pl.loop(1, 8)
    def _(k):
        emb_copy(k).wait_send()

    gather_sent(texts, text_ss, text_rs)
    gather_sent(msgs, msg_ss, msg_rs)


def body(tokens, w_in, w_out, text_emb, labels, logit_scale, logit_bias):
    vmem = pl.BlockSpec(memory_space=pltpu.VMEM)
    smem = pl.BlockSpec(memory_space=pltpu.SMEM)
    hbm = pl.BlockSpec(memory_space=pl.ANY)
    msg = D + HID + 256
    scratch = [
        pltpu.VMEM((ROWS, D), BF16),
        pltpu.VMEM((ROWS, 1), F32),
        pltpu.VMEM((ROWS, HID), F32),
        pltpu.VMEM((ROWS, HID), BF16),
        pltpu.VMEM((D, ROWS), BF16),
        pltpu.VMEM((D, HID), BF16),
        pltpu.VMEM((HID, D), BF16),
        pltpu.VMEM((IMGS, D), F32),
        pltpu.VMEM((IMGS, HID), F32),
        pltpu.VMEM((IMGS, HID), F32),
        pltpu.VMEM((16, HALF), F32),
        pltpu.VMEM((1, HID), F32),
        pltpu.VMEM((TOKS, 128), F32),
        pltpu.VMEM((TOKS, 128), F32),
        pltpu.VMEM((256, HALF), F32),
        pltpu.VMEM((16, 16, HALF), BF16),
        pltpu.VMEM((8, 16, HALF), BF16),
        pltpu.VMEM((16, 16, msg), BF16),
        pltpu.VMEM((CHUNKS, 4, 2, 192, TOKS), BF16),
        pltpu.VMEM((CHUNKS, 192, TOKS), BF16),
        pltpu.VMEM((CHUNKS, 192, TOKS), BF16),
        pltpu.VMEM((CHUNKS, 2, 192, TOKS), BF16),
        pltpu.VMEM((CHUNKS, 2, 192, TOKS), BF16),
        pltpu.VMEM((CHUNKS, 192, TOKS), BF16),
        pltpu.VMEM((max(PAIR_FIRST, 1), 4, 192, TOKS), BF16),
        pltpu.VMEM((4, 2, 2, 96, HID), BF16),
        pltpu.VMEM((4, 2, 96, HID), BF16),
        pltpu.VMEM((4, 2, 96, HID), BF16),
        pltpu.VMEM((96, HID), BF16),
        pltpu.VMEM((96, HID), BF16),
        pltpu.VMEM((2, 96, HID), BF16),
        pltpu.VMEM((2, 96, HID), BF16),
        pltpu.VMEM((96, HID), BF16),
        pltpu.SemaphoreType.DMA((CHUNKS,)),
        pltpu.SemaphoreType.DMA((2,)),
        pltpu.SemaphoreType.DMA((2, 8)),
        pltpu.SemaphoreType.DMA((16,)),
        pltpu.SemaphoreType.DMA((8,)),
        pltpu.SemaphoreType.DMA((8,)),
        pltpu.SemaphoreType.DMA((2, 8)),
        pltpu.SemaphoreType.DMA((16,)),
        pltpu.SemaphoreType.DMA((CHUNKS, 7)),
        pltpu.SemaphoreType.DMA((CHUNKS, 7)),
        pltpu.SemaphoreType.DMA((6,)),
        pltpu.SemaphoreType.DMA((6,)),
    ]
    return pl.pallas_call(
        kernel,
        out_shape=(
            jax.ShapeDtypeStruct((ROWS, D // 8), BF16),
            jax.ShapeDtypeStruct((D // 16, HID), BF16),
            jax.ShapeDtypeStruct((HID, D // 16), BF16),
            jax.ShapeDtypeStruct((IMGS, D), BF16),
        ),
        in_specs=[hbm, hbm, hbm, vmem, smem, smem, smem],
        out_specs=(vmem, vmem, vmem, vmem),
        scratch_shapes=scratch,
        compiler_params=pltpu.CompilerParams(
            collective_id=0, has_side_effects=True, vmem_limit_bytes=61 * 2**20
        ),
        cost_estimate=pl.CostEstimate(
            flops=6 * ROWS * D * HID, bytes_accessed=14 * 2**20, transcendentals=2 * ROWS * HID
        ),
    )(tokens, w_in, w_out, text_emb, labels, logit_scale, logit_bias)


def solution(mesh):
    in_specs = (
        P("dp", None),
        P(None, "tensor"),
        P("tensor", None),
        P("dp", None),
        P("dp"),
        P(),
        P(),
    )
    out_specs = (P("dp", "tensor"), P("dp", "tensor"), P("tensor", "dp"), P("dp", None))
    return jax.shard_map(body, mesh=mesh, in_specs=in_specs, out_specs=out_specs, check_vma=False)
```

```python
import math

import jax
import jax.numpy as jnp
from jax import lax
from jax.experimental import pallas as pl
from jax.experimental.pallas import tpu as pltpu
from jax.sharding import PartitionSpec as P

F32 = jnp.float32
BF16 = jnp.bfloat16

D = 1536
HALF = D // 2
HID = 768
ROWS = 2048
TOKS = 256
IMGS = 8
LOSS_SCALE = 64.0
EPS = 1e-06
GELU_A = math.sqrt(2.0 / math.pi)
GELU_B = 0.044715

CHUNKS = 8
GROUPS = ((0, 4), (4, 8))
PAIR_FIRST = (1, 3, 5)

NN = (((1,), (0,)), ((), ()))
NT = (((1,), (1,)), ((), ()))
TN = (((0,), (0,)), ((), ()))


def dot(a, b, dims=NN):
    return lax.dot_general(a, b, dims, preferred_element_type=F32)


def kernel(
    tokens_hbm, w_in_hbm, w_out_hbm, text_ref, labels_ref, scale_ref, bias_ref,
    out_hbm, win_hbm, wout_hbm, tgrad_hbm,
    tok, inv, minv, hpre, hg, nt, w_in, w_out,
    tmean, pooled, pgs, egs, csum, inv_t, eg_t, tdir,
    texts, ebuf, msgs,
    q, ra, rb, sa, sb, yr, yq,
    g, gc, gx, gra, grb, gsa, gsb, gyr,
    out, win, wout, tgrad,
    tok_sem, w_sem,
    text_ss, text_rs, emb_ss, emb_rs, msg_ss, msg_rs,
    q_ss, q_rs, g_ss, g_rs, out_sem,
):
    dp = lax.axis_index("dp")
    tp = lax.axis_index("tensor")
    yh, local = dp // 8, dp % 8
    x, core = local // 2, dp % 2
    z, y = tp // 2, tp % 2

    def mesh_z(step):
        return (dp, ((z + step) % 4) * 2 + y)

    def mesh_x(step):
        return (yh * 8 + ((x + step) % 4) * 2 + core, tp)

    y_pair = (dp, z * 2 + (1 - y))
    core_pair = (dp - core + (1 - core), tp)
    y_far = ((1 - yh) * 8 + local, tp)

    def octet(k):
        return (yh * 8 + (local + k) % 8, tp)

    def remote(src, dst, ssem, rsem, dev):
        return pltpu.make_async_remote_copy(
            src_ref=src, dst_ref=dst, send_sem=ssem, recv_sem=rsem,
            device_id=dev, device_id_type=pl.DeviceIdType.MESH,
        )

    def tok_copy(c):
        rows = pl.ds(c * TOKS, TOKS)
        return pltpu.make_async_copy(tokens_hbm.at[rows], tok.at[rows], tok_sem.at[c])

    tok_copy(0).start()
    w_in_copy = pltpu.make_async_copy(w_in_hbm, w_in, w_sem.at[0])
    w_out_copy = pltpu.make_async_copy(w_out_hbm, w_out, w_sem.at[1])
    w_in_copy.start()
    for c in range(1, CHUNKS):
        tok_copy(c).start()
    w_out_copy.start()

    barrier = pltpu.get_barrier_semaphore()

    def greet(dev):
        pl.semaphore_signal(barrier, inc=1, device_id=dev, device_id_type=pl.DeviceIdType.MESH)

    greet(y_far)
    for k in range(1, 8):
        greet(octet(k))
        greet((dp, (tp + k) % 8))

    text_vals = text_ref[...].astype(F32)
    text_inv = lax.rsqrt(jnp.sum(text_vals * text_vals, axis=1, keepdims=True) + EPS)
    text_nrm = text_vals * text_inv
    texts[dp] = jnp.concatenate([text_nrm[:, :HALF], text_nrm[:, HALF:]], axis=0).astype(BF16)
    tmean[...] = jnp.zeros_like(tmean)
    pooled[...] = jnp.zeros_like(pooled)

    def gather_send(buf, slot, ss, rs, row):
        @pl.loop(1, 8)
        def _(k):
            remote(buf.at[slot], buf.at[slot], ss.at[row, k], rs.at[slot], octet(k)).start()

    def gather_far(buf, ss, rs):
        return remote(buf.at[dp], buf.at[dp], ss.at[0, 0], rs.at[dp], y_far)

    def gather_recv(buf, slot, ss, rs):
        remote(buf.at[slot], buf.at[slot], ss.at[0, 0], rs.at[slot], y_far).wait_recv()

    def gather_first(buf, ss, rs):
        gather_far(buf, ss, rs).start()
        gather_send(buf, dp, ss, rs, 0)

    far_slot = (1 - yh) * 8 + local

    def gather_relay(buf, ss, rs):
        gather_recv(buf, far_slot, ss, rs)
        gather_send(buf, far_slot, ss, rs, 1)

    def gather_rest(buf, ss, rs):
        @pl.loop(1, 8)
        def _(k):
            gather_recv(buf, yh * 8 + (local + k) % 8, ss, rs)
            gather_recv(buf, (1 - yh) * 8 + (local + k) % 8, ss, rs)

    def gather_sent(buf, ss, rs):
        gather_far(buf, ss, rs).wait_send()

        @pl.loop(1, 8)
        def _(k):
            for row in range(2):
                remote(buf.at[dp], buf.at[dp], ss.at[row, k], rs.at[dp], octet(k)).wait_send()

    def project(c):
        rows = pl.ds(c * TOKS, TOKS)
        hpre[rows, :] = dot(tok[rows, :], w_in[...])

    def statistics(c):
        acc = jnp.zeros((8, D), F32)
        for b in range(TOKS // 16):
            rows = pl.ds(c * TOKS + b * 16, 16)
            vals = tok[rows, :].astype(F32)
            mean = jnp.sum(vals, axis=1, keepdims=True) * (1.0 / D)
            center = vals - mean
            var = jnp.sum(center * center, axis=1, keepdims=True) * (1.0 / D)
            scale = lax.rsqrt(var + EPS)
            inv[rows, :] = scale
            minv[rows, :] = mean * scale
            acc = acc + (vals[:8] + vals[8:])
        tmean[pl.ds(c, 1), :] = jnp.sum(acc, axis=0, keepdims=True) * (1.0 / TOKS)

    def pool(c):
        cs = csum[...]
        acc = jnp.zeros((8, HID), F32)
        for b in range(TOKS // 16):
            rows = pl.ds(c * TOKS + b * 16, 16)
            h = hpre[rows, :] * inv[rows, :] - minv[rows, :] * cs
            hpre[rows, :] = h
            t = jnp.tanh(h * (GELU_A + (GELU_A * GELU_B) * (h * h)))
            act = h + h * t
            acc = acc + (act[:8] + act[8:])
        pooled[pl.ds(c, 1), :] = jnp.sum(acc, axis=0, keepdims=True) * (0.5 / TOKS)

    def forward(first, last):
        for c in range(first, last):
            project(c)
            statistics(c)
            if c > first:
                pool(c - 1)
        pool(last - 1)

    def emb_copy(n, k):
        return remote(
            ebuf.at[n, tp], ebuf.at[n, tp], emb_ss.at[n, k], emb_rs.at[n, tp], (dp, (tp + k) % 8)
        )

    def exchange_start(n):
        part = dot(pooled[...].astype(BF16), w_out[...])
        ebuf[n, tp] = jnp.concatenate([part[:, :HALF], part[:, HALF:]], axis=0).astype(BF16)

        @pl.loop(1, 8)
        def _(k):
            emb_copy(n, k).start()

    def exchange_wait(n):
        @pl.loop(1, 8)
        def _(k):
            src = (tp + k) % 8
            remote(
                ebuf.at[n, src], ebuf.at[n, src], emb_ss.at[n, k], emb_rs.at[n, src], (dp, src)
            ).wait_recv()

    def flip(c):
        rows = pl.ds(c * TOKS, TOKS)
        scale = inv[rows, :]
        normed = (tok[rows, :].astype(F32) * scale - minv[rows, :]).astype(BF16)
        nt[:, rows] = normed.T
        inv_t[pl.ds(c, 1), :] = jnp.broadcast_to(scale, (TOKS, 128)).T[0:1, :]

    def both(sums):
        total = sums[:IMGS] + sums[IMGS:]
        return jnp.concatenate([total, total], axis=0)

    scale = scale_ref[0]

    def loss(n):
        tm = tmean[...]
        emb = jnp.concatenate([tm[:, :HALF], tm[:, HALF:]], axis=0)
        for k in range(8):
            emb = emb + ebuf[n, k].astype(F32)
        emb_inv = lax.rsqrt(both(jnp.sum(emb * emb, axis=1, keepdims=True)) + EPS)
        image_bf = (emb * emb_inv).astype(BF16)
        text_all = texts[...].reshape(256, HALF)
        prod = dot(image_bf, text_all, NT)
        logits = scale * (prod[:IMGS] + pltpu.roll(prod[IMGS:], 256 - IMGS, 1)) + bias_ref[0]
        lane = lax.broadcasted_iota(jnp.int32, (IMGS, 256), 1)
        row = lax.broadcasted_iota(jnp.int32, (IMGS, 256), 0)
        valid = (lane % 16) < 8
        text_id = (lane // 16) * 8 + lane % 16
        label = jnp.zeros((IMGS, 256), jnp.int32)
        for k in range(IMGS):
            label = jnp.where(row == k, labels_ref[k], label)
        signs = jnp.where(label == text_id, 1.0, -1.0)
        grad = -signs * jax.nn.sigmoid(-signs * logits) * LOSS_SCALE
        grad = jnp.where(valid, grad, 0.0)
        grad = jnp.concatenate([grad, pltpu.roll(grad, IMGS, 1)], axis=0).astype(BF16)
        image_dir = scale * dot(grad, text_all)
        emb_grad = emb_inv * image_dir - (emb_inv * emb_inv * emb_inv) * emb * both(
            jnp.sum(emb * image_dir, axis=1, keepdims=True)
        )
        eg_bf = emb_grad.astype(BF16)
        pgs[...] = (
            dot(eg_bf[:IMGS], w_out[:, :HALF], NT) + dot(eg_bf[IMGS:], w_out[:, HALF:], NT)
        ) * (1.0 / TOKS)
        if n == len(GROUPS) - 1:
            egs[...] = emb_grad * (1.0 / TOKS)
            msgs[dp, :, 0:HALF] = image_bf
            msgs[dp, :, HALF:D] = eg_bf
            pooled_f = pooled[...]
            msgs[dp, :, D:D + HID] = jnp.concatenate([pooled_f, pooled_f], axis=0).astype(BF16)
            msgs[dp, :, D + HID:D + HID + 256] = grad

    def hidden_chunk(c):
        pg = pgs[pl.ds(c, 1), :]
        cs = csum[...]
        first, second = [], []
        for b in range(TOKS // 16):
            rows = pl.ds(c * TOKS + b * 16, 16)
            h = hpre[rows, :]
            h2 = h * h
            t = jnp.tanh(h * (GELU_A + (GELU_A * GELU_B) * h2))
            slope = (1.0 + t) + h * (1.0 - t * t) * (GELU_A + (3.0 * GELU_A * GELU_B) * h2)
            grad_bf = (slope * (0.5 * pg)).astype(BF16)
            hg[rows, :] = grad_bf
            grad_h = grad_bf.astype(F32)
            p1 = grad_h * cs
            p2 = grad_h * h
            s1 = p1[:, 0:128]
            s2 = p2[:, 0:128]
            for i in range(1, HID // 128):
                s1 = s1 + p1[:, i * 128:(i + 1) * 128]
                s2 = s2 + p2[:, i * 128:(i + 1) * 128]
            first.append(s1)
            second.append(s2)
        m1 = jnp.sum(jnp.concatenate(first, axis=0).T, axis=0, keepdims=True) * (1.0 / D)
        m2 = jnp.sum(jnp.concatenate(second, axis=0).T, axis=0, keepdims=True) * (1.0 / D)
        rows = pl.ds(c * TOKS, TOKS)
        hgc = hg[rows, :]
        for zb in range(4):
            feats = pl.ds(zb * 384, 384)
            block = dot(w_in[feats, :], hgc, NT) - m1 - nt[feats, rows].astype(F32) * m2
            block = block.astype(BF16)
            q[c, zb, 0] = block[:192]
            q[c, zb, 1] = block[192:]

    zp, zn, zo = (z + 1) % 4, (z + 3) % 4, (z + 2) % 4
    up, down = mesh_z(1), mesh_z(3)
    lo, hi = pl.ds(0, 96), pl.ds(96, 96)

    def add_into(dst, a, b):
        dst[...] = (a[...].astype(F32) + b[...].astype(F32)).astype(BF16)

    def pair_copy(c):
        n = PAIR_FIRST.index(c)
        return remote(q.at[c, :, 1 - y], yq.at[n], q_ss.at[c, 0], q_rs.at[c, 0], y_pair)

    def pair_ring1(c):
        return (
            remote(q.at[c, zo, y, lo], ra.at[c, lo], q_ss.at[c, 1], q_rs.at[c, 1], up),
            remote(q.at[c, zo, y, hi], rb.at[c, lo], q_ss.at[c, 2], q_rs.at[c, 2], down),
            remote(q.at[c, zp, y, hi], sa.at[c, 0, hi], q_ss.at[c, 3], q_rs.at[c, 3], up),
            remote(q.at[c, zn, y, lo], sb.at[c, 0, lo], q_ss.at[c, 4], q_rs.at[c, 4], down),
        )

    def pair_ring2(c):
        return (
            remote(q.at[c, zp, y, lo], sa.at[c, 0, lo], q_ss.at[c, 5], q_rs.at[c, 5], up),
            remote(q.at[c, zn, y, hi], sb.at[c, 0, hi], q_ss.at[c, 6], q_rs.at[c, 6], down),
        )

    def ring1(c):
        return (
            remote(q.at[c, zo, 0], ra.at[c], q_ss.at[c, 1], q_rs.at[c, 1], up),
            remote(q.at[c, zo, 1], rb.at[c], q_ss.at[c, 2], q_rs.at[c, 2], down),
            remote(q.at[c, zp, 1], sa.at[c, 1], q_ss.at[c, 3], q_rs.at[c, 3], up),
            remote(q.at[c, zn, 0], sb.at[c, 0], q_ss.at[c, 4], q_rs.at[c, 4], down),
        )

    def ring2(c):
        return (
            remote(q.at[c, zp, 0], sa.at[c, 0], q_ss.at[c, 5], q_rs.at[c, 5], up),
            remote(q.at[c, zn, 1], sb.at[c, 1], q_ss.at[c, 6], q_rs.at[c, 6], down),
        )

    def ring_pair(c):
        return remote(q.at[c, z, 1 - y], yr.at[c], q_ss.at[c, 0], q_rs.at[c, 0], y_pair)

    def start(copies):
        for copy in copies:
            copy.start()

    def step_a(c):
        hidden_chunk(c)
        start((pair_copy(c),) if c in PAIR_FIRST else ring1(c))

    def step_b(c):
        if c in PAIR_FIRST:
            pair_copy(c).wait_recv()
            for zb in range(4):
                blk = q.at[c, zb, y]
                add_into(blk, blk, yq.at[PAIR_FIRST.index(c), zb])
            start(pair_ring1(c))
        else:
            first, second = ring1(c)[:2]
            first.wait_recv()
            add_into(q.at[c, zp, 0], q.at[c, zp, 0], ra.at[c])
            second.wait_recv()
            add_into(q.at[c, zn, 1], q.at[c, zn, 1], rb.at[c])
            start(ring2(c))

    def step_c(c):
        if c in PAIR_FIRST:
            first, second = pair_ring1(c)[:2]
            first.wait_recv()
            add_into(q.at[c, zp, y, lo], q.at[c, zp, y, lo], ra.at[c, lo])
            second.wait_recv()
            add_into(q.at[c, zn, y, hi], q.at[c, zn, y, hi], rb.at[c, lo])
            start(pair_ring2(c))
        else:
            for copy in ring1(c)[2:] + ring2(c):
                copy.wait_recv()
            for half in range(2):
                blk = q.at[c, z, half]
                blk[...] = (
                    blk[...].astype(F32) + sa[c, half].astype(F32) + sb[c, half].astype(F32)
                ).astype(BF16)
            ring_pair(c).start()

    def out_copy(c):
        rows = pl.ds(c * TOKS, TOKS)
        return pltpu.make_async_copy(out.at[:, rows], out_hbm.at[:, rows], out_sem.at[c])

    def step_d(c):
        if c in PAIR_FIRST:
            for copy in pair_ring1(c)[2:] + pair_ring2(c):
                copy.wait_recv()
            total = q[c, z, y].astype(F32) + sa[c, 0].astype(F32) + sb[c, 0].astype(F32)
        else:
            ring_pair(c).wait_recv()
            total = q[c, z, y].astype(F32) + yr[c].astype(F32)
        rows = pl.ds(c * TOKS, TOKS)
        out[:, rows] = (
            inv_t[pl.ds(c, 1), :] * total + eg_t[0:192, c:c + 1]
        ).astype(BF16)
        out_copy(c).start()

    xp, xn, xo = (x + 1) % 4, (x + 3) % 4, (x + 2) % 4
    right, left = mesh_x(1), mesh_x(3)

    core_copy = remote(g.at[:, :, 1 - core], gc, g_ss.at[0], g_rs.at[0], core_pair)
    g1a = remote(gx.at[xo, 0], gra, g_ss.at[1], g_rs.at[1], right)
    g1b = remote(gx.at[xo, 1], grb, g_ss.at[2], g_rs.at[2], left)
    g2a = remote(gx.at[xp], gsa, g_ss.at[3], g_rs.at[3], right)
    g2b = remote(gx.at[xn], gsb, g_ss.at[4], g_rs.at[4], left)
    g3 = remote(gx.at[x, 1 - yh], gyr, g_ss.at[5], g_rs.at[5], y_far)

    def weight_a():
        @pl.loop(0, 4)
        def _(i):
            feats = pl.ds(pl.multiple_of(i * 384, 384), 384)
            block = dot(nt[feats, :], hg[...]).astype(BF16)
            for k in range(4):
                g[i, k // 2, k % 2] = block[k * 96:(k + 1) * 96]

        core_copy.start()

    def weight_b():
        core_copy.wait_recv()

        @pl.loop(0, 8)
        def _(k):
            xb, yb = k // 2, k % 2
            i, j = yb * 2 + xb // 2, xb % 2
            add_into(gx.at[xb, yb], g.at[i, j, core], gc.at[i, j])

        g1a.start()
        g1b.start()

    def weight_c():
        g1a.wait_recv()
        add_into(gx.at[xp, 0], gx.at[xp, 0], gra)
        g1b.wait_recv()
        add_into(gx.at[xn, 1], gx.at[xn, 1], grb)
        g2a.start()
        g2b.start()

    def weight_d():
        g2a.wait_recv()
        g2b.wait_recv()
        for half in range(2):
            blk = gx.at[x, half]
            blk[...] = (
                blk[...].astype(F32) + gsa[half].astype(F32) + gsb[half].astype(F32)
            ).astype(BF16)
        g3.start()

    def small_out(src, dst, k):
        return pltpu.make_async_copy(src, dst, out_sem.at[CHUNKS + k])

    def weight_e():
        g3.wait_recv()
        win[...] = (gx[x, yh].astype(F32) + gyr[...].astype(F32)).astype(BF16)
        small_out(win, win_hbm, 0).start()

    def gathered():
        gather_rest(msgs, msg_ss, msg_rs)
        all_msgs = msgs[...].reshape(256, D + HID + 256)
        tdir[...] = dot(all_msgs[:, D + HID:], all_msgs[:, :HALF], TN)
        text_dir = scale * tdir[pl.ds(pl.multiple_of(dp * 16, 16), 16), :]
        text_dir = jnp.concatenate([text_dir[:IMGS], text_dir[IMGS:]], axis=1)
        vals = text_ref[...].astype(F32)
        t_inv = lax.rsqrt(jnp.sum(vals * vals, axis=1, keepdims=True) + EPS)
        tgrad[...] = (
            t_inv * text_dir
            - (t_inv * t_inv * t_inv) * vals * jnp.sum(vals * text_dir, axis=1, keepdims=True)
        ).astype(BF16)
        small_out(tgrad, tgrad_hbm, 1).start()
        feat = lax.broadcasted_iota(jnp.int32, (HALF, 128), 0)
        col = lax.broadcasted_iota(jnp.int32, (HALF, 128), 1)
        pick = jnp.where(feat == col + local * 96, 1.0, 0.0).astype(BF16)
        emb_cols = dot(all_msgs[:, HALF:D], pick)
        slot_row = lax.broadcasted_iota(jnp.int32, (256, 128), 0)
        emb_cols = jnp.where((slot_row // 8) % 2 == yh, emb_cols, 0.0).astype(BF16)
        wout[...] = dot(emb_cols, all_msgs[:, D:D + HID], TN)[:96].astype(BF16)
        small_out(wout, wout_hbm, 2).start()

    def own_columns():
        cols = egs[pl.ds(pl.multiple_of((z // 2) * 8, 8), 8),
                   pl.ds(pl.multiple_of((z % 2) * 384, 128), 384)]
        cols = jnp.where(y == 0, cols[:, :192], cols[:, 192:])
        square = jnp.concatenate([cols, jnp.zeros((8, 64), F32)], axis=1)
        square = jnp.concatenate([square, jnp.zeros((120, 256), F32)], axis=0)
        eg_t[...] = square.T

    w_in_copy.wait()
    for c in range(0, 4):
        tok_copy(c).wait()
    csum[...] = dot(jnp.full((16, D), 1.0, BF16), w_in[...])[0:1]
    pl.semaphore_wait(barrier, 15)
    gather_first(texts, text_ss, text_rs)
    forward(*GROUPS[0])
    w_out_copy.wait()
    exchange_start(0)
    gather_relay(texts, text_ss, text_rs)
    for c in range(*GROUPS[0]):
        flip(c)
    exchange_wait(0)
    gather_rest(texts, text_ss, text_rs)
    loss(0)
    for c in range(*GROUPS[0]):
        step_a(c)

    for c in range(4, CHUNKS):
        tok_copy(c).wait()
    forward(*GROUPS[1])
    exchange_start(1)
    step_b(0)
    for c in range(*GROUPS[1]):
        flip(c)
    step_b(1)
    exchange_wait(1)
    loss(1)
    step_b(2)
    step_a(4)
    gather_first(msgs, msg_ss, msg_rs)
    step_c(0)
    step_a(5)
    step_b(3)
    step_a(6)
    step_c(2)
    step_a(7)
    step_c(1)
    own_columns()
    weight_a()
    gather_relay(msgs, msg_ss, msg_rs)
    step_b(4)
    step_c(3)
    weight_b()
    step_d(0)
    step_b(6)
    step_b(7)
    step_b(5)
    step_d(2)
    weight_c()
    gathered()
    step_c(4)
    step_d(1)
    step_d(3)
    weight_d()
    step_c(6)
    step_c(7)
    step_c(5)
    step_d(4)
    weight_e()
    step_d(6)
    step_d(7)
    step_d(5)

    for c in range(CHUNKS):
        if c in PAIR_FIRST:
            copies = (pair_copy(c),) + pair_ring1(c) + pair_ring2(c)
        else:
            copies = (ring_pair(c),) + ring1(c) + ring2(c)
        for copy in copies:
            copy.wait_send()
    for copy in (core_copy, g1a, g1b, g2a, g2b, g3):
        copy.wait_send()
    for n in range(len(GROUPS)):
        @pl.loop(1, 8)
        def _(k):
            emb_copy(n, k).wait_send()

    gather_sent(texts, text_ss, text_rs)
    gather_sent(msgs, msg_ss, msg_rs)
    for c in range(CHUNKS):
        out_copy(c).wait()
    small_out(win, win_hbm, 0).wait()
    small_out(tgrad, tgrad_hbm, 1).wait()
    small_out(wout, wout_hbm, 2).wait()


def hand_out(a, b, c, d, a_out, b_out, c_out, d_out, sem):
    copies = [
        pltpu.make_async_copy(src, dst, sem.at[k])
        for k, (src, dst) in enumerate(((a, a_out), (b, b_out), (c, c_out), (d, d_out)))
    ]
    for copy in copies:
        copy.start()
    for copy in copies:
        copy.wait()


def body(tokens, w_in, w_out, text_emb, labels, logit_scale, logit_bias):
    vmem = pl.BlockSpec(memory_space=pltpu.VMEM)
    smem = pl.BlockSpec(memory_space=pltpu.SMEM)
    hbm = pl.BlockSpec(memory_space=pl.ANY)
    msg = D + HID + 256
    groups = len(GROUPS)
    scratch = [
        pltpu.VMEM((ROWS, D), BF16),
        pltpu.VMEM((ROWS, 1), F32),
        pltpu.VMEM((ROWS, 1), F32),
        pltpu.VMEM((ROWS, HID), F32),
        pltpu.VMEM((ROWS, HID), BF16),
        pltpu.VMEM((D, ROWS), BF16),
        pltpu.VMEM((D, HID), BF16),
        pltpu.VMEM((HID, D), BF16),
        pltpu.VMEM((IMGS, D), F32),
        pltpu.VMEM((IMGS, HID), F32),
        pltpu.VMEM((IMGS, HID), F32),
        pltpu.VMEM((16, HALF), F32),
        pltpu.VMEM((1, HID), F32),
        pltpu.VMEM((CHUNKS, TOKS), F32),
        pltpu.VMEM((256, 128), F32),
        pltpu.VMEM((256, HALF), F32),
        pltpu.VMEM((16, 16, HALF), BF16),
        pltpu.VMEM((groups, 8, 16, HALF), BF16),
        pltpu.VMEM((16, 16, msg), BF16),
        pltpu.VMEM((CHUNKS, 4, 2, 192, TOKS), BF16),
        pltpu.VMEM((CHUNKS, 192, TOKS), BF16),
        pltpu.VMEM((CHUNKS, 192, TOKS), BF16),
        pltpu.VMEM((CHUNKS, 2, 192, TOKS), BF16),
        pltpu.VMEM((CHUNKS, 2, 192, TOKS), BF16),
        pltpu.VMEM((CHUNKS, 192, TOKS), BF16),
        pltpu.VMEM((len(PAIR_FIRST), 4, 192, TOKS), BF16),
        pltpu.VMEM((4, 2, 2, 96, HID), BF16),
        pltpu.VMEM((4, 2, 96, HID), BF16),
        pltpu.VMEM((4, 2, 96, HID), BF16),
        pltpu.VMEM((96, HID), BF16),
        pltpu.VMEM((96, HID), BF16),
        pltpu.VMEM((2, 96, HID), BF16),
        pltpu.VMEM((2, 96, HID), BF16),
        pltpu.VMEM((96, HID), BF16),
        pltpu.VMEM((192, ROWS), BF16),
        pltpu.VMEM((96, HID), BF16),
        pltpu.VMEM((96, HID), BF16),
        pltpu.VMEM((IMGS, D), BF16),
        pltpu.SemaphoreType.DMA((CHUNKS,)),
        pltpu.SemaphoreType.DMA((2,)),
        pltpu.SemaphoreType.DMA((2, 8)),
        pltpu.SemaphoreType.DMA((16,)),
        pltpu.SemaphoreType.DMA((groups, 8)),
        pltpu.SemaphoreType.DMA((groups, 8)),
        pltpu.SemaphoreType.DMA((2, 8)),
        pltpu.SemaphoreType.DMA((16,)),
        pltpu.SemaphoreType.DMA((CHUNKS, 7)),
        pltpu.SemaphoreType.DMA((CHUNKS, 7)),
        pltpu.SemaphoreType.DMA((6,)),
        pltpu.SemaphoreType.DMA((6,)),
        pltpu.SemaphoreType.DMA((CHUNKS + 3,)),
    ]
    shapes = (
        jax.ShapeDtypeStruct((D // 8, ROWS), BF16),
        jax.ShapeDtypeStruct((D // 16, HID), BF16),
        jax.ShapeDtypeStruct((D // 16, HID), BF16),
        jax.ShapeDtypeStruct((IMGS, D), BF16),
    )
    results = pl.pallas_call(
        kernel,
        out_shape=shapes,
        in_specs=[hbm, hbm, hbm, vmem, smem, smem, smem],
        out_specs=(hbm, hbm, hbm, hbm),
        scratch_shapes=scratch,
        compiler_params=pltpu.CompilerParams(
            collective_id=0, has_side_effects=True, vmem_limit_bytes=61 * 2**20
        ),
        cost_estimate=pl.CostEstimate(
            flops=6 * ROWS * D * HID, bytes_accessed=14 * 2**20, transcendentals=2 * ROWS * HID
        ),
    )(tokens, w_in, w_out, text_emb, labels, logit_scale, logit_bias)
    token_t, w_in_grad, w_out_t, text_grad = pl.pallas_call(
        hand_out,
        out_shape=shapes,
        in_specs=[hbm, hbm, hbm, hbm],
        out_specs=(hbm, hbm, hbm, hbm),
        scratch_shapes=[pltpu.SemaphoreType.DMA((4,))],
        compiler_params=pltpu.CompilerParams(vmem_limit_bytes=61 * 2**20),
        cost_estimate=pl.CostEstimate(flops=0, bytes_accessed=2 * 2**20, transcendentals=0),
    )(*results)
    return token_t.T, w_in_grad, w_out_t.T, text_grad


def solution(mesh):
    in_specs = (
        P("dp", None),
        P(None, "tensor"),
        P("tensor", None),
        P("dp", None),
        P("dp"),
        P(),
        P(),
    )
    out_specs = (P("dp", "tensor"), P("dp", "tensor"), P("tensor", "dp"), P("dp", None))
    return jax.shard_map(body, mesh=mesh, in_specs=in_specs, out_specs=out_specs, check_vma=False)
```

```python
import math

import jax
import jax.numpy as jnp
from jax import lax
from jax.experimental import pallas as pl
from jax.experimental.pallas import tpu as pltpu
from jax.sharding import PartitionSpec as P

F32 = jnp.float32
BF16 = jnp.bfloat16

D = 1536
HALF = D // 2
HID = 768
ROWS = 2048
TOKS = 256
IMGS = 8
LOSS_SCALE = 64.0
EPS = 1e-06
GELU_A = math.sqrt(2.0 / math.pi)
GELU_B = 0.044715

CHUNKS = 8
GROUPS = 2
PER = CHUNKS // GROUPS
PAIR_FIRST = 3

NN = (((1,), (0,)), ((), ()))
NT = (((1,), (1,)), ((), ()))
TN = (((0,), (0,)), ((), ()))


def dot(a, b, dims=NN):
    return lax.dot_general(a, b, dims, preferred_element_type=F32)


def kernel(
    tokens_hbm, w_in_hbm, w_out_hbm, text_ref, labels_ref, scale_ref, bias_ref,
    out_hbm, win_hbm, wout_hbm, tgrad_hbm,
    tok, inv, minv, hpre, hg, nt, w_in, w_out,
    tmean, pooled, pgs, egs, csum, inv_t, eg_t, tdir,
    texts, ebuf, msgs,
    q, ra, rb, sa, sb, yr, yq,
    g, gc, gx, gra, grb, gsa, gsb, gyr,
    out, win, wout, tgrad,
    tok_sem, w_sem,
    text_ss, text_rs, emb_ss, emb_rs, msg_ss, msg_rs,
    q_ss, q_rs, g_ss, g_rs, out_sem,
):
    dp = lax.axis_index("dp")
    tp = lax.axis_index("tensor")
    yh, local = dp // 8, dp % 8
    x, core = local // 2, dp % 2
    z, y = tp // 2, tp % 2

    def mesh_z(step):
        return (dp, ((z + step) % 4) * 2 + y)

    def mesh_x(step):
        return (yh * 8 + ((x + step) % 4) * 2 + core, tp)

    y_pair = (dp, z * 2 + (1 - y))
    core_pair = (dp - core + (1 - core), tp)
    y_far = ((1 - yh) * 8 + local, tp)

    def octet(k):
        return (yh * 8 + (local + k) % 8, tp)

    def remote(src, dst, ssem, rsem, dev):
        return pltpu.make_async_remote_copy(
            src_ref=src, dst_ref=dst, send_sem=ssem, recv_sem=rsem,
            device_id=dev, device_id_type=pl.DeviceIdType.MESH,
        )

    def tok_copy(c):
        rows = pl.ds(c * TOKS, TOKS)
        return pltpu.make_async_copy(tokens_hbm.at[rows], tok.at[rows], tok_sem.at[c])

    tok_copy(0).start()
    w_in_copy = pltpu.make_async_copy(w_in_hbm, w_in, w_sem.at[0])
    w_out_copy = pltpu.make_async_copy(w_out_hbm, w_out, w_sem.at[1])
    w_in_copy.start()
    for c in range(1, CHUNKS):
        tok_copy(c).start()
    w_out_copy.start()

    barrier = pltpu.get_barrier_semaphore()

    def greet(dev):
        pl.semaphore_signal(barrier, inc=1, device_id=dev, device_id_type=pl.DeviceIdType.MESH)

    greet(y_far)
    for k in range(1, 8):
        greet(octet(k))
        greet((dp, (tp + k) % 8))

    text_vals = text_ref[...].astype(F32)
    text_inv = lax.rsqrt(jnp.sum(text_vals * text_vals, axis=1, keepdims=True) + EPS)
    text_nrm = text_vals * text_inv
    texts[dp] = jnp.concatenate([text_nrm[:, :HALF], text_nrm[:, HALF:]], axis=0).astype(BF16)
    tmean[...] = jnp.zeros_like(tmean)
    pooled[...] = jnp.zeros_like(pooled)

    def gather_send(buf, slot, ss, rs, row):
        @pl.loop(1, 8)
        def _(k):
            remote(buf.at[slot], buf.at[slot], ss.at[row, k], rs.at[slot], octet(k)).start()

    def gather_far(buf, ss, rs):
        return remote(buf.at[dp], buf.at[dp], ss.at[0, 0], rs.at[dp], y_far)

    def gather_recv(buf, slot, ss, rs):
        remote(buf.at[slot], buf.at[slot], ss.at[0, 0], rs.at[slot], y_far).wait_recv()

    def gather_first(buf, ss, rs):
        gather_far(buf, ss, rs).start()
        gather_send(buf, dp, ss, rs, 0)

    far_slot = (1 - yh) * 8 + local

    def gather_relay(buf, ss, rs):
        gather_recv(buf, far_slot, ss, rs)
        gather_send(buf, far_slot, ss, rs, 1)

    def gather_rest(buf, ss, rs):
        @pl.loop(1, 8)
        def _(k):
            gather_recv(buf, yh * 8 + (local + k) % 8, ss, rs)
            gather_recv(buf, (1 - yh) * 8 + (local + k) % 8, ss, rs)

    def gather_sent(buf, ss, rs):
        gather_far(buf, ss, rs).wait_send()

        @pl.loop(1, 8)
        def _(k):
            for row in range(2):
                remote(buf.at[dp], buf.at[dp], ss.at[row, k], rs.at[dp], octet(k)).wait_send()

    def chunk_rows(c):
        return pl.ds(pl.multiple_of(c * TOKS, TOKS), TOKS)

    def forward(c):
        block = tok[chunk_rows(c), :]
        accs = [dot(block, w_in[:, j * 256:(j + 1) * 256]) for j in range(3)]
        scales, shifts = [], []
        acc = jnp.zeros((8, D), F32)
        for b in range(TOKS // 16):
            rows = pl.ds(pl.multiple_of(c * TOKS + b * 16, 16), 16)
            vals = tok[rows, :].astype(F32)
            mean = jnp.sum(vals, axis=1, keepdims=True) * (1.0 / D)
            center = vals - mean
            var = jnp.sum(center * center, axis=1, keepdims=True) * (1.0 / D)
            scale = lax.rsqrt(var + EPS)
            shift = mean * scale
            inv[rows, :] = scale
            minv[rows, :] = shift
            scales.append(scale)
            shifts.append(shift)
            acc = acc + (vals[:8] + vals[8:])
        tmean[pl.ds(c, 1), :] = jnp.sum(acc, axis=0, keepdims=True) * (1.0 / TOKS)
        for j in range(3):
            cols = slice(j * 256, (j + 1) * 256)
            cs = csum[:, cols]
            acc = jnp.zeros((8, 256), F32)
            for b in range(TOKS // 16):
                rows = pl.ds(pl.multiple_of(c * TOKS + b * 16, 16), 16)
                h = accs[j][b * 16:(b + 1) * 16] * scales[b] - shifts[b] * cs
                hpre[rows, cols] = h
                t = jnp.tanh(h * (GELU_A + (GELU_A * GELU_B) * (h * h)))
                act = h + h * t
                acc = acc + (act[:8] + act[8:])
            pooled[pl.ds(c, 1), cols] = jnp.sum(acc, axis=0, keepdims=True) * (0.5 / TOKS)

    def emb_copy(n, k):
        return remote(
            ebuf.at[n, tp], ebuf.at[n, tp], emb_ss.at[n, k], emb_rs.at[n, tp], (dp, (tp + k) % 8)
        )

    def exchange_start(n):
        part = dot(pooled[...].astype(BF16), w_out[...])
        ebuf[n, tp] = jnp.concatenate([part[:, :HALF], part[:, HALF:]], axis=0).astype(BF16)

        @pl.loop(1, 8)
        def _(k):
            emb_copy(n, k).start()

    def exchange_wait(n):
        @pl.loop(1, 8)
        def _(k):
            src = (tp + k) % 8
            remote(
                ebuf.at[n, src], ebuf.at[n, src], emb_ss.at[n, k], emb_rs.at[n, src], (dp, src)
            ).wait_recv()

    def flip(c):
        rows = chunk_rows(c)
        scale = inv[rows, :]
        normed = (tok[rows, :].astype(F32) * scale - minv[rows, :]).astype(BF16)
        nt[:, rows] = normed.T
        inv_t[pl.ds(c, 1), :] = jnp.broadcast_to(scale, (TOKS, 128)).T[0:1, :]

    def both(sums):
        total = sums[:IMGS] + sums[IMGS:]
        return jnp.concatenate([total, total], axis=0)

    scale = scale_ref[0]

    def loss(n):
        tm = tmean[...]
        emb = jnp.concatenate([tm[:, :HALF], tm[:, HALF:]], axis=0)
        for k in range(8):
            emb = emb + ebuf[n, k].astype(F32)
        emb_inv = lax.rsqrt(both(jnp.sum(emb * emb, axis=1, keepdims=True)) + EPS)
        image_bf = (emb * emb_inv).astype(BF16)
        text_all = texts[...].reshape(256, HALF)
        prod = dot(image_bf, text_all, NT)
        logits = scale * (prod[:IMGS] + pltpu.roll(prod[IMGS:], 256 - IMGS, 1)) + bias_ref[0]
        lane = lax.broadcasted_iota(jnp.int32, (IMGS, 256), 1)
        row = lax.broadcasted_iota(jnp.int32, (IMGS, 256), 0)
        valid = (lane % 16) < 8
        text_id = (lane // 16) * 8 + lane % 16
        label = jnp.zeros((IMGS, 256), jnp.int32)
        for k in range(IMGS):
            label = jnp.where(row == k, labels_ref[k], label)
        signs = jnp.where(label == text_id, 1.0, -1.0)
        grad = -signs * jax.nn.sigmoid(-signs * logits) * LOSS_SCALE
        grad = jnp.where(valid, grad, 0.0)
        grad = jnp.concatenate([grad, pltpu.roll(grad, IMGS, 1)], axis=0).astype(BF16)
        image_dir = scale * dot(grad, text_all)
        emb_grad = emb_inv * image_dir - (emb_inv * emb_inv * emb_inv) * emb * both(
            jnp.sum(emb * image_dir, axis=1, keepdims=True)
        )
        eg_bf = emb_grad.astype(BF16)
        pgs[...] = (
            dot(eg_bf[:IMGS], w_out[:, :HALF], NT) + dot(eg_bf[IMGS:], w_out[:, HALF:], NT)
        ) * (1.0 / TOKS)
        egs[...] = emb_grad * (1.0 / TOKS)
        msgs[dp, :, 0:HALF] = image_bf
        msgs[dp, :, HALF:D] = eg_bf
        pooled_f = pooled[...]
        msgs[dp, :, D:D + HID] = jnp.concatenate([pooled_f, pooled_f], axis=0).astype(BF16)
        msgs[dp, :, D + HID:D + HID + 256] = grad

    def hidden_chunk(c):
        pg = pgs[pl.ds(c, 1), :]
        cs = csum[...]
        first, second = [], []
        for b in range(TOKS // 16):
            rows = pl.ds(pl.multiple_of(c * TOKS + b * 16, 16), 16)
            h = hpre[rows, :]
            h2 = h * h
            t = jnp.tanh(h * (GELU_A + (GELU_A * GELU_B) * h2))
            slope = (1.0 + t) + h * (1.0 - t * t) * (GELU_A + (3.0 * GELU_A * GELU_B) * h2)
            grad_bf = (slope * (0.5 * pg)).astype(BF16)
            hg[rows, :] = grad_bf
            grad_h = grad_bf.astype(F32)
            p1 = grad_h * cs
            p2 = grad_h * h
            s1 = p1[:, 0:128]
            s2 = p2[:, 0:128]
            for i in range(1, HID // 128):
                s1 = s1 + p1[:, i * 128:(i + 1) * 128]
                s2 = s2 + p2[:, i * 128:(i + 1) * 128]
            first.append(s1)
            second.append(s2)
        m1 = jnp.sum(jnp.concatenate(first, axis=0).T, axis=0, keepdims=True) * (1.0 / D)
        m2 = jnp.sum(jnp.concatenate(second, axis=0).T, axis=0, keepdims=True) * (1.0 / D)
        rows = chunk_rows(c)
        hgc = hg[rows, :]
        for zb in range(4):
            feats = pl.ds(zb * 384, 384)
            block = dot(w_in[feats, :], hgc, NT) - m1 - nt[feats, rows].astype(F32) * m2
            block = block.astype(BF16)
            q[c, zb, 0] = block[:192]
            q[c, zb, 1] = block[192:]

    zp, zn, zo = (z + 1) % 4, (z + 3) % 4, (z + 2) % 4
    up, down = mesh_z(1), mesh_z(3)
    lo, hi = pl.ds(0, 96), pl.ds(96, 96)

    def add_into(dst, a, b):
        dst[...] = (a[...].astype(F32) + b[...].astype(F32)).astype(BF16)

    def pair_copy(c):
        return remote(q.at[c, :, 1 - y], yq.at[c // 2], q_ss.at[c, 0], q_rs.at[c, 0], y_pair)

    def pair_ring1(c):
        return (
            remote(q.at[c, zo, y, lo], ra.at[c, lo], q_ss.at[c, 1], q_rs.at[c, 1], up),
            remote(q.at[c, zo, y, hi], rb.at[c, lo], q_ss.at[c, 2], q_rs.at[c, 2], down),
            remote(q.at[c, zp, y, hi], sa.at[c, 0, hi], q_ss.at[c, 3], q_rs.at[c, 3], up),
            remote(q.at[c, zn, y, lo], sb.at[c, 0, lo], q_ss.at[c, 4], q_rs.at[c, 4], down),
        )

    def pair_ring2(c):
        return (
            remote(q.at[c, zp, y, lo], sa.at[c, 0, lo], q_ss.at[c, 5], q_rs.at[c, 5], up),
            remote(q.at[c, zn, y, hi], sb.at[c, 0, hi], q_ss.at[c, 6], q_rs.at[c, 6], down),
        )

    def ring1(c):
        return (
            remote(q.at[c, zo, 0], ra.at[c], q_ss.at[c, 1], q_rs.at[c, 1], up),
            remote(q.at[c, zo, 1], rb.at[c], q_ss.at[c, 2], q_rs.at[c, 2], down),
            remote(q.at[c, zp, 1], sa.at[c, 1], q_ss.at[c, 3], q_rs.at[c, 3], up),
            remote(q.at[c, zn, 0], sb.at[c, 0], q_ss.at[c, 4], q_rs.at[c, 4], down),
        )

    def ring2(c):
        return (
            remote(q.at[c, zp, 0], sa.at[c, 0], q_ss.at[c, 5], q_rs.at[c, 5], up),
            remote(q.at[c, zn, 1], sb.at[c, 1], q_ss.at[c, 6], q_rs.at[c, 6], down),
        )

    def ring_pair(c):
        return remote(q.at[c, z, 1 - y], yr.at[c], q_ss.at[c, 0], q_rs.at[c, 0], y_pair)

    def start(copies):
        for copy in copies:
            copy.start()

    def pair_b(c):
        pair_copy(c).wait_recv()

        @pl.loop(0, 4)
        def _(zb):
            blk = q.at[c, zb, y]
            add_into(blk, blk, yq.at[c // 2, zb])

        start(pair_ring1(c))

    def ring_b(c):
        first, second = ring1(c)[:2]
        first.wait_recv()
        add_into(q.at[c, zp, 0], q.at[c, zp, 0], ra.at[c])
        second.wait_recv()
        add_into(q.at[c, zn, 1], q.at[c, zn, 1], rb.at[c])
        start(ring2(c))

    def pair_c(c):
        first, second = pair_ring1(c)[:2]
        first.wait_recv()
        add_into(q.at[c, zp, y, lo], q.at[c, zp, y, lo], ra.at[c, lo])
        second.wait_recv()
        add_into(q.at[c, zn, y, hi], q.at[c, zn, y, hi], rb.at[c, lo])
        start(pair_ring2(c))

    def ring_c(c):
        for copy in ring1(c)[2:] + ring2(c):
            copy.wait_recv()

        @pl.loop(0, 2)
        def _(half):
            blk = q.at[c, z, half]
            blk[...] = (
                blk[...].astype(F32) + sa[c, half].astype(F32) + sb[c, half].astype(F32)
            ).astype(BF16)

        ring_pair(c).start()

    def out_copy(c):
        rows = chunk_rows(c)
        return pltpu.make_async_copy(out.at[:, rows], out_hbm.at[:, rows], out_sem.at[c])

    def finish(c, total):
        lane = lax.broadcasted_iota(jnp.int32, (192, 128), 1)
        col = jnp.sum(jnp.where(lane == c, eg_t[0:192, :], 0.0), axis=1, keepdims=True)
        out[:, chunk_rows(c)] = (inv_t[pl.ds(c, 1), :] * total + col).astype(BF16)
        out_copy(c).start()

    def pair_d(c):
        for copy in pair_ring1(c)[2:] + pair_ring2(c):
            copy.wait_recv()
        finish(c, q[c, z, y].astype(F32) + sa[c, 0].astype(F32) + sb[c, 0].astype(F32))

    def ring_d(c):
        ring_pair(c).wait_recv()
        finish(c, q[c, z, y].astype(F32) + yr[c].astype(F32))

    xp, xn, xo = (x + 1) % 4, (x + 3) % 4, (x + 2) % 4
    right, left = mesh_x(1), mesh_x(3)

    core_copy = remote(g.at[:, :, 1 - core], gc, g_ss.at[0], g_rs.at[0], core_pair)
    g1a = remote(gx.at[xo, 0], gra, g_ss.at[1], g_rs.at[1], right)
    g1b = remote(gx.at[xo, 1], grb, g_ss.at[2], g_rs.at[2], left)
    g2a = remote(gx.at[xp], gsa, g_ss.at[3], g_rs.at[3], right)
    g2b = remote(gx.at[xn], gsb, g_ss.at[4], g_rs.at[4], left)
    g3 = remote(gx.at[x, 1 - yh], gyr, g_ss.at[5], g_rs.at[5], y_far)

    def weight_a():
        @pl.loop(0, 4)
        def _(i):
            feats = pl.ds(pl.multiple_of(i * 384, 384), 384)
            block = dot(nt[feats, :], hg[...]).astype(BF16)
            for k in range(4):
                g[i, k // 2, k % 2] = block[k * 96:(k + 1) * 96]

        core_copy.start()

    def weight_b():
        core_copy.wait_recv()

        @pl.loop(0, 8)
        def _(k):
            xb, yb = k // 2, k % 2
            i, j = yb * 2 + xb // 2, xb % 2
            add_into(gx.at[xb, yb], g.at[i, j, core], gc.at[i, j])

        g1a.start()
        g1b.start()

    def weight_c():
        g1a.wait_recv()
        add_into(gx.at[xp, 0], gx.at[xp, 0], gra)
        g1b.wait_recv()
        add_into(gx.at[xn, 1], gx.at[xn, 1], grb)
        g2a.start()
        g2b.start()

    def weight_d():
        g2a.wait_recv()
        g2b.wait_recv()
        for half in range(2):
            blk = gx.at[x, half]
            blk[...] = (
                blk[...].astype(F32) + gsa[half].astype(F32) + gsb[half].astype(F32)
            ).astype(BF16)
        g3.start()

    def small_out(src, dst, k):
        return pltpu.make_async_copy(src, dst, out_sem.at[CHUNKS + k])

    def weight_e():
        g3.wait_recv()
        win[...] = (gx[x, yh].astype(F32) + gyr[...].astype(F32)).astype(BF16)
        small_out(win, win_hbm, 0).start()

    def gathered():
        gather_rest(msgs, msg_ss, msg_rs)
        all_msgs = msgs[...].reshape(256, D + HID + 256)
        tdir[...] = dot(all_msgs[:, D + HID:], all_msgs[:, :HALF], TN)
        text_dir = scale * tdir[pl.ds(pl.multiple_of(dp * 16, 16), 16), :]
        text_dir = jnp.concatenate([text_dir[:IMGS], text_dir[IMGS:]], axis=1)
        vals = text_ref[...].astype(F32)
        t_inv = lax.rsqrt(jnp.sum(vals * vals, axis=1, keepdims=True) + EPS)
        tgrad[...] = (
            t_inv * text_dir
            - (t_inv * t_inv * t_inv) * vals * jnp.sum(vals * text_dir, axis=1, keepdims=True)
        ).astype(BF16)
        small_out(tgrad, tgrad_hbm, 1).start()
        feat = lax.broadcasted_iota(jnp.int32, (HALF, 128), 0)
        col = lax.broadcasted_iota(jnp.int32, (HALF, 128), 1)
        pick = jnp.where(feat == col + local * 96, 1.0, 0.0).astype(BF16)
        emb_cols = dot(all_msgs[:, HALF:D], pick)
        slot_row = lax.broadcasted_iota(jnp.int32, (256, 128), 0)
        emb_cols = jnp.where((slot_row // 8) % 2 == yh, emb_cols, 0.0).astype(BF16)
        wout[...] = dot(emb_cols, all_msgs[:, D:D + HID], TN)[:96].astype(BF16)
        small_out(wout, wout_hbm, 2).start()

    def own_columns():
        cols = egs[pl.ds(pl.multiple_of((z // 2) * 8, 8), 8),
                   pl.ds(pl.multiple_of((z % 2) * 384, 128), 384)]
        cols = jnp.where(y == 0, cols[:, :192], cols[:, 192:])
        square = jnp.concatenate([cols, jnp.zeros((8, 64), F32)], axis=1)
        square = jnp.concatenate([square, jnp.zeros((120, 256), F32)], axis=0)
        eg_t[...] = square.T

    w_in_copy.wait()
    csum[...] = dot(jnp.full((16, D), 1.0, BF16), w_in[...])[0:1]
    pl.semaphore_wait(barrier, 15)
    gather_first(texts, text_ss, text_rs)

    def is_pair(c):
        return (c % 2 == 1) & (c < 6)

    @pl.loop(0, GROUPS)
    def _(n):
        @pl.loop(0, PER)
        def _(p):
            c = n * PER + p
            tok_copy(c).wait()
            forward(c)

        @pl.when(n == 0)
        def _():
            w_out_copy.wait()

        exchange_start(n)

        @pl.when(n == 0)
        def _():
            gather_relay(texts, text_ss, text_rs)

        @pl.when(n == 1)
        def _():
            @pl.loop(0, 2)
            def _(k):
                ring_b(2 * k)

        @pl.loop(0, PER)
        def _(p):
            flip(n * PER + p)

        @pl.when(n == 1)
        def _():
            pair_b(1)

        exchange_wait(n)

        @pl.when(n == 0)
        def _():
            gather_rest(texts, text_ss, text_rs)

        loss(n)

        @pl.when(n == 1)
        def _():
            pair_b(3)

        @pl.loop(0, PER)
        def _(p):
            c = n * PER + p
            hidden_chunk(c)

            @pl.when(is_pair(c))
            def _():
                pair_copy(c).start()

            @pl.when(jnp.logical_not(is_pair(c)))
            def _():
                start(ring1(c))

            @pl.when((n == 1) & (p < 2))
            def _():
                ring_c(2 * p)

            @pl.when((n == 1) & (p >= 2))
            def _():
                pair_c(2 * p - 3)

    def late_ring(k):
        return jnp.minimum(4 + 2 * k, 7)

    gather_first(msgs, msg_ss, msg_rs)
    own_columns()
    weight_a()

    @pl.loop(0, 3)
    def _(k):
        ring_b(late_ring(k))

    weight_b()
    pair_b(5)

    @pl.loop(0, 2)
    def _(k):
        ring_d(2 * k)

    gather_relay(msgs, msg_ss, msg_rs)
    weight_c()

    @pl.loop(0, 2)
    def _(k):
        pair_d(2 * k + 1)

    gathered()
    pair_c(5)

    @pl.loop(0, 3)
    def _(k):
        ring_c(late_ring(k))

    weight_d()
    pair_d(5)

    @pl.loop(0, 3)
    def _(k):
        ring_d(late_ring(k))

    weight_e()

    @pl.loop(0, CHUNKS)
    def _(c):
        out_copy(c).wait()

        @pl.when(is_pair(c))
        def _():
            for copy in (pair_copy(c),) + pair_ring1(c) + pair_ring2(c):
                copy.wait_send()

        @pl.when(jnp.logical_not(is_pair(c)))
        def _():
            for copy in (ring_pair(c),) + ring1(c) + ring2(c):
                copy.wait_send()

    for copy in (core_copy, g1a, g1b, g2a, g2b, g3):
        copy.wait_send()

    @pl.loop(1, 8)
    def _(k):
        for n in range(GROUPS):
            emb_copy(n, k).wait_send()

    gather_sent(texts, text_ss, text_rs)
    gather_sent(msgs, msg_ss, msg_rs)
    small_out(win, win_hbm, 0).wait()
    small_out(tgrad, tgrad_hbm, 1).wait()
    small_out(wout, wout_hbm, 2).wait()


def hand_out(a, b, c, d, a_out, b_out, c_out, d_out):
    a_out[...] = a[...]
    b_out[...] = b[...]
    c_out[...] = c[...]
    d_out[...] = d[...]


def body(tokens, w_in, w_out, text_emb, labels, logit_scale, logit_bias):
    vmem = pl.BlockSpec(memory_space=pltpu.VMEM)
    smem = pl.BlockSpec(memory_space=pltpu.SMEM)
    hbm = pl.BlockSpec(memory_space=pl.ANY)
    msg = D + HID + 256
    scratch = [
        pltpu.VMEM((ROWS, D), BF16),
        pltpu.VMEM((ROWS, 1), F32),
        pltpu.VMEM((ROWS, 1), F32),
        pltpu.VMEM((ROWS, HID), F32),
        pltpu.VMEM((ROWS, HID), BF16),
        pltpu.VMEM((D, ROWS), BF16),
        pltpu.VMEM((D, HID), BF16),
        pltpu.VMEM((HID, D), BF16),
        pltpu.VMEM((IMGS, D), F32),
        pltpu.VMEM((IMGS, HID), F32),
        pltpu.VMEM((IMGS, HID), F32),
        pltpu.VMEM((16, HALF), F32),
        pltpu.VMEM((1, HID), F32),
        pltpu.VMEM((CHUNKS, TOKS), F32),
        pltpu.VMEM((256, 128), F32),
        pltpu.VMEM((256, HALF), F32),
        pltpu.VMEM((16, 16, HALF), BF16),
        pltpu.VMEM((GROUPS, 8, 16, HALF), BF16),
        pltpu.VMEM((16, 16, msg), BF16),
        pltpu.VMEM((CHUNKS, 4, 2, 192, TOKS), BF16),
        pltpu.VMEM((CHUNKS, 192, TOKS), BF16),
        pltpu.VMEM((CHUNKS, 192, TOKS), BF16),
        pltpu.VMEM((CHUNKS, 2, 192, TOKS), BF16),
        pltpu.VMEM((CHUNKS, 2, 192, TOKS), BF16),
        pltpu.VMEM((CHUNKS, 192, TOKS), BF16),
        pltpu.VMEM((PAIR_FIRST, 4, 192, TOKS), BF16),
        pltpu.VMEM((4, 2, 2, 96, HID), BF16),
        pltpu.VMEM((4, 2, 96, HID), BF16),
        pltpu.VMEM((4, 2, 96, HID), BF16),
        pltpu.VMEM((96, HID), BF16),
        pltpu.VMEM((96, HID), BF16),
        pltpu.VMEM((2, 96, HID), BF16),
        pltpu.VMEM((2, 96, HID), BF16),
        pltpu.VMEM((96, HID), BF16),
        pltpu.VMEM((192, ROWS), BF16),
        pltpu.VMEM((96, HID), BF16),
        pltpu.VMEM((96, HID), BF16),
        pltpu.VMEM((IMGS, D), BF16),
        pltpu.SemaphoreType.DMA((CHUNKS,)),
        pltpu.SemaphoreType.DMA((2,)),
        pltpu.SemaphoreType.DMA((2, 8)),
        pltpu.SemaphoreType.DMA((16,)),
        pltpu.SemaphoreType.DMA((GROUPS, 8)),
        pltpu.SemaphoreType.DMA((GROUPS, 8)),
        pltpu.SemaphoreType.DMA((2, 8)),
        pltpu.SemaphoreType.DMA((16,)),
        pltpu.SemaphoreType.DMA((CHUNKS, 7)),
        pltpu.SemaphoreType.DMA((CHUNKS, 7)),
        pltpu.SemaphoreType.DMA((6,)),
        pltpu.SemaphoreType.DMA((6,)),
        pltpu.SemaphoreType.DMA((CHUNKS + 3,)),
    ]
    shapes = (
        jax.ShapeDtypeStruct((D // 8, ROWS), BF16),
        jax.ShapeDtypeStruct((D // 16, HID), BF16),
        jax.ShapeDtypeStruct((D // 16, HID), BF16),
        jax.ShapeDtypeStruct((IMGS, D), BF16),
    )
    results = pl.pallas_call(
        kernel,
        out_shape=shapes,
        in_specs=[hbm, hbm, hbm, vmem, smem, smem, smem],
        out_specs=(hbm, hbm, hbm, hbm),
        scratch_shapes=scratch,
        compiler_params=pltpu.CompilerParams(
            collective_id=0, has_side_effects=True, vmem_limit_bytes=61 * 2**20
        ),
        cost_estimate=pl.CostEstimate(
            flops=6 * ROWS * D * HID, bytes_accessed=14 * 2**20, transcendentals=2 * ROWS * HID
        ),
    )(tokens, w_in, w_out, text_emb, labels, logit_scale, logit_bias)
    token_t, w_in_grad, w_out_t, text_grad = pl.pallas_call(
        hand_out,
        out_shape=shapes,
        in_specs=[vmem, vmem, vmem, vmem],
        out_specs=(vmem, vmem, vmem, vmem),
        compiler_params=pltpu.CompilerParams(vmem_limit_bytes=61 * 2**20),
        cost_estimate=pl.CostEstimate(flops=0, bytes_accessed=2 * 2**20, transcendentals=0),
    )(*results)
    return token_t.T, w_in_grad, w_out_t.T, text_grad


def solution(mesh):
    in_specs = (
        P("dp", None),
        P(None, "tensor"),
        P("tensor", None),
        P("dp", None),
        P("dp"),
        P(),
        P(),
    )
    out_specs = (P("dp", "tensor"), P("dp", "tensor"), P("tensor", "dp"), P("dp", None))
    return jax.shard_map(body, mesh=mesh, in_specs=in_specs, out_specs=out_specs, check_vma=False)
```

```python
import math

import jax
import jax.numpy as jnp
from jax import lax
from jax.experimental import pallas as pl
from jax.experimental.pallas import tpu as pltpu
from jax.sharding import PartitionSpec as P

F32 = jnp.float32
BF16 = jnp.bfloat16

D = 1536
HALF = D // 2
HID = 768
ROWS = 2048
TOKS = 256
IMGS = 8
LOSS_SCALE = 64.0
EPS = 1e-06
GELU_A = math.sqrt(2.0 / math.pi)
GELU_B = 0.044715

CHUNKS = 8
GROUPS = 2
PER = CHUNKS // GROUPS
PAIR_FIRST = 3

NN = (((1,), (0,)), ((), ()))
NT = (((1,), (1,)), ((), ()))
TN = (((0,), (0,)), ((), ()))


def dot(a, b, dims=NN):
    return lax.dot_general(a, b, dims, preferred_element_type=F32)


def kernel(
    tokens_hbm, w_in_hbm, w_out_hbm, text_ref, labels_ref, scale_ref, bias_ref,
    out_hbm, win_hbm, wout_hbm, tgrad_hbm,
    tok, inv, hpre, hs, cur, nxt, tok_t, w_in, w_out,
    tmean, pooled, pgs, egs, csum, sums, inv_t, shift_t, eg_t, tdir,
    texts, ebuf, msgs,
    q, ra, rb, sa, sb, yr, yq,
    g, gc, gx, gra, grb, gsa, gsb, gyr,
    out, win, wout, tgrad,
    tok_sem, w_sem,
    text_ss, text_rs, emb_ss, emb_rs, msg_ss, msg_rs,
    q_ss, q_rs, g_ss, g_rs, out_sem,
):
    dp = lax.axis_index("dp")
    tp = lax.axis_index("tensor")
    yh, local = dp // 8, dp % 8
    x, core = local // 2, dp % 2
    z, y = tp // 2, tp % 2

    def mesh_z(step):
        return (dp, ((z + step) % 4) * 2 + y)

    def mesh_x(step):
        return (yh * 8 + ((x + step) % 4) * 2 + core, tp)

    y_pair = (dp, z * 2 + (1 - y))
    core_pair = (dp - core + (1 - core), tp)
    y_far = ((1 - yh) * 8 + local, tp)

    def remote(src, dst, ssem, rsem, dev):
        return pltpu.make_async_remote_copy(
            src_ref=src, dst_ref=dst, send_sem=ssem, recv_sem=rsem,
            device_id=dev, device_id_type=pl.DeviceIdType.MESH,
        )

    def tok_copy(c):
        rows = pl.ds(c * TOKS, TOKS)
        return pltpu.make_async_copy(tokens_hbm.at[rows], tok.at[rows], tok_sem.at[c])

    def w_in_copy(k):
        feats = pl.ds(k * 256, 256)
        return pltpu.make_async_copy(w_in_hbm.at[feats], w_in.at[feats], w_sem.at[k])

    w_out_copy = pltpu.make_async_copy(w_out_hbm, w_out, w_sem.at[6])
    tok_copy(0).start()
    for k in range(6):
        w_in_copy(k).start()
    tok_copy(1).start()

    barrier = pltpu.get_barrier_semaphore()

    def greet(dev):
        pl.semaphore_signal(barrier, inc=1, device_id=dev, device_id_type=pl.DeviceIdType.MESH)

    greet(y_far)
    greet(core_pair)
    for k in range(1, 4):
        greet(mesh_x(k))
    for k in range(1, 8):
        greet((dp, (tp + k) % 8))

    mine, far = yh * 4 + x, (1 - yh) * 4 + x
    text_vals = text_ref[...].astype(F32)
    text_inv = lax.rsqrt(jnp.sum(text_vals * text_vals, axis=1, keepdims=True) + EPS)
    text_nrm = text_vals * text_inv
    texts[core, mine] = jnp.concatenate([text_nrm[:, :HALF], text_nrm[:, HALF:]], axis=0).astype(BF16)
    tmean[...] = jnp.zeros_like(tmean)
    pooled[...] = jnp.zeros_like(pooled)

    def gather_far(buf, ss, rs):
        return remote(buf.at[core, mine], buf.at[core, mine], ss.at[0], rs.at[mine], y_far)

    def gather_x(buf, slot, k, ss, rs, first):
        block = buf.at[core, slot]
        return remote(block, block, ss.at[first + k], rs.at[slot], mesh_x(k))

    def gather_core(buf, ss, rs):
        return remote(buf.at[core], buf.at[core], ss.at[7], rs.at[8], core_pair)

    def gather_first(buf, ss, rs):
        gather_far(buf, ss, rs).start()
        for k in range(1, 4):
            gather_x(buf, mine, k, ss, rs, 0).start()

    def gather_relay(buf, ss, rs):
        gather_x(buf, far, 1, ss, rs, 3).wait_recv()
        for k in range(1, 4):
            gather_x(buf, far, k, ss, rs, 3).start()

    def gather_pass(buf, ss, rs):
        for k in range(1, 4):
            for side in range(2):
                gather_x(buf, side * 4 + (x + k) % 4, k, ss, rs, 0).wait_recv()
        gather_core(buf, ss, rs).start()

    def gather_rest(buf, ss, rs):
        remote(buf.at[1 - core], buf.at[1 - core], ss.at[7], rs.at[8], core_pair).wait_recv()

    def gather_sent(buf, ss, rs):
        gather_far(buf, ss, rs).wait_send()
        for k in range(1, 4):
            gather_x(buf, mine, k, ss, rs, 0).wait_send()
            gather_x(buf, far, k, ss, rs, 3).wait_send()
        gather_core(buf, ss, rs).wait_send()

    def split(vals):
        top = vals.astype(BF16).astype(F32)
        return jnp.concatenate(
            [top, vals - top, jnp.zeros((14,) + vals.shape[1:], F32)], axis=0
        ).astype(BF16)

    def chunk_rows(c):
        return pl.ds(pl.multiple_of(c * TOKS, TOKS), TOKS)

    def forward(c):
        accs = [
            dot(tok[chunk_rows(c), :], w_in[0:D, j * 256:(j + 1) * 256]) for j in range(3)
        ]
        means, scales, shifts = [], [], []
        acc = jnp.zeros((8, D), F32)
        for b in range(TOKS // 16):
            rows = pl.ds(pl.multiple_of(c * TOKS + b * 16, 16), 16)
            vals = tok[rows, :].astype(F32)
            mean = jnp.sum(vals, axis=1, keepdims=True) * (1.0 / D)
            center = vals - mean
            var = jnp.sum(center * center, axis=1, keepdims=True) * (1.0 / D)
            scale = lax.rsqrt(var + EPS)
            shift = mean * scale
            inv[rows, :] = scale
            means.append(mean)
            scales.append(scale)
            shifts.append(shift)
            acc = acc + (vals[:8] + vals[8:])
        tok_t[0:D, chunk_rows(c)] = tok[chunk_rows(c), :].T
        lane = lax.broadcasted_iota(jnp.int32, (TOKS, 128), 1)
        trio = jnp.where(lane == 0, jnp.concatenate(scales, 0), jnp.concatenate(shifts, 0))
        trio = jnp.where(lane == 2, jnp.concatenate(means, 0), trio).T
        inv_t[pl.ds(c, 1), :] = trio[0:1, :]
        shift_t[pl.ds(c, 1), :] = trio[1:2, :]
        tok_t[D:D + 16, chunk_rows(c)] = split(trio[2:3, :])
        tmean[pl.ds(c, 1), :] = jnp.sum(acc, axis=0, keepdims=True) * (1.0 / TOKS)
        for j in range(3):
            cols = slice(j * 256, (j + 1) * 256)
            cs = csum[:, cols]
            acc = jnp.zeros((8, 256), F32)
            for b in range(TOKS // 16):
                rows = pl.ds(pl.multiple_of(c * TOKS + b * 16, 16), 16)
                h = accs[j][b * 16:(b + 1) * 16] * scales[b] - shifts[b] * cs
                hpre[rows, cols] = h
                t = jnp.tanh(h * (GELU_A + (GELU_A * GELU_B) * (h * h)))
                act = h + h * t
                acc = acc + (act[:8] + act[8:])
            pooled[pl.ds(c, 1), cols] = jnp.sum(acc, axis=0, keepdims=True) * (0.5 / TOKS)

    def emb_copy(n, k):
        return remote(
            ebuf.at[n, tp], ebuf.at[n, tp], emb_ss.at[n, k], emb_rs.at[n, tp], (dp, (tp + k) % 8)
        )

    def exchange_start(n):
        part = dot(pooled[...].astype(BF16), w_out[...])
        ebuf[n, tp] = jnp.concatenate([part[:, :HALF], part[:, HALF:]], axis=0).astype(BF16)

        @pl.loop(1, 8)
        def _(k):
            emb_copy(n, k).start()

    def exchange_wait(n):
        @pl.loop(1, 8)
        def _(k):
            src = (tp + k) % 8
            remote(
                ebuf.at[n, src], ebuf.at[n, src], emb_ss.at[n, k], emb_rs.at[n, src], (dp, src)
            ).wait_recv()

    def both(sums):
        total = sums[:IMGS] + sums[IMGS:]
        return jnp.concatenate([total, total], axis=0)

    scale = scale_ref[0]

    def loss(n):
        tm = tmean[...]
        emb = jnp.concatenate([tm[:, :HALF], tm[:, HALF:]], axis=0)
        for k in range(8):
            emb = emb + ebuf[n, k].astype(F32)
        emb_inv = lax.rsqrt(both(jnp.sum(emb * emb, axis=1, keepdims=True)) + EPS)
        image_bf = (emb * emb_inv).astype(BF16)
        text_all = texts[...].reshape(256, HALF)
        prod = dot(image_bf, text_all, NT)
        logits = scale * (prod[:IMGS] + pltpu.roll(prod[IMGS:], 256 - IMGS, 1)) + bias_ref[0]
        lane = lax.broadcasted_iota(jnp.int32, (IMGS, 256), 1)
        row = lax.broadcasted_iota(jnp.int32, (IMGS, 256), 0)
        valid = (lane % 16) < 8
        slot = lane // 16
        text_id = ((slot // 4) % 2 * 8 + slot % 4 * 2 + slot // 8) * 8 + lane % 16
        label = jnp.zeros((IMGS, 256), jnp.int32)
        for k in range(IMGS):
            label = jnp.where(row == k, labels_ref[k], label)
        signs = jnp.where(label == text_id, 1.0, -1.0)
        grad = -signs * jax.nn.sigmoid(-signs * logits) * LOSS_SCALE
        grad = jnp.where(valid, grad, 0.0)
        grad = jnp.concatenate([grad, pltpu.roll(grad, IMGS, 1)], axis=0).astype(BF16)
        image_dir = scale * dot(grad, text_all)
        emb_grad = emb_inv * image_dir - (emb_inv * emb_inv * emb_inv) * emb * both(
            jnp.sum(emb * image_dir, axis=1, keepdims=True)
        )
        eg_bf = emb_grad.astype(BF16)
        pgs[...] = (
            dot(eg_bf[:IMGS], w_out[:, :HALF], NT) + dot(eg_bf[IMGS:], w_out[:, HALF:], NT)
        ) * (1.0 / TOKS)
        egs[...] = emb_grad * (1.0 / TOKS)
        msgs[core, mine, :, 0:HALF] = image_bf
        msgs[core, mine, :, HALF:D] = eg_bf
        pooled_f = pooled[...]
        msgs[core, mine, :, D:D + HID] = jnp.concatenate([pooled_f, pooled_f], axis=0).astype(BF16)
        msgs[core, mine, :, D + HID:D + HID + 256] = grad

    def hidden_rows(c):
        half_pg = 0.5 * pgs[pl.ds(c, 1), :]
        second = []
        for b in range(TOKS // 16):
            rows = pl.ds(pl.multiple_of(c * TOKS + b * 16, 16), 16)
            h = hpre[rows, :]
            h2 = h * h
            t = jnp.tanh(h * (GELU_A + (GELU_A * GELU_B) * h2))
            slope = (1.0 + t) + h * (1.0 - t * t) * (GELU_A + (3.0 * GELU_A * GELU_B) * h2)
            grad_bf = (slope * half_pg * inv[rows, :]).astype(BF16)
            hs[rows, :] = grad_bf
            nxt[b * 16:(b + 1) * 16, :] = grad_bf
            p2 = grad_bf.astype(F32) * h
            s2 = p2[:, 0:128]
            for i in range(1, HID // 128):
                s2 = s2 + p2[:, i * 128:(i + 1) * 128]
            second.append(s2)
        m2 = jnp.sum(jnp.concatenate(second, axis=0).T, axis=0, keepdims=True) * (1.0 / D)
        sums[0:1, :] = inv_t[pl.ds(c, 1), :] * m2
        sums[1:2, :] = shift_t[pl.ds(c, 1), :] * m2

    def feature_rows(c):
        rows = chunk_rows(c)
        full = dot(w_in[...], cur[...], NT)
        slope = sums[0:1, :]
        shift = (full[D:D + 1] + full[D + 1:D + 2]) * (1.0 / D) - sums[1:2, :]
        for k in range(8):
            feats = slice(k * 192, (k + 1) * 192)
            block = full[feats] - tok_t[feats, rows].astype(F32) * slope - shift
            q[c, k // 2, k % 2] = block.astype(BF16)

    zp, zn, zo = (z + 1) % 4, (z + 3) % 4, (z + 2) % 4
    up, down = mesh_z(1), mesh_z(3)
    lo, hi = pl.ds(0, 96), pl.ds(96, 96)

    def add_into(dst, a, b):
        dst[...] = (a[...].astype(F32) + b[...].astype(F32)).astype(BF16)

    def pair_copy(c):
        return remote(q.at[c, :, 1 - y], yq.at[c // 2], q_ss.at[c, 0], q_rs.at[c, 0], y_pair)

    def pair_ring1(c):
        return (
            remote(q.at[c, zo, y, lo], ra.at[c, lo], q_ss.at[c, 1], q_rs.at[c, 1], up),
            remote(q.at[c, zo, y, hi], rb.at[c, lo], q_ss.at[c, 2], q_rs.at[c, 2], down),
            remote(q.at[c, zp, y, hi], sa.at[c, 0, hi], q_ss.at[c, 3], q_rs.at[c, 3], up),
            remote(q.at[c, zn, y, lo], sb.at[c, 0, lo], q_ss.at[c, 4], q_rs.at[c, 4], down),
        )

    def pair_ring2(c):
        return (
            remote(q.at[c, zp, y, lo], sa.at[c, 0, lo], q_ss.at[c, 5], q_rs.at[c, 5], up),
            remote(q.at[c, zn, y, hi], sb.at[c, 0, hi], q_ss.at[c, 6], q_rs.at[c, 6], down),
        )

    def ring1(c):
        return (
            remote(q.at[c, zo, 0], ra.at[c], q_ss.at[c, 1], q_rs.at[c, 1], up),
            remote(q.at[c, zo, 1], rb.at[c], q_ss.at[c, 2], q_rs.at[c, 2], down),
            remote(q.at[c, zp, 1], sa.at[c, 1], q_ss.at[c, 3], q_rs.at[c, 3], up),
            remote(q.at[c, zn, 0], sb.at[c, 0], q_ss.at[c, 4], q_rs.at[c, 4], down),
        )

    def ring2(c):
        return (
            remote(q.at[c, zp, 0], sa.at[c, 0], q_ss.at[c, 5], q_rs.at[c, 5], up),
            remote(q.at[c, zn, 1], sb.at[c, 1], q_ss.at[c, 6], q_rs.at[c, 6], down),
        )

    def ring_pair(c):
        return remote(q.at[c, z, 1 - y], yr.at[c], q_ss.at[c, 0], q_rs.at[c, 0], y_pair)

    def start(copies):
        for copy in copies:
            copy.start()

    def pair_b(c):
        pair_copy(c).wait_recv()

        @pl.loop(0, 4)
        def _(zb):
            blk = q.at[c, zb, y]
            add_into(blk, blk, yq.at[c // 2, zb])

        start(pair_ring1(c))

    def ring_b(c):
        first, second = ring1(c)[:2]
        first.wait_recv()
        add_into(q.at[c, zp, 0], q.at[c, zp, 0], ra.at[c])
        second.wait_recv()
        add_into(q.at[c, zn, 1], q.at[c, zn, 1], rb.at[c])
        start(ring2(c))

    def pair_c(c):
        first, second = pair_ring1(c)[:2]
        first.wait_recv()
        add_into(q.at[c, zp, y, lo], q.at[c, zp, y, lo], ra.at[c, lo])
        second.wait_recv()
        add_into(q.at[c, zn, y, hi], q.at[c, zn, y, hi], rb.at[c, lo])
        start(pair_ring2(c))

    def ring_c(c):
        for copy in ring1(c)[2:] + ring2(c):
            copy.wait_recv()

        @pl.loop(0, 2)
        def _(half):
            blk = q.at[c, z, half]
            blk[...] = (
                blk[...].astype(F32) + sa[c, half].astype(F32) + sb[c, half].astype(F32)
            ).astype(BF16)

        ring_pair(c).start()

    def out_copy(c):
        rows = chunk_rows(c)
        return pltpu.make_async_copy(out.at[:, rows], out_hbm.at[:, rows], out_sem.at[c])

    def finish(c, total):
        lane = lax.broadcasted_iota(jnp.int32, (192, 128), 1)
        col = jnp.sum(jnp.where(lane == c, eg_t[0:192, :], 0.0), axis=1, keepdims=True)
        out[:, chunk_rows(c)] = (total + col).astype(BF16)
        out_copy(c).start()

    def pair_d(c):
        for copy in pair_ring1(c)[2:] + pair_ring2(c):
            copy.wait_recv()
        finish(c, q[c, z, y].astype(F32) + sa[c, 0].astype(F32) + sb[c, 0].astype(F32))

    def ring_d(c):
        ring_pair(c).wait_recv()
        finish(c, q[c, z, y].astype(F32) + yr[c].astype(F32))

    xp, xn, xo = (x + 1) % 4, (x + 3) % 4, (x + 2) % 4
    right, left = mesh_x(1), mesh_x(3)

    def core_copy(j):
        return remote(g.at[j, :, :, 1 - core], gc.at[j], g_ss.at[j, 0], g_rs.at[j, 0], core_pair)

    def g1(j):
        return (
            remote(gx.at[j, xo, 0], gra.at[j], g_ss.at[j, 1], g_rs.at[j, 1], right),
            remote(gx.at[j, xo, 1], grb.at[j], g_ss.at[j, 2], g_rs.at[j, 2], left),
        )

    def g2(j):
        return (
            remote(gx.at[j, xp], gsa.at[j], g_ss.at[j, 3], g_rs.at[j, 3], right),
            remote(gx.at[j, xn], gsb.at[j], g_ss.at[j, 4], g_rs.at[j, 4], left),
        )

    def g3(j):
        return remote(gx.at[j, x, 1 - yh], gyr.at[j], g_ss.at[j, 5], g_rs.at[j, 5], y_far)

    def weight_a(j):
        cols = pl.ds(pl.multiple_of(j * 256, 256), 256)
        full = dot(tok_t[...], hs[:, cols])
        lift = full[D:D + 1] + full[D + 1:D + 2]
        g[j] = (full[:D] - lift).astype(BF16).reshape(4, 2, 2, 96, 256)
        core_copy(j).start()

    def weight_b(j):
        core_copy(j).wait_recv()

        @pl.loop(0, 8)
        def _(k):
            xb, yb = k // 2, k % 2
            i, m = yb * 2 + xb // 2, xb % 2
            add_into(gx.at[j, xb, yb], g.at[j, i, m, core], gc.at[j, i, m])

        start(g1(j))

    def weight_c(j):
        first, second = g1(j)
        first.wait_recv()
        add_into(gx.at[j, xp, 0], gx.at[j, xp, 0], gra.at[j])
        second.wait_recv()
        add_into(gx.at[j, xn, 1], gx.at[j, xn, 1], grb.at[j])
        start(g2(j))

    def weight_d(j):
        for copy in g2(j):
            copy.wait_recv()
        for half in range(2):
            blk = gx.at[j, x, half]
            blk[...] = (
                blk[...].astype(F32) + gsa[j, half].astype(F32) + gsb[j, half].astype(F32)
            ).astype(BF16)
        g3(j).start()

    def weight_e():
        for j in range(3):
            g3(j).wait_recv()
            win[:, j * 256:(j + 1) * 256] = (
                gx[j, x, yh].astype(F32) + gyr[j].astype(F32)
            ).astype(BF16)
        small_out(win, win_hbm, 0).start()

    def small_out(src, dst, k):
        return pltpu.make_async_copy(src, dst, out_sem.at[CHUNKS + k])

    def gathered():
        gather_rest(msgs, msg_ss, msg_rs)
        all_msgs = msgs[...].reshape(256, D + HID + 256)
        tdir[...] = dot(all_msgs[:, D + HID:], all_msgs[:, :HALF], TN)
        text_dir = scale * tdir[pl.ds(pl.multiple_of((core * 8 + mine) * 16, 16), 16), :]
        text_dir = jnp.concatenate([text_dir[:IMGS], text_dir[IMGS:]], axis=1)
        vals = text_ref[...].astype(F32)
        t_inv = lax.rsqrt(jnp.sum(vals * vals, axis=1, keepdims=True) + EPS)
        tgrad[...] = (
            t_inv * text_dir
            - (t_inv * t_inv * t_inv) * vals * jnp.sum(vals * text_dir, axis=1, keepdims=True)
        ).astype(BF16)
        small_out(tgrad, tgrad_hbm, 1).start()
        feat = lax.broadcasted_iota(jnp.int32, (HALF, 128), 0)
        col = lax.broadcasted_iota(jnp.int32, (HALF, 128), 1)
        pick = jnp.where(feat == col + local * 96, 1.0, 0.0).astype(BF16)
        emb_cols = dot(all_msgs[:, HALF:D], pick)
        slot_row = lax.broadcasted_iota(jnp.int32, (256, 128), 0)
        emb_cols = jnp.where((slot_row // 8) % 2 == yh, emb_cols, 0.0).astype(BF16)
        wout[...] = dot(emb_cols, all_msgs[:, D:D + HID], TN)[:96].astype(BF16)
        small_out(wout, wout_hbm, 2).start()

    def own_columns():
        cols = egs[pl.ds(pl.multiple_of((z // 2) * 8, 8), 8),
                   pl.ds(pl.multiple_of((z % 2) * 384, 128), 384)]
        cols = jnp.where(y == 0, cols[:, :192], cols[:, 192:])
        square = jnp.concatenate([cols, jnp.zeros((8, 64), F32)], axis=1)
        square = jnp.concatenate([square, jnp.zeros((120, 256), F32)], axis=0)
        eg_t[...] = square.T

    for k in range(6):
        w_in_copy(k).wait()

    @pl.loop(2, CHUNKS)
    def _(c):
        tok_copy(c).start()

    w_out_copy.start()
    cs = dot(jnp.full((16, D), 1.0, BF16), w_in[0:D, :])[0:1]
    csum[...] = cs
    w_in[D:D + 16, :] = split(cs)
    pl.semaphore_wait(barrier, 12)
    gather_first(texts, text_ss, text_rs)

    def is_pair(c):
        return (c % 2 == 1) & (c < 6)

    def forward_loop(first, last):
        @pl.loop(first, last)
        def _(c):
            tok_copy(c).wait()
            forward(c)

    @pl.loop(0, GROUPS)
    def _(n):
        @pl.loop(5 * n, 4 + 4 * n)
        def _(c):
            tok_copy(c).wait()
            forward(c)

            @pl.when(c == 6)
            def _():
                ring_b(2)

        @pl.when(n == 0)
        def _():
            w_out_copy.wait()

        exchange_start(n)

        @pl.when(n == 0)
        def _():
            gather_relay(texts, text_ss, text_rs)
            forward_loop(4, 5)
            gather_pass(texts, text_ss, text_rs)

        @pl.when(n == 1)
        def _():
            pair_b(1)
            ring_c(0)

        exchange_wait(n)

        @pl.when(n == 0)
        def _():
            gather_rest(texts, text_ss, text_rs)

        loss(n)

        @pl.when(n == 1)
        def _():
            pair_c(1)
            ring_c(2)
            gather_first(msgs, msg_ss, msg_rs)

        hidden_rows(n * PER)

        @pl.loop(0, PER)
        def _(p):
            c = n * PER + p
            cur[...] = nxt[...]
            feature_rows(c)
            hidden_rows(jnp.minimum(c + 1, n * PER + PER - 1))

            @pl.when(is_pair(c))
            def _():
                pair_copy(c).start()

            @pl.when(jnp.logical_not(is_pair(c)))
            def _():
                start(ring1(c))

            @pl.when(c == 3)
            def _():
                ring_b(0)

            @pl.when(c == 5)
            def _():
                pair_b(3)

            @pl.when(c == 6)
            def _():
                ring_b(4)
                gather_relay(msgs, msg_ss, msg_rs)

            @pl.when(c == 7)
            def _():
                pair_c(3)

    own_columns()

    @pl.loop(0, 3)
    def _(j):
        weight_a(j)

        @pl.when(j == 0)
        def _():
            ring_b(6)
            gather_pass(msgs, msg_ss, msg_rs)

        @pl.when(j == 1)
        def _():
            ring_b(7)
            ring_c(4)
            weight_b(0)

        @pl.when(j == 2)
        def _():
            pair_b(5)

    weight_b(1)
    ring_c(6)
    weight_c(0)
    weight_b(2)
    pair_c(5)
    ring_c(7)
    weight_c(1)
    ring_d(0)
    pair_d(1)
    weight_d(0)
    weight_c(2)
    gathered()
    weight_d(1)
    ring_d(2)
    pair_d(3)
    weight_d(2)
    ring_d(4)
    ring_d(6)
    pair_d(5)
    ring_d(7)
    weight_e()

    @pl.loop(0, CHUNKS)
    def _(c):
        out_copy(c).wait()

        @pl.when(is_pair(c))
        def _():
            for copy in (pair_copy(c),) + pair_ring1(c) + pair_ring2(c):
                copy.wait_send()

        @pl.when(jnp.logical_not(is_pair(c)))
        def _():
            for copy in (ring_pair(c),) + ring1(c) + ring2(c):
                copy.wait_send()

    @pl.loop(0, 3)
    def _(j):
        for copy in (core_copy(j), g3(j)) + g1(j) + g2(j):
            copy.wait_send()

    @pl.loop(1, 8)
    def _(k):
        for n in range(GROUPS):
            emb_copy(n, k).wait_send()

    gather_sent(texts, text_ss, text_rs)
    gather_sent(msgs, msg_ss, msg_rs)
    small_out(win, win_hbm, 0).wait()
    small_out(tgrad, tgrad_hbm, 1).wait()
    small_out(wout, wout_hbm, 2).wait()


def hand_out(a, b, c, d, a_out, b_out, c_out, d_out):
    a_out[...] = a[...]
    b_out[...] = b[...]
    c_out[...] = c[...]
    d_out[...] = d[...]


def body(tokens, w_in, w_out, text_emb, labels, logit_scale, logit_bias):
    vmem = pl.BlockSpec(memory_space=pltpu.VMEM)
    smem = pl.BlockSpec(memory_space=pltpu.SMEM)
    hbm = pl.BlockSpec(memory_space=pl.ANY)
    msg = D + HID + 256
    scratch = [
        pltpu.VMEM((ROWS, D), BF16),
        pltpu.VMEM((ROWS, 1), F32),
        pltpu.VMEM((ROWS, HID), F32),
        pltpu.VMEM((ROWS, HID), BF16),
        pltpu.VMEM((TOKS, HID), BF16),
        pltpu.VMEM((TOKS, HID), BF16),
        pltpu.VMEM((D + 16, ROWS), BF16),
        pltpu.VMEM((D + 16, HID), BF16),
        pltpu.VMEM((HID, D), BF16),
        pltpu.VMEM((IMGS, D), F32),
        pltpu.VMEM((IMGS, HID), F32),
        pltpu.VMEM((IMGS, HID), F32),
        pltpu.VMEM((16, HALF), F32),
        pltpu.VMEM((1, HID), F32),
        pltpu.VMEM((8, TOKS), F32),
        pltpu.VMEM((CHUNKS, TOKS), F32),
        pltpu.VMEM((CHUNKS, TOKS), F32),
        pltpu.VMEM((256, 128), F32),
        pltpu.VMEM((256, HALF), F32),
        pltpu.VMEM((2, 8, 16, HALF), BF16),
        pltpu.VMEM((GROUPS, 8, 16, HALF), BF16),
        pltpu.VMEM((2, 8, 16, msg), BF16),
        pltpu.VMEM((CHUNKS, 4, 2, 192, TOKS), BF16),
        pltpu.VMEM((CHUNKS, 192, TOKS), BF16),
        pltpu.VMEM((CHUNKS, 192, TOKS), BF16),
        pltpu.VMEM((CHUNKS, 2, 192, TOKS), BF16),
        pltpu.VMEM((CHUNKS, 2, 192, TOKS), BF16),
        pltpu.VMEM((CHUNKS, 192, TOKS), BF16),
        pltpu.VMEM((PAIR_FIRST, 4, 192, TOKS), BF16),
        pltpu.VMEM((3, 4, 2, 2, 96, 256), BF16),
        pltpu.VMEM((3, 4, 2, 96, 256), BF16),
        pltpu.VMEM((3, 4, 2, 96, 256), BF16),
        pltpu.VMEM((3, 96, 256), BF16),
        pltpu.VMEM((3, 96, 256), BF16),
        pltpu.VMEM((3, 2, 96, 256), BF16),
        pltpu.VMEM((3, 2, 96, 256), BF16),
        pltpu.VMEM((3, 96, 256), BF16),
        pltpu.VMEM((192, ROWS), BF16),
        pltpu.VMEM((96, HID), BF16),
        pltpu.VMEM((96, HID), BF16),
        pltpu.VMEM((IMGS, D), BF16),
        pltpu.SemaphoreType.DMA((CHUNKS,)),
        pltpu.SemaphoreType.DMA((7,)),
        pltpu.SemaphoreType.DMA((8,)),
        pltpu.SemaphoreType.DMA((9,)),
        pltpu.SemaphoreType.DMA((GROUPS, 8)),
        pltpu.SemaphoreType.DMA((GROUPS, 8)),
        pltpu.SemaphoreType.DMA((8,)),
        pltpu.SemaphoreType.DMA((9,)),
        pltpu.SemaphoreType.DMA((CHUNKS, 7)),
        pltpu.SemaphoreType.DMA((CHUNKS, 7)),
        pltpu.SemaphoreType.DMA((3, 6)),
        pltpu.SemaphoreType.DMA((3, 6)),
        pltpu.SemaphoreType.DMA((CHUNKS + 3,)),
    ]
    shapes = (
        jax.ShapeDtypeStruct((D // 8, ROWS), BF16),
        jax.ShapeDtypeStruct((D // 16, HID), BF16),
        jax.ShapeDtypeStruct((D // 16, HID), BF16),
        jax.ShapeDtypeStruct((IMGS, D), BF16),
    )
    results = pl.pallas_call(
        kernel,
        out_shape=shapes,
        in_specs=[hbm, hbm, hbm, vmem, smem, smem, smem],
        out_specs=(hbm, hbm, hbm, hbm),
        scratch_shapes=scratch,
        compiler_params=pltpu.CompilerParams(
            collective_id=0, has_side_effects=True, vmem_limit_bytes=61 * 2**20
        ),
        cost_estimate=pl.CostEstimate(
            flops=6 * ROWS * D * HID, bytes_accessed=14 * 2**20, transcendentals=2 * ROWS * HID
        ),
    )(tokens, w_in, w_out, text_emb, labels, logit_scale, logit_bias)
    token_t, w_in_grad, w_out_t, text_grad = pl.pallas_call(
        hand_out,
        out_shape=shapes,
        in_specs=[vmem, vmem, vmem, vmem],
        out_specs=(vmem, vmem, vmem, vmem),
        compiler_params=pltpu.CompilerParams(vmem_limit_bytes=61 * 2**20),
        cost_estimate=pl.CostEstimate(flops=0, bytes_accessed=2 * 2**20, transcendentals=0),
    )(*results)
    return token_t.T, w_in_grad, w_out_t.T, text_grad


def solution(mesh):
    in_specs = (
        P("dp", None),
        P(None, "tensor"),
        P("tensor", None),
        P("dp", None),
        P("dp"),
        P(),
        P(),
    )
    out_specs = (P("dp", "tensor"), P("dp", "tensor"), P("tensor", "dp"), P("dp", None))
    return jax.shard_map(body, mesh=mesh, in_specs=in_specs, out_specs=out_specs, check_vma=False)
```

```python
import math

import jax
import jax.numpy as jnp
from jax import lax
from jax.experimental import pallas as pl
from jax.experimental.pallas import tpu as pltpu
from jax.sharding import PartitionSpec as P

F32 = jnp.float32
BF16 = jnp.bfloat16

D = 1536
HALF = D // 2
HID = 768
ROWS = 2048
TOKS = 256
IMGS = 8
LOSS_SCALE = 64.0
EPS = 1e-06
GELU_A = math.sqrt(2.0 / math.pi)
GELU_B = 0.044715

CHUNKS = 8
GROUPS = 2
PER = CHUNKS // GROUPS
PAIR_FIRST = 3

NN = (((1,), (0,)), ((), ()))
NT = (((1,), (1,)), ((), ()))
TN = (((0,), (0,)), ((), ()))


def dot(a, b, dims=NN):
    return lax.dot_general(a, b, dims, preferred_element_type=F32)


def kernel(
    tokens_hbm, w_in_hbm, w_out_hbm, text_ref, labels_ref, scale_ref, bias_ref,
    out_hbm, win_hbm, wout_hbm, tgrad_hbm,
    tok, inv, hpre, hs, cur, nxt, tok_t, w_in, w_out,
    tmean, mlp_out, pooled, pgs, egs, csum, sums, inv_t, shift_t, eg_t, tdir,
    texts, ebuf, msgs,
    q, ra, rb, sa, sb, yr, yq,
    g, gc, gx, gra, grb, gsa, gsb, gyr,
    out, win, wout, tgrad,
    tok_sem, w_sem,
    text_ss, text_rs, emb_ss, emb_rs, msg_ss, msg_rs,
    q_ss, q_rs, g_ss, g_rs, out_sem,
):
    dp = lax.axis_index("dp")
    tp = lax.axis_index("tensor")
    yh, local = dp // 8, dp % 8
    x, core = local // 2, dp % 2
    z, y = tp // 2, tp % 2

    def mesh_z(step):
        return (dp, ((z + step) % 4) * 2 + y)

    def mesh_x(step):
        return (yh * 8 + ((x + step) % 4) * 2 + core, tp)

    y_pair = (dp, z * 2 + (1 - y))
    core_pair = (dp - core + (1 - core), tp)
    y_far = ((1 - yh) * 8 + local, tp)

    def remote(src, dst, ssem, rsem, dev):
        return pltpu.make_async_remote_copy(
            src_ref=src, dst_ref=dst, send_sem=ssem, recv_sem=rsem,
            device_id=dev, device_id_type=pl.DeviceIdType.MESH,
        )

    def tok_copy(c):
        rows = pl.ds(c * TOKS, TOKS)
        return pltpu.make_async_copy(tokens_hbm.at[rows], tok.at[rows], tok_sem.at[c])

    def w_in_copy(k):
        feats = pl.ds(k * 256, 256)
        return pltpu.make_async_copy(w_in_hbm.at[feats], w_in.at[feats], w_sem.at[k])

    w_out_copy = pltpu.make_async_copy(w_out_hbm, w_out, w_sem.at[6])
    tok_copy(0).start()
    for k in range(6):
        w_in_copy(k).start()
    tok_copy(1).start()

    barrier = pltpu.get_barrier_semaphore()

    def greet(dev):
        pl.semaphore_signal(barrier, inc=1, device_id=dev, device_id_type=pl.DeviceIdType.MESH)

    greet(y_far)
    greet(core_pair)
    for k in range(1, 4):
        greet(mesh_x(k))
    for k in range(1, 8):
        greet((dp, (tp + k) % 8))

    mine, far = yh * 4 + x, (1 - yh) * 4 + x
    text_vals = text_ref[...].astype(F32)
    text_inv = lax.rsqrt(jnp.sum(text_vals * text_vals, axis=1, keepdims=True) + EPS)
    text_nrm = text_vals * text_inv
    texts[core, mine] = jnp.concatenate([text_nrm[:, :HALF], text_nrm[:, HALF:]], axis=0).astype(BF16)
    tmean[...] = jnp.zeros_like(tmean)
    mlp_out[...] = jnp.zeros_like(mlp_out)
    pooled[...] = jnp.zeros_like(pooled)

    def gather_far(buf, ss, rs):
        return remote(buf.at[core, mine], buf.at[core, mine], ss.at[0], rs.at[mine], y_far)

    def gather_x(buf, slot, k, ss, rs, first):
        block = buf.at[core, slot]
        return remote(block, block, ss.at[first + k], rs.at[slot], mesh_x(k))

    def gather_core(buf, ss, rs):
        return remote(buf.at[core], buf.at[core], ss.at[7], rs.at[8], core_pair)

    def gather_first(buf, ss, rs):
        gather_far(buf, ss, rs).start()
        for k in range(1, 4):
            gather_x(buf, mine, k, ss, rs, 0).start()

    def gather_relay(buf, ss, rs):
        gather_x(buf, far, 1, ss, rs, 3).wait_recv()
        for k in range(1, 4):
            gather_x(buf, far, k, ss, rs, 3).start()

    def gather_pass(buf, ss, rs):
        for k in range(1, 4):
            for side in range(2):
                gather_x(buf, side * 4 + (x + k) % 4, k, ss, rs, 0).wait_recv()
        gather_core(buf, ss, rs).start()

    def gather_rest(buf, ss, rs):
        remote(buf.at[1 - core], buf.at[1 - core], ss.at[7], rs.at[8], core_pair).wait_recv()

    def gather_sent(buf, ss, rs):
        gather_far(buf, ss, rs).wait_send()
        for k in range(1, 4):
            gather_x(buf, mine, k, ss, rs, 0).wait_send()
            gather_x(buf, far, k, ss, rs, 3).wait_send()
        gather_core(buf, ss, rs).wait_send()

    def split(vals):
        top = vals.astype(BF16).astype(F32)
        return jnp.concatenate(
            [top, vals - top, jnp.zeros((14,) + vals.shape[1:], F32)], axis=0
        ).astype(BF16)

    def chunk_rows(c):
        return pl.ds(pl.multiple_of(c * TOKS, TOKS), TOKS)

    def forward(c):
        accs = [
            dot(tok[chunk_rows(c), :], w_in[0:D, j * 256:(j + 1) * 256]) for j in range(3)
        ]
        means, scales, shifts = [], [], []
        acc = jnp.zeros((8, D), F32)
        for b in range(TOKS // 16):
            rows = pl.ds(pl.multiple_of(c * TOKS + b * 16, 16), 16)
            vals = tok[rows, :].astype(F32)
            mean = jnp.sum(vals, axis=1, keepdims=True) * (1.0 / D)
            center = vals - mean
            var = jnp.sum(center * center, axis=1, keepdims=True) * (1.0 / D)
            scale = lax.rsqrt(var + EPS)
            shift = mean * scale
            inv[rows, :] = scale
            means.append(mean)
            scales.append(scale)
            shifts.append(shift)
            acc = acc + (vals[:8] + vals[8:])
        tok_t[0:D, chunk_rows(c)] = tok[chunk_rows(c), :].T
        lane = lax.broadcasted_iota(jnp.int32, (TOKS, 128), 1)
        trio = jnp.where(lane == 0, jnp.concatenate(scales, 0), jnp.concatenate(shifts, 0))
        trio = jnp.where(lane == 2, jnp.concatenate(means, 0), trio).T
        inv_t[pl.ds(c, 1), :] = trio[0:1, :]
        shift_t[pl.ds(c, 1), :] = trio[1:2, :]
        tok_t[D:D + 16, chunk_rows(c)] = split(trio[2:3, :])
        tmean[pl.ds(c, 1), :] = jnp.sum(acc, axis=0, keepdims=True) * (1.0 / TOKS)
        for j in range(3):
            cols = slice(j * 256, (j + 1) * 256)
            cs = csum[:, cols]
            acc = jnp.zeros((8, 256), F32)
            for b in range(TOKS // 16):
                rows = pl.ds(pl.multiple_of(c * TOKS + b * 16, 16), 16)
                h = accs[j][b * 16:(b + 1) * 16] * scales[b] - shifts[b] * cs
                hpre[rows, cols] = h
                t = jnp.tanh(h * (GELU_A + (GELU_A * GELU_B) * (h * h)))
                act = h + h * t
                acc = acc + (act[:8] + act[8:])
            pooled[pl.ds(c, 1), cols] = jnp.sum(acc, axis=0, keepdims=True) * (0.5 / TOKS)

    def emb_copy(n, k):
        return remote(
            ebuf.at[n, tp], ebuf.at[n, tp], emb_ss.at[n, k], emb_rs.at[n, tp], (dp, (tp + k) % 8)
        )

    def exchange_start(n):
        part = dot(pooled[...].astype(BF16), w_out[...])
        own = jnp.where(n == 0, part[:PER], part[PER:])
        ebuf[n, tp] = jnp.concatenate(
            [own[:, k * 384:(k + 1) * 384] for k in range(4)], axis=0
        ).astype(BF16)

        @pl.loop(1, 8)
        def _(k):
            emb_copy(n, k).start()

    def exchange_wait(n):
        @pl.loop(1, 8)
        def _(k):
            src = (tp + k) % 8
            remote(
                ebuf.at[n, src], ebuf.at[n, src], emb_ss.at[n, k], emb_rs.at[n, src], (dp, src)
            ).wait_recv()

    def both(sums):
        total = sums[:IMGS] + sums[IMGS:]
        return jnp.concatenate([total, total], axis=0)

    scale = scale_ref[0]

    def loss(n):
        tm = tmean[...]
        own = ebuf[n, 0].astype(F32)
        for k in range(1, 8):
            own = own + ebuf[n, k].astype(F32)
        own = jnp.concatenate([own[k * PER:(k + 1) * PER] for k in range(4)], axis=1)
        image = lax.broadcasted_iota(jnp.int32, (IMGS, D), 0)
        mlp = jnp.where(image // PER == n, jnp.concatenate([own, own], axis=0), mlp_out[...])
        mlp_out[...] = mlp
        full = tm + mlp
        emb = jnp.concatenate([full[:, :HALF], full[:, HALF:]], axis=0)
        emb_inv = lax.rsqrt(both(jnp.sum(emb * emb, axis=1, keepdims=True)) + EPS)
        image_bf = (emb * emb_inv).astype(BF16)
        text_all = texts[...].reshape(256, HALF)
        prod = dot(image_bf, text_all, NT)
        logits = scale * (prod[:IMGS] + pltpu.roll(prod[IMGS:], 256 - IMGS, 1)) + bias_ref[0]
        lane = lax.broadcasted_iota(jnp.int32, (IMGS, 256), 1)
        row = lax.broadcasted_iota(jnp.int32, (IMGS, 256), 0)
        valid = (lane % 16) < 8
        slot = lane // 16
        text_id = ((slot // 4) % 2 * 8 + slot % 4 * 2 + slot // 8) * 8 + lane % 16
        label = jnp.zeros((IMGS, 256), jnp.int32)
        for k in range(IMGS):
            label = jnp.where(row == k, labels_ref[k], label)
        signs = jnp.where(label == text_id, 1.0, -1.0)
        grad = -signs * jax.nn.sigmoid(-signs * logits) * LOSS_SCALE
        grad = jnp.where(valid, grad, 0.0)
        grad = jnp.concatenate([grad, pltpu.roll(grad, IMGS, 1)], axis=0).astype(BF16)
        image_dir = scale * dot(grad, text_all)
        emb_grad = emb_inv * image_dir - (emb_inv * emb_inv * emb_inv) * emb * both(
            jnp.sum(emb * image_dir, axis=1, keepdims=True)
        )
        eg_bf = emb_grad.astype(BF16)
        pgs[...] = (
            dot(eg_bf[:IMGS], w_out[:, :HALF], NT) + dot(eg_bf[IMGS:], w_out[:, HALF:], NT)
        ) * (1.0 / TOKS)
        egs[...] = emb_grad * (1.0 / TOKS)
        msgs[core, mine, :, 0:HALF] = image_bf
        msgs[core, mine, :, HALF:D] = eg_bf
        pooled_f = pooled[...]
        msgs[core, mine, :, D:D + HID] = jnp.concatenate([pooled_f, pooled_f], axis=0).astype(BF16)
        msgs[core, mine, :, D + HID:D + HID + 256] = grad

    def hidden_rows(c):
        half_pg = 0.5 * pgs[pl.ds(c, 1), :]
        second = []
        for b in range(TOKS // 16):
            rows = pl.ds(pl.multiple_of(c * TOKS + b * 16, 16), 16)
            h = hpre[rows, :]
            h2 = h * h
            t = jnp.tanh(h * (GELU_A + (GELU_A * GELU_B) * h2))
            slope = (1.0 + t) + h * (1.0 - t * t) * (GELU_A + (3.0 * GELU_A * GELU_B) * h2)
            grad_bf = (slope * half_pg * inv[rows, :]).astype(BF16)
            hs[rows, :] = grad_bf
            nxt[b * 16:(b + 1) * 16, :] = grad_bf
            p2 = grad_bf.astype(F32) * h
            s2 = p2[:, 0:128]
            for i in range(1, HID // 128):
                s2 = s2 + p2[:, i * 128:(i + 1) * 128]
            second.append(s2)
        m2 = jnp.sum(jnp.concatenate(second, axis=0).T, axis=0, keepdims=True) * (1.0 / D)
        sums[0:1, :] = inv_t[pl.ds(c, 1), :] * m2
        sums[1:2, :] = shift_t[pl.ds(c, 1), :] * m2

    def feature_rows(c):
        rows = chunk_rows(c)
        full = dot(w_in[...], cur[...], NT)
        slope = sums[0:1, :]
        shift = (full[D:D + 1] + full[D + 1:D + 2]) * (1.0 / D) - sums[1:2, :]
        for k in range(8):
            feats = slice(k * 192, (k + 1) * 192)
            block = full[feats] - tok_t[feats, rows].astype(F32) * slope - shift
            q[c, k // 2, k % 2] = block.astype(BF16)

    zp, zn, zo = (z + 1) % 4, (z + 3) % 4, (z + 2) % 4
    up, down = mesh_z(1), mesh_z(3)
    lo, hi = pl.ds(0, 96), pl.ds(96, 96)

    def add_into(dst, a, b):
        dst[...] = (a[...].astype(F32) + b[...].astype(F32)).astype(BF16)

    def pair_copy(c):
        return remote(q.at[c, :, 1 - y], yq.at[c // 2], q_ss.at[c, 0], q_rs.at[c, 0], y_pair)

    def pair_ring1(c):
        return (
            remote(q.at[c, zo, y, lo], ra.at[c, lo], q_ss.at[c, 1], q_rs.at[c, 1], up),
            remote(q.at[c, zo, y, hi], rb.at[c, lo], q_ss.at[c, 2], q_rs.at[c, 2], down),
            remote(q.at[c, zp, y, hi], sa.at[c, 0, hi], q_ss.at[c, 3], q_rs.at[c, 3], up),
            remote(q.at[c, zn, y, lo], sb.at[c, 0, lo], q_ss.at[c, 4], q_rs.at[c, 4], down),
        )

    def pair_ring2(c):
        return (
            remote(q.at[c, zp, y, lo], sa.at[c, 0, lo], q_ss.at[c, 5], q_rs.at[c, 5], up),
            remote(q.at[c, zn, y, hi], sb.at[c, 0, hi], q_ss.at[c, 6], q_rs.at[c, 6], down),
        )

    def ring1(c):
        return (
            remote(q.at[c, zo, 0], ra.at[c], q_ss.at[c, 1], q_rs.at[c, 1], up),
            remote(q.at[c, zo, 1], rb.at[c], q_ss.at[c, 2], q_rs.at[c, 2], down),
            remote(q.at[c, zp, 1], sa.at[c, 1], q_ss.at[c, 3], q_rs.at[c, 3], up),
            remote(q.at[c, zn, 0], sb.at[c, 0], q_ss.at[c, 4], q_rs.at[c, 4], down),
        )

    def ring2(c):
        return (
            remote(q.at[c, zp, 0], sa.at[c, 0], q_ss.at[c, 5], q_rs.at[c, 5], up),
            remote(q.at[c, zn, 1], sb.at[c, 1], q_ss.at[c, 6], q_rs.at[c, 6], down),
        )

    def ring_pair(c):
        return remote(q.at[c, z, 1 - y], yr.at[c], q_ss.at[c, 0], q_rs.at[c, 0], y_pair)

    def start(copies):
        for copy in copies:
            copy.start()

    def pair_b(c):
        pair_copy(c).wait_recv()

        @pl.loop(0, 4)
        def _(zb):
            blk = q.at[c, zb, y]
            add_into(blk, blk, yq.at[c // 2, zb])

        start(pair_ring1(c))

    def ring_b(c):
        first, second = ring1(c)[:2]
        first.wait_recv()
        add_into(q.at[c, zp, 0], q.at[c, zp, 0], ra.at[c])
        second.wait_recv()
        add_into(q.at[c, zn, 1], q.at[c, zn, 1], rb.at[c])
        start(ring2(c))

    def pair_c(c):
        first, second = pair_ring1(c)[:2]
        first.wait_recv()
        add_into(q.at[c, zp, y, lo], q.at[c, zp, y, lo], ra.at[c, lo])
        second.wait_recv()
        add_into(q.at[c, zn, y, hi], q.at[c, zn, y, hi], rb.at[c, lo])
        start(pair_ring2(c))

    def ring_c(c):
        for copy in ring1(c)[2:] + ring2(c):
            copy.wait_recv()

        @pl.loop(0, 2)
        def _(half):
            blk = q.at[c, z, half]
            blk[...] = (
                blk[...].astype(F32) + sa[c, half].astype(F32) + sb[c, half].astype(F32)
            ).astype(BF16)

        ring_pair(c).start()

    def out_copy(c):
        rows = chunk_rows(c)
        return pltpu.make_async_copy(out.at[:, rows], out_hbm.at[:, rows], out_sem.at[c])

    def finish(c, total):
        lane = lax.broadcasted_iota(jnp.int32, (192, 128), 1)
        col = jnp.sum(jnp.where(lane == c, eg_t[0:192, :], 0.0), axis=1, keepdims=True)
        out[:, chunk_rows(c)] = (total + col).astype(BF16)
        out_copy(c).start()

    def pair_d(c):
        for copy in pair_ring1(c)[2:] + pair_ring2(c):
            copy.wait_recv()
        finish(c, q[c, z, y].astype(F32) + sa[c, 0].astype(F32) + sb[c, 0].astype(F32))

    def ring_d(c):
        ring_pair(c).wait_recv()
        finish(c, q[c, z, y].astype(F32) + yr[c].astype(F32))

    xp, xn, xo = (x + 1) % 4, (x + 3) % 4, (x + 2) % 4
    right, left = mesh_x(1), mesh_x(3)

    def core_copy(j):
        return remote(g.at[j, :, :, 1 - core], gc.at[j], g_ss.at[j, 0], g_rs.at[j, 0], core_pair)

    def g1(j):
        return (
            remote(gx.at[j, xo, 0], gra.at[j], g_ss.at[j, 1], g_rs.at[j, 1], right),
            remote(gx.at[j, xo, 1], grb.at[j], g_ss.at[j, 2], g_rs.at[j, 2], left),
        )

    def g2(j):
        return (
            remote(gx.at[j, xp], gsa.at[j], g_ss.at[j, 3], g_rs.at[j, 3], right),
            remote(gx.at[j, xn], gsb.at[j], g_ss.at[j, 4], g_rs.at[j, 4], left),
        )

    def g3(j):
        return remote(gx.at[j, x, 1 - yh], gyr.at[j], g_ss.at[j, 5], g_rs.at[j, 5], y_far)

    def weight_a(j):
        cols = pl.ds(pl.multiple_of(j * 256, 256), 256)
        full = dot(tok_t[...], hs[:, cols])
        lift = full[D:D + 1] + full[D + 1:D + 2]
        g[j] = (full[:D] - lift).astype(BF16).reshape(4, 2, 2, 96, 256)
        core_copy(j).start()

    def weight_b(j):
        core_copy(j).wait_recv()

        @pl.loop(0, 8)
        def _(k):
            xb, yb = k // 2, k % 2
            i, m = yb * 2 + xb // 2, xb % 2
            add_into(gx.at[j, xb, yb], g.at[j, i, m, core], gc.at[j, i, m])

        start(g1(j))

    def weight_c(j):
        first, second = g1(j)
        first.wait_recv()
        add_into(gx.at[j, xp, 0], gx.at[j, xp, 0], gra.at[j])
        second.wait_recv()
        add_into(gx.at[j, xn, 1], gx.at[j, xn, 1], grb.at[j])
        start(g2(j))

    def weight_d(j):
        for copy in g2(j):
            copy.wait_recv()
        for half in range(2):
            blk = gx.at[j, x, half]
            blk[...] = (
                blk[...].astype(F32) + gsa[j, half].astype(F32) + gsb[j, half].astype(F32)
            ).astype(BF16)
        g3(j).start()

    def weight_e():
        for j in range(3):
            g3(j).wait_recv()
            win[:, j * 256:(j + 1) * 256] = (
                gx[j, x, yh].astype(F32) + gyr[j].astype(F32)
            ).astype(BF16)
        small_out(win, win_hbm, 0).start()

    def small_out(src, dst, k):
        return pltpu.make_async_copy(src, dst, out_sem.at[CHUNKS + k])

    def gathered():
        gather_rest(msgs, msg_ss, msg_rs)
        all_msgs = msgs[...].reshape(256, D + HID + 256)
        tdir[...] = dot(all_msgs[:, D + HID:], all_msgs[:, :HALF], TN)
        text_dir = scale * tdir[pl.ds(pl.multiple_of((core * 8 + mine) * 16, 16), 16), :]
        text_dir = jnp.concatenate([text_dir[:IMGS], text_dir[IMGS:]], axis=1)
        vals = text_ref[...].astype(F32)
        t_inv = lax.rsqrt(jnp.sum(vals * vals, axis=1, keepdims=True) + EPS)
        tgrad[...] = (
            t_inv * text_dir
            - (t_inv * t_inv * t_inv) * vals * jnp.sum(vals * text_dir, axis=1, keepdims=True)
        ).astype(BF16)
        small_out(tgrad, tgrad_hbm, 1).start()
        feat = lax.broadcasted_iota(jnp.int32, (HALF, 128), 0)
        col = lax.broadcasted_iota(jnp.int32, (HALF, 128), 1)
        pick = jnp.where(feat == col + local * 96, 1.0, 0.0).astype(BF16)
        emb_cols = dot(all_msgs[:, HALF:D], pick)
        slot_row = lax.broadcasted_iota(jnp.int32, (256, 128), 0)
        emb_cols = jnp.where((slot_row // 8) % 2 == yh, emb_cols, 0.0).astype(BF16)
        wout[...] = dot(emb_cols, all_msgs[:, D:D + HID], TN)[:96].astype(BF16)
        small_out(wout, wout_hbm, 2).start()

    def own_columns():
        cols = egs[pl.ds(pl.multiple_of((z // 2) * 8, 8), 8),
                   pl.ds(pl.multiple_of((z % 2) * 384, 128), 384)]
        cols = jnp.where(y == 0, cols[:, :192], cols[:, 192:])
        square = jnp.concatenate([cols, jnp.zeros((8, 64), F32)], axis=1)
        square = jnp.concatenate([square, jnp.zeros((120, 256), F32)], axis=0)
        eg_t[...] = square.T

    for k in range(6):
        w_in_copy(k).wait()

    @pl.loop(2, CHUNKS)
    def _(c):
        tok_copy(c).start()

    w_out_copy.start()
    cs = dot(jnp.full((16, D), 1.0, BF16), w_in[0:D, :])[0:1]
    csum[...] = cs
    w_in[D:D + 16, :] = split(cs)
    pl.semaphore_wait(barrier, 12)
    gather_first(texts, text_ss, text_rs)

    def is_pair(c):
        return (c % 2 == 1) & (c < 6)

    def forward_loop(first, last):
        @pl.loop(first, last)
        def _(c):
            tok_copy(c).wait()
            forward(c)

    @pl.loop(0, 3)
    def _(stage):
        @pl.when(stage < 2)
        def _():
            @pl.loop(5 * stage, 4 + 4 * stage)
            def _(c):
                tok_copy(c).wait()
                forward(c)

                @pl.when(c == 5)
                def _():
                    ring_b(0)

            @pl.when(stage == 0)
            def _():
                w_out_copy.wait()

            exchange_start(stage)

        @pl.when(stage == 0)
        def _():
            gather_relay(texts, text_ss, text_rs)
            forward_loop(4, 5)
            gather_pass(texts, text_ss, text_rs)

        @pl.when(stage != 1)
        def _():
            n = stage // 2
            exchange_wait(n)

            @pl.when(n == 0)
            def _():
                gather_rest(texts, text_ss, text_rs)

            loss(n)

            @pl.when(n == 1)
            def _():
                gather_first(msgs, msg_ss, msg_rs)
                pair_b(1)
                ring_b(2)

            hidden_rows(n * PER)

        @pl.loop(2 * stage, 2 * stage + 2 + 2 * (stage // 2))
        def _(c):
            cur[...] = nxt[...]
            feature_rows(c)

            @pl.when(is_pair(c))
            def _():
                pair_copy(c).start()

            @pl.when(jnp.logical_not(is_pair(c)))
            def _():
                start(ring1(c))

            hidden_rows(c + 1 - (c % 4) // 3)

            @pl.when(c == 2)
            def _():
                ring_c(0)

            @pl.when(c == 5)
            def _():
                pair_c(1)

            @pl.when(c == 6)
            def _():
                ring_c(2)
                gather_relay(msgs, msg_ss, msg_rs)

            @pl.when(c == 7)
            def _():
                ring_b(4)

    own_columns()

    @pl.loop(0, 3)
    def _(j):
        weight_a(j)

        @pl.when(j == 0)
        def _():
            ring_b(6)
            gather_pass(msgs, msg_ss, msg_rs)

        @pl.when(j == 1)
        def _():
            pair_b(3)
            weight_b(0)

        @pl.when(j == 2)
        def _():
            ring_b(7)
            ring_c(4)

    weight_b(1)
    weight_c(0)
    pair_c(3)
    weight_b(2)
    ring_d(0)
    pair_d(1)
    gathered()
    pair_b(5)
    ring_c(6)
    weight_c(1)
    weight_d(0)
    weight_c(2)
    ring_d(2)
    pair_c(5)
    ring_c(7)
    weight_d(1)
    pair_d(3)
    weight_d(2)
    ring_d(4)
    ring_d(6)
    weight_e()
    pair_d(5)
    ring_d(7)

    @pl.loop(0, CHUNKS)
    def _(c):
        out_copy(c).wait()

        @pl.when(is_pair(c))
        def _():
            for copy in (pair_copy(c),) + pair_ring1(c) + pair_ring2(c):
                copy.wait_send()

        @pl.when(jnp.logical_not(is_pair(c)))
        def _():
            for copy in (ring_pair(c),) + ring1(c) + ring2(c):
                copy.wait_send()

    @pl.loop(0, 3)
    def _(j):
        for copy in (core_copy(j), g3(j)) + g1(j) + g2(j):
            copy.wait_send()

    @pl.loop(1, 8)
    def _(k):
        for n in range(GROUPS):
            emb_copy(n, k).wait_send()

    gather_sent(texts, text_ss, text_rs)
    gather_sent(msgs, msg_ss, msg_rs)
    small_out(win, win_hbm, 0).wait()
    small_out(tgrad, tgrad_hbm, 1).wait()
    small_out(wout, wout_hbm, 2).wait()


def hand_out(a, b, c, d, a_out, b_out, c_out, d_out):
    a_out[...] = a[...]
    b_out[...] = b[...]
    c_out[...] = c[...]
    d_out[...] = d[...]


def body(tokens, w_in, w_out, text_emb, labels, logit_scale, logit_bias):
    vmem = pl.BlockSpec(memory_space=pltpu.VMEM)
    smem = pl.BlockSpec(memory_space=pltpu.SMEM)
    hbm = pl.BlockSpec(memory_space=pl.ANY)
    msg = D + HID + 256
    scratch = [
        pltpu.VMEM((ROWS, D), BF16),
        pltpu.VMEM((ROWS, 1), F32),
        pltpu.VMEM((ROWS, HID), F32),
        pltpu.VMEM((ROWS, HID), BF16),
        pltpu.VMEM((TOKS, HID), BF16),
        pltpu.VMEM((TOKS, HID), BF16),
        pltpu.VMEM((D + 16, ROWS), BF16),
        pltpu.VMEM((D + 16, HID), BF16),
        pltpu.VMEM((HID, D), BF16),
        pltpu.VMEM((IMGS, D), F32),
        pltpu.VMEM((IMGS, D), F32),
        pltpu.VMEM((IMGS, HID), F32),
        pltpu.VMEM((IMGS, HID), F32),
        pltpu.VMEM((16, HALF), F32),
        pltpu.VMEM((1, HID), F32),
        pltpu.VMEM((8, TOKS), F32),
        pltpu.VMEM((CHUNKS, TOKS), F32),
        pltpu.VMEM((CHUNKS, TOKS), F32),
        pltpu.VMEM((256, 128), F32),
        pltpu.VMEM((256, HALF), F32),
        pltpu.VMEM((2, 8, 16, HALF), BF16),
        pltpu.VMEM((GROUPS, 8, 16, 384), BF16),
        pltpu.VMEM((2, 8, 16, msg), BF16),
        pltpu.VMEM((CHUNKS, 4, 2, 192, TOKS), BF16),
        pltpu.VMEM((CHUNKS, 192, TOKS), BF16),
        pltpu.VMEM((CHUNKS, 192, TOKS), BF16),
        pltpu.VMEM((CHUNKS, 2, 192, TOKS), BF16),
        pltpu.VMEM((CHUNKS, 2, 192, TOKS), BF16),
        pltpu.VMEM((CHUNKS, 192, TOKS), BF16),
        pltpu.VMEM((PAIR_FIRST, 4, 192, TOKS), BF16),
        pltpu.VMEM((3, 4, 2, 2, 96, 256), BF16),
        pltpu.VMEM((3, 4, 2, 96, 256), BF16),
        pltpu.VMEM((3, 4, 2, 96, 256), BF16),
        pltpu.VMEM((3, 96, 256), BF16),
        pltpu.VMEM((3, 96, 256), BF16),
        pltpu.VMEM((3, 2, 96, 256), BF16),
        pltpu.VMEM((3, 2, 96, 256), BF16),
        pltpu.VMEM((3, 96, 256), BF16),
        pltpu.VMEM((192, ROWS), BF16),
        pltpu.VMEM((96, HID), BF16),
        pltpu.VMEM((96, HID), BF16),
        pltpu.VMEM((IMGS, D), BF16),
        pltpu.SemaphoreType.DMA((CHUNKS,)),
        pltpu.SemaphoreType.DMA((7,)),
        pltpu.SemaphoreType.DMA((8,)),
        pltpu.SemaphoreType.DMA((9,)),
        pltpu.SemaphoreType.DMA((GROUPS, 8)),
        pltpu.SemaphoreType.DMA((GROUPS, 8)),
        pltpu.SemaphoreType.DMA((8,)),
        pltpu.SemaphoreType.DMA((9,)),
        pltpu.SemaphoreType.DMA((CHUNKS, 7)),
        pltpu.SemaphoreType.DMA((CHUNKS, 7)),
        pltpu.SemaphoreType.DMA((3, 6)),
        pltpu.SemaphoreType.DMA((3, 6)),
        pltpu.SemaphoreType.DMA((CHUNKS + 3,)),
    ]
    shapes = (
        jax.ShapeDtypeStruct((D // 8, ROWS), BF16),
        jax.ShapeDtypeStruct((D // 16, HID), BF16),
        jax.ShapeDtypeStruct((D // 16, HID), BF16),
        jax.ShapeDtypeStruct((IMGS, D), BF16),
    )
    results = pl.pallas_call(
        kernel,
        out_shape=shapes,
        in_specs=[hbm, hbm, hbm, vmem, smem, smem, smem],
        out_specs=(hbm, hbm, hbm, hbm),
        scratch_shapes=scratch,
        compiler_params=pltpu.CompilerParams(
            collective_id=0, has_side_effects=True, vmem_limit_bytes=61 * 2**20
        ),
        cost_estimate=pl.CostEstimate(
            flops=6 * ROWS * D * HID, bytes_accessed=14 * 2**20, transcendentals=2 * ROWS * HID
        ),
    )(tokens, w_in, w_out, text_emb, labels, logit_scale, logit_bias)
    token_t, w_in_grad, w_out_t, text_grad = pl.pallas_call(
        hand_out,
        out_shape=shapes,
        in_specs=[vmem, vmem, vmem, vmem],
        out_specs=(vmem, vmem, vmem, vmem),
        compiler_params=pltpu.CompilerParams(vmem_limit_bytes=61 * 2**20),
        cost_estimate=pl.CostEstimate(flops=0, bytes_accessed=2 * 2**20, transcendentals=0),
    )(*results)
    return token_t.T, w_in_grad, w_out_t.T, text_grad


def solution(mesh):
    in_specs = (
        P("dp", None),
        P(None, "tensor"),
        P("tensor", None),
        P("dp", None),
        P("dp"),
        P(),
        P(),
    )
    out_specs = (P("dp", "tensor"), P("dp", "tensor"), P("tensor", "dp"), P("dp", None))
    return jax.shard_map(body, mesh=mesh, in_specs=in_specs, out_specs=out_specs, check_vma=False)
```

```python
import math

import jax
import jax.numpy as jnp
from jax import lax
from jax.experimental import pallas as pl
from jax.experimental.pallas import tpu as pltpu
from jax.sharding import PartitionSpec as P

F32 = jnp.float32
BF16 = jnp.bfloat16

D = 1536
HALF = D // 2
HID = 768
ROWS = 2048
TOKS = 256
IMGS = 8
LOSS_SCALE = 64.0
EPS = 1e-06
GELU_A = math.sqrt(2.0 / math.pi)
GELU_B = 0.044715

CHUNKS = 8
GROUPS = 2
PER = CHUNKS // GROUPS
PAIR_FIRST = 3

NN = (((1,), (0,)), ((), ()))
NT = (((1,), (1,)), ((), ()))
TN = (((0,), (0,)), ((), ()))


def dot(a, b, dims=NN):
    return lax.dot_general(a, b, dims, preferred_element_type=F32)


def kernel(
    tokens_hbm, w_in_hbm, w_out_hbm, text_ref, labels_ref, scale_ref, bias_ref,
    out_hbm, win_hbm, wout_hbm, tgrad_hbm,
    tok, inv, hpre, hs, cur, nxt, tok_t, w_in, w_out,
    tmean, mlp_out, pooled, pgs, egs, csum, sums, inv_t, shift_t, eg_t, tdir,
    texts, ebuf, msgs,
    q, ra, rb, sa, sb, yr, yq,
    g, gc, gx, gra, grb, gsa, gsb, gyr,
    out, win, wout, tgrad,
    tok_sem, w_sem,
    text_ss, text_rs, emb_ss, emb_rs, msg_ss, msg_rs,
    q_ss, q_rs, g_ss, g_rs, out_sem,
):
    dp = lax.axis_index("dp")
    tp = lax.axis_index("tensor")
    yh, local = dp // 8, dp % 8
    x, core = local // 2, dp % 2
    z, y = tp // 2, tp % 2

    def mesh_z(step):
        return (dp, ((z + step) % 4) * 2 + y)

    def mesh_x(step):
        return (yh * 8 + ((x + step) % 4) * 2 + core, tp)

    y_pair = (dp, z * 2 + (1 - y))
    core_pair = (dp - core + (1 - core), tp)
    y_far = ((1 - yh) * 8 + local, tp)

    def remote(src, dst, ssem, rsem, dev):
        return pltpu.make_async_remote_copy(
            src_ref=src, dst_ref=dst, send_sem=ssem, recv_sem=rsem,
            device_id=dev, device_id_type=pl.DeviceIdType.MESH,
        )

    def tok_copy(c):
        rows = pl.ds(c * TOKS, TOKS)
        return pltpu.make_async_copy(tokens_hbm.at[rows], tok.at[rows], tok_sem.at[c])

    def w_in_copy(k):
        feats = pl.ds(k * 256, 256)
        return pltpu.make_async_copy(w_in_hbm.at[feats], w_in.at[feats], w_sem.at[k])

    w_out_copy = pltpu.make_async_copy(w_out_hbm, w_out, w_sem.at[6])
    tok_copy(0).start()
    for k in range(6):
        w_in_copy(k).start()
    tok_copy(1).start()

    barrier = pltpu.get_barrier_semaphore()

    def greet(dev):
        pl.semaphore_signal(barrier, inc=1, device_id=dev, device_id_type=pl.DeviceIdType.MESH)

    greet(y_far)
    greet(core_pair)
    for k in range(1, 4):
        greet(mesh_x(k))
    for k in range(1, 8):
        greet((dp, (tp + k) % 8))

    mine, far = yh * 4 + x, (1 - yh) * 4 + x
    text_vals = text_ref[...].astype(F32)
    text_inv = lax.rsqrt(jnp.sum(text_vals * text_vals, axis=1, keepdims=True) + EPS)
    text_nrm = text_vals * text_inv
    texts[core, mine] = jnp.concatenate([text_nrm[:, :HALF], text_nrm[:, HALF:]], axis=0).astype(BF16)
    tmean[...] = jnp.zeros_like(tmean)
    mlp_out[...] = jnp.zeros_like(mlp_out)
    pooled[...] = jnp.zeros_like(pooled)

    def gather_far(buf, ss, rs):
        return remote(buf.at[core, mine], buf.at[core, mine], ss.at[0], rs.at[mine], y_far)

    def gather_x(buf, slot, k, ss, rs, first):
        block = buf.at[core, slot]
        return remote(block, block, ss.at[first + k], rs.at[slot], mesh_x(k))

    def gather_core(buf, ss, rs):
        return remote(buf.at[core], buf.at[core], ss.at[7], rs.at[8], core_pair)

    def gather_first(buf, ss, rs):
        gather_far(buf, ss, rs).start()
        for k in range(1, 4):
            gather_x(buf, mine, k, ss, rs, 0).start()

    def gather_relay(buf, ss, rs):
        gather_x(buf, far, 1, ss, rs, 3).wait_recv()
        for k in range(1, 4):
            gather_x(buf, far, k, ss, rs, 3).start()

    def gather_pass(buf, ss, rs):
        for k in range(1, 4):
            for side in range(2):
                gather_x(buf, side * 4 + (x + k) % 4, k, ss, rs, 0).wait_recv()
        gather_core(buf, ss, rs).start()

    def gather_rest(buf, ss, rs):
        remote(buf.at[1 - core], buf.at[1 - core], ss.at[7], rs.at[8], core_pair).wait_recv()

    def gather_sent(buf, ss, rs):
        gather_far(buf, ss, rs).wait_send()
        for k in range(1, 4):
            gather_x(buf, mine, k, ss, rs, 0).wait_send()
            gather_x(buf, far, k, ss, rs, 3).wait_send()
        gather_core(buf, ss, rs).wait_send()

    def split(vals):
        top = vals.astype(BF16).astype(F32)
        return jnp.concatenate(
            [top, vals - top, jnp.zeros((14,) + vals.shape[1:], F32)], axis=0
        ).astype(BF16)

    def chunk_rows(c):
        return pl.ds(pl.multiple_of(c * TOKS, TOKS), TOKS)

    def forward(c):
        accs = [
            dot(tok[chunk_rows(c), :], w_in[0:D, j * 256:(j + 1) * 256]) for j in range(3)
        ]
        means, scales, shifts = [], [], []
        acc = jnp.zeros((8, D), F32)
        for b in range(TOKS // 16):
            rows = pl.ds(pl.multiple_of(c * TOKS + b * 16, 16), 16)
            vals = tok[rows, :].astype(F32)
            mean = jnp.sum(vals, axis=1, keepdims=True) * (1.0 / D)
            center = vals - mean
            var = jnp.sum(center * center, axis=1, keepdims=True) * (1.0 / D)
            scale = lax.rsqrt(var + EPS)
            shift = mean * scale
            inv[rows, :] = scale
            means.append(mean)
            scales.append(scale)
            shifts.append(shift)
            acc = acc + (vals[:8] + vals[8:])
        tok_t[0:D, chunk_rows(c)] = tok[chunk_rows(c), :].T
        lane = lax.broadcasted_iota(jnp.int32, (TOKS, 128), 1)
        trio = jnp.where(lane == 0, jnp.concatenate(scales, 0), jnp.concatenate(shifts, 0))
        trio = jnp.where(lane == 2, jnp.concatenate(means, 0), trio).T
        inv_t[pl.ds(c, 1), :] = trio[0:1, :]
        shift_t[pl.ds(c, 1), :] = trio[1:2, :]
        tok_t[D:D + 16, chunk_rows(c)] = split(trio[2:3, :])
        tmean[pl.ds(c, 1), :] = jnp.sum(acc, axis=0, keepdims=True) * (1.0 / TOKS)
        for j in range(3):
            cols = slice(j * 256, (j + 1) * 256)
            cs = csum[:, cols]
            acc = jnp.zeros((8, 256), F32)
            for b in range(TOKS // 16):
                rows = pl.ds(pl.multiple_of(c * TOKS + b * 16, 16), 16)
                h = accs[j][b * 16:(b + 1) * 16] * scales[b] - shifts[b] * cs
                hpre[rows, cols] = h
                t = jnp.tanh(h * (GELU_A + (GELU_A * GELU_B) * (h * h)))
                act = h + h * t
                acc = acc + (act[:8] + act[8:])
            pooled[pl.ds(c, 1), cols] = jnp.sum(acc, axis=0, keepdims=True) * (0.5 / TOKS)

    def emb_copy(n, k):
        return remote(
            ebuf.at[n, tp], ebuf.at[n, tp], emb_ss.at[n, k], emb_rs.at[n, tp], (dp, (tp + k) % 8)
        )

    def exchange_start(n):
        part = dot(pooled[...].astype(BF16), w_out[...])
        own = jnp.where(n == 0, part[:PER], part[PER:])
        ebuf[n, tp] = jnp.concatenate(
            [own[:, k * 384:(k + 1) * 384] for k in range(4)], axis=0
        ).astype(BF16)

        @pl.loop(1, 8)
        def _(k):
            emb_copy(n, k).start()

    def exchange_wait(n):
        @pl.loop(1, 8)
        def _(k):
            src = (tp + k) % 8
            remote(
                ebuf.at[n, src], ebuf.at[n, src], emb_ss.at[n, k], emb_rs.at[n, src], (dp, src)
            ).wait_recv()

    def both(sums):
        total = sums[:IMGS] + sums[IMGS:]
        return jnp.concatenate([total, total], axis=0)

    scale = scale_ref[0]

    def loss(n):
        tm = tmean[...]
        own = ebuf[n, 0].astype(F32)
        for k in range(1, 8):
            own = own + ebuf[n, k].astype(F32)
        own = jnp.concatenate([own[k * PER:(k + 1) * PER] for k in range(4)], axis=1)
        image = lax.broadcasted_iota(jnp.int32, (IMGS, D), 0)
        mlp = jnp.where(image // PER == n, jnp.concatenate([own, own], axis=0), mlp_out[...])
        mlp_out[...] = mlp
        full = tm + mlp
        emb = jnp.concatenate([full[:, :HALF], full[:, HALF:]], axis=0)
        emb_inv = lax.rsqrt(both(jnp.sum(emb * emb, axis=1, keepdims=True)) + EPS)
        image_bf = (emb * emb_inv).astype(BF16)
        text_all = texts[...].reshape(256, HALF)
        prod = dot(image_bf, text_all, NT)
        logits = scale * (prod[:IMGS] + pltpu.roll(prod[IMGS:], 256 - IMGS, 1)) + bias_ref[0]
        lane = lax.broadcasted_iota(jnp.int32, (IMGS, 256), 1)
        row = lax.broadcasted_iota(jnp.int32, (IMGS, 256), 0)
        valid = (lane % 16) < 8
        slot = lane // 16
        text_id = ((slot // 4) % 2 * 8 + slot % 4 * 2 + slot // 8) * 8 + lane % 16
        label = jnp.zeros((IMGS, 256), jnp.int32)
        for k in range(IMGS):
            label = jnp.where(row == k, labels_ref[k], label)
        signs = jnp.where(label == text_id, 1.0, -1.0)
        grad = -signs * jax.nn.sigmoid(-signs * logits) * LOSS_SCALE
        grad = jnp.where(valid, grad, 0.0)
        grad = jnp.concatenate([grad, pltpu.roll(grad, IMGS, 1)], axis=0).astype(BF16)
        image_dir = scale * dot(grad, text_all)
        emb_grad = emb_inv * image_dir - (emb_inv * emb_inv * emb_inv) * emb * both(
            jnp.sum(emb * image_dir, axis=1, keepdims=True)
        )
        eg_bf = emb_grad.astype(BF16)
        pgs[...] = (
            dot(eg_bf[:IMGS], w_out[:, :HALF], NT) + dot(eg_bf[IMGS:], w_out[:, HALF:], NT)
        ) * (1.0 / TOKS)
        egs[...] = emb_grad * (1.0 / TOKS)
        msgs[core, mine, :, 0:HALF] = image_bf
        msgs[core, mine, :, HALF:D] = eg_bf
        pooled_f = pooled[...]
        msgs[core, mine, :, D:D + HID] = jnp.concatenate([pooled_f, pooled_f], axis=0).astype(BF16)
        msgs[core, mine, :, D + HID:D + HID + 256] = grad

    def hidden_rows(c):
        half_pg = 0.5 * pgs[pl.ds(c, 1), :]
        second = []
        for b in range(TOKS // 16):
            rows = pl.ds(pl.multiple_of(c * TOKS + b * 16, 16), 16)
            h = hpre[rows, :]
            h2 = h * h
            t = jnp.tanh(h * (GELU_A + (GELU_A * GELU_B) * h2))
            slope = (1.0 + t) + h * (1.0 - t * t) * (GELU_A + (3.0 * GELU_A * GELU_B) * h2)
            grad_bf = (slope * half_pg * inv[rows, :]).astype(BF16)
            hs[rows, :] = grad_bf
            nxt[b * 16:(b + 1) * 16, :] = grad_bf
            p2 = grad_bf.astype(F32) * h
            s2 = p2[:, 0:128]
            for i in range(1, HID // 128):
                s2 = s2 + p2[:, i * 128:(i + 1) * 128]
            second.append(s2)
        m2 = jnp.sum(jnp.concatenate(second, axis=0).T, axis=0, keepdims=True) * (1.0 / D)
        sums[0:1, :] = inv_t[pl.ds(c, 1), :] * m2
        sums[1:2, :] = shift_t[pl.ds(c, 1), :] * m2

    def feature_rows(c):
        rows = chunk_rows(c)
        full = dot(w_in[...], cur[...], NT)
        slope = sums[0:1, :]
        shift = (full[D:D + 1] + full[D + 1:D + 2]) * (1.0 / D) - sums[1:2, :]
        for k in range(8):
            feats = slice(k * 192, (k + 1) * 192)
            block = full[feats] - tok_t[feats, rows].astype(F32) * slope - shift
            q[c, k // 2, k % 2] = block.astype(BF16)

    zp, zn, zo = (z + 1) % 4, (z + 3) % 4, (z + 2) % 4
    up, down = mesh_z(1), mesh_z(3)
    lo, hi = pl.ds(0, 96), pl.ds(96, 96)

    def add_into(dst, a, b):
        dst[...] = (a[...].astype(F32) + b[...].astype(F32)).astype(BF16)

    def pair_copy(c):
        return remote(q.at[c, :, 1 - y], yq.at[c // 2], q_ss.at[c, 0], q_rs.at[c, 0], y_pair)

    def pair_ring1(c):
        return (
            remote(q.at[c, zo, y, lo], ra.at[c, lo], q_ss.at[c, 1], q_rs.at[c, 1], up),
            remote(q.at[c, zo, y, hi], rb.at[c, lo], q_ss.at[c, 2], q_rs.at[c, 2], down),
            remote(q.at[c, zp, y, hi], sa.at[c, 0, hi], q_ss.at[c, 3], q_rs.at[c, 3], up),
            remote(q.at[c, zn, y, lo], sb.at[c, 0, lo], q_ss.at[c, 4], q_rs.at[c, 4], down),
        )

    def pair_ring2(c):
        return (
            remote(q.at[c, zp, y, lo], sa.at[c, 0, lo], q_ss.at[c, 5], q_rs.at[c, 5], up),
            remote(q.at[c, zn, y, hi], sb.at[c, 0, hi], q_ss.at[c, 6], q_rs.at[c, 6], down),
        )

    def ring1(c):
        return (
            remote(q.at[c, zo, 0], ra.at[c], q_ss.at[c, 1], q_rs.at[c, 1], up),
            remote(q.at[c, zo, 1], rb.at[c], q_ss.at[c, 2], q_rs.at[c, 2], down),
            remote(q.at[c, zp, 1], sa.at[c, 1], q_ss.at[c, 3], q_rs.at[c, 3], up),
            remote(q.at[c, zn, 0], sb.at[c, 0], q_ss.at[c, 4], q_rs.at[c, 4], down),
        )

    def ring2(c):
        return (
            remote(q.at[c, zp, 0], sa.at[c, 0], q_ss.at[c, 5], q_rs.at[c, 5], up),
            remote(q.at[c, zn, 1], sb.at[c, 1], q_ss.at[c, 6], q_rs.at[c, 6], down),
        )

    def ring_pair(c):
        return remote(q.at[c, z, 1 - y], yr.at[c], q_ss.at[c, 0], q_rs.at[c, 0], y_pair)

    def start(copies):
        for copy in copies:
            copy.start()

    def pair_b(c):
        pair_copy(c).wait_recv()

        @pl.loop(0, 4)
        def _(zb):
            blk = q.at[c, zb, y]
            add_into(blk, blk, yq.at[c // 2, zb])

        start(pair_ring1(c))

    def ring_b(c):
        first, second = ring1(c)[:2]
        first.wait_recv()
        add_into(q.at[c, zp, 0], q.at[c, zp, 0], ra.at[c])
        second.wait_recv()
        add_into(q.at[c, zn, 1], q.at[c, zn, 1], rb.at[c])
        start(ring2(c))

    def pair_c(c):
        first, second = pair_ring1(c)[:2]
        first.wait_recv()
        add_into(q.at[c, zp, y, lo], q.at[c, zp, y, lo], ra.at[c, lo])
        second.wait_recv()
        add_into(q.at[c, zn, y, hi], q.at[c, zn, y, hi], rb.at[c, lo])
        start(pair_ring2(c))

    def ring_c(c):
        for copy in ring1(c)[2:] + ring2(c):
            copy.wait_recv()

        @pl.loop(0, 2)
        def _(half):
            blk = q.at[c, z, half]
            blk[...] = (
                blk[...].astype(F32) + sa[c, half].astype(F32) + sb[c, half].astype(F32)
            ).astype(BF16)

        ring_pair(c).start()

    def out_copy(c):
        rows = chunk_rows(c)
        return pltpu.make_async_copy(out.at[:, rows], out_hbm.at[:, rows], out_sem.at[c])

    def finish(c, total):
        lane = lax.broadcasted_iota(jnp.int32, (192, 128), 1)
        col = jnp.sum(jnp.where(lane == c, eg_t[0:192, :], 0.0), axis=1, keepdims=True)
        out[:, chunk_rows(c)] = (total + col).astype(BF16)
        out_copy(c).start()

    def pair_d(c):
        for copy in pair_ring1(c)[2:] + pair_ring2(c):
            copy.wait_recv()
        finish(c, q[c, z, y].astype(F32) + sa[c, 0].astype(F32) + sb[c, 0].astype(F32))

    def ring_d(c):
        ring_pair(c).wait_recv()
        finish(c, q[c, z, y].astype(F32) + yr[c].astype(F32))

    xp, xn, xo = (x + 1) % 4, (x + 3) % 4, (x + 2) % 4
    right, left = mesh_x(1), mesh_x(3)

    def core_copy(j):
        return remote(g.at[j, :, :, 1 - core], gc.at[j], g_ss.at[j, 0], g_rs.at[j, 0], core_pair)

    def g1(j):
        return (
            remote(gx.at[j, xo, 0], gra.at[j], g_ss.at[j, 1], g_rs.at[j, 1], right),
            remote(gx.at[j, xo, 1], grb.at[j], g_ss.at[j, 2], g_rs.at[j, 2], left),
        )

    def g2(j):
        return (
            remote(gx.at[j, xp], gsa.at[j], g_ss.at[j, 3], g_rs.at[j, 3], right),
            remote(gx.at[j, xn], gsb.at[j], g_ss.at[j, 4], g_rs.at[j, 4], left),
        )

    def g3(j):
        return remote(gx.at[j, x, 1 - yh], gyr.at[j], g_ss.at[j, 5], g_rs.at[j, 5], y_far)

    def weight_a(j):
        cols = pl.ds(pl.multiple_of(j * 256, 256), 256)
        full = dot(tok_t[...], hs[:, cols])
        lift = full[D:D + 1] + full[D + 1:D + 2]
        g[j] = (full[:D] - lift).astype(BF16).reshape(4, 2, 2, 96, 256)
        core_copy(j).start()

    def weight_b(j):
        core_copy(j).wait_recv()

        @pl.loop(0, 8)
        def _(k):
            xb, yb = k // 2, k % 2
            i, m = yb * 2 + xb // 2, xb % 2
            add_into(gx.at[j, xb, yb], g.at[j, i, m, core], gc.at[j, i, m])

        start(g1(j))

    def weight_c(j):
        first, second = g1(j)
        first.wait_recv()
        add_into(gx.at[j, xp, 0], gx.at[j, xp, 0], gra.at[j])
        second.wait_recv()
        add_into(gx.at[j, xn, 1], gx.at[j, xn, 1], grb.at[j])
        start(g2(j))

    def weight_d(j):
        for copy in g2(j):
            copy.wait_recv()
        for half in range(2):
            blk = gx.at[j, x, half]
            blk[...] = (
                blk[...].astype(F32) + gsa[j, half].astype(F32) + gsb[j, half].astype(F32)
            ).astype(BF16)
        g3(j).start()

    def weight_e():
        for j in range(3):
            g3(j).wait_recv()
            win[:, j * 256:(j + 1) * 256] = (
                gx[j, x, yh].astype(F32) + gyr[j].astype(F32)
            ).astype(BF16)
        small_out(win, win_hbm, 0).start()

    def small_out(src, dst, k):
        return pltpu.make_async_copy(src, dst, out_sem.at[CHUNKS + k])

    def gathered():
        gather_rest(msgs, msg_ss, msg_rs)
        all_msgs = msgs[...].reshape(256, D + HID + 256)
        tdir[...] = dot(all_msgs[:, D + HID:], all_msgs[:, :HALF], TN)
        text_dir = scale * tdir[pl.ds(pl.multiple_of((core * 8 + mine) * 16, 16), 16), :]
        text_dir = jnp.concatenate([text_dir[:IMGS], text_dir[IMGS:]], axis=1)
        vals = text_ref[...].astype(F32)
        t_inv = lax.rsqrt(jnp.sum(vals * vals, axis=1, keepdims=True) + EPS)
        tgrad[...] = (
            t_inv * text_dir
            - (t_inv * t_inv * t_inv) * vals * jnp.sum(vals * text_dir, axis=1, keepdims=True)
        ).astype(BF16)
        small_out(tgrad, tgrad_hbm, 1).start()
        feat = lax.broadcasted_iota(jnp.int32, (HALF, 128), 0)
        col = lax.broadcasted_iota(jnp.int32, (HALF, 128), 1)
        pick = jnp.where(feat == col + local * 96, 1.0, 0.0).astype(BF16)
        emb_cols = dot(all_msgs[:, HALF:D], pick)
        slot_row = lax.broadcasted_iota(jnp.int32, (256, 128), 0)
        emb_cols = jnp.where((slot_row // 8) % 2 == yh, emb_cols, 0.0).astype(BF16)
        wout[...] = dot(emb_cols, all_msgs[:, D:D + HID], TN)[:96].astype(BF16)
        small_out(wout, wout_hbm, 2).start()

    def own_columns():
        cols = egs[pl.ds(pl.multiple_of((z // 2) * 8, 8), 8),
                   pl.ds(pl.multiple_of((z % 2) * 384, 128), 384)]
        cols = jnp.where(y == 0, cols[:, :192], cols[:, 192:])
        square = jnp.concatenate([cols, jnp.zeros((8, 64), F32)], axis=1)
        square = jnp.concatenate([square, jnp.zeros((120, 256), F32)], axis=0)
        eg_t[...] = square.T

    for k in range(6):
        w_in_copy(k).wait()

    @pl.loop(2, CHUNKS)
    def _(c):
        tok_copy(c).start()

    w_out_copy.start()
    cs = dot(jnp.full((16, D), 1.0, BF16), w_in[0:D, :])[0:1]
    csum[...] = cs
    w_in[D:D + 16, :] = split(cs)
    pl.semaphore_wait(barrier, 12)
    gather_first(texts, text_ss, text_rs)

    def is_pair(c):
        return (c % 2 == 1) & (c < 6)

    def forward_loop(first, last):
        @pl.loop(first, last)
        def _(c):
            tok_copy(c).wait()
            forward(c)

    @pl.loop(0, 4)
    def _(stage):
        later = (stage + 3) // 4

        @pl.when(stage < 3)
        def _():
            @pl.loop(5 * later + stage // 2, 4 + 2 * stage)
            def _(c):
                tok_copy(c).wait()
                forward(c)

                @pl.when(c == 5)
                def _():
                    ring_b(0)

        @pl.when(stage == 0)
        def _():
            w_out_copy.wait()

        @pl.when(stage % 2 == 0)
        def _():
            exchange_start(stage // 2)

        @pl.when(stage == 0)
        def _():
            gather_relay(texts, text_ss, text_rs)
            forward_loop(4, 5)
            gather_pass(texts, text_ss, text_rs)

        @pl.when(stage % 3 == 0)
        def _():
            n = stage // 3
            exchange_wait(n)

            @pl.when(n == 0)
            def _():
                gather_rest(texts, text_ss, text_rs)

            loss(n)

            @pl.when(n == 1)
            def _():
                pair_c(1)
                ring_c(0)

            hidden_rows(n * PER)

        @pl.loop(stage + later, stage + 2 + 3 * (stage // 3))
        def _(c):
            cur[...] = nxt[...]
            feature_rows(c)

            @pl.when(is_pair(c))
            def _():
                pair_copy(c).start()

            @pl.when(jnp.logical_not(is_pair(c)))
            def _():
                start(ring1(c))

            hidden_rows(c + 1 - (c % 4) // 3)

            @pl.when(c == 3)
            def _():
                ring_b(2)
                pair_b(1)

            @pl.when(c == 4)
            def _():
                gather_first(msgs, msg_ss, msg_rs)

            @pl.when(c == 5)
            def _():
                ring_c(2)

            @pl.when(c == 6)
            def _():
                pair_b(3)
                gather_relay(msgs, msg_ss, msg_rs)

            @pl.when(c == 7)
            def _():
                ring_b(4)

    own_columns()

    @pl.loop(0, 3)
    def _(j):
        weight_a(j)

        @pl.when(j == 0)
        def _():
            ring_b(6)
            pair_c(3)
            gather_pass(msgs, msg_ss, msg_rs)

        @pl.when(j == 1)
        def _():
            ring_b(7)
            weight_b(0)

        @pl.when(j == 2)
        def _():
            pair_b(5)
            ring_c(4)

    weight_b(1)
    weight_c(0)
    weight_b(2)
    ring_d(0)
    pair_d(1)
    gathered()
    ring_c(6)
    weight_c(1)
    pair_c(5)
    weight_d(0)
    weight_c(2)
    ring_d(2)
    ring_c(7)
    weight_d(1)
    pair_d(3)
    weight_d(2)
    ring_d(4)
    ring_d(6)
    weight_e()
    pair_d(5)
    ring_d(7)

    @pl.loop(0, CHUNKS)
    def _(c):
        out_copy(c).wait()

        @pl.when(is_pair(c))
        def _():
            for copy in (pair_copy(c),) + pair_ring1(c) + pair_ring2(c):
                copy.wait_send()

        @pl.when(jnp.logical_not(is_pair(c)))
        def _():
            for copy in (ring_pair(c),) + ring1(c) + ring2(c):
                copy.wait_send()

    @pl.loop(0, 3)
    def _(j):
        for copy in (core_copy(j), g3(j)) + g1(j) + g2(j):
            copy.wait_send()

    @pl.loop(1, 8)
    def _(k):
        for n in range(GROUPS):
            emb_copy(n, k).wait_send()

    gather_sent(texts, text_ss, text_rs)
    gather_sent(msgs, msg_ss, msg_rs)
    small_out(win, win_hbm, 0).wait()
    small_out(tgrad, tgrad_hbm, 1).wait()
    small_out(wout, wout_hbm, 2).wait()


def hand_out(a, b, c, d, a_out, b_out, c_out, d_out):
    a_out[...] = a[...]
    b_out[...] = b[...]
    c_out[...] = c[...]
    d_out[...] = d[...]


def body(tokens, w_in, w_out, text_emb, labels, logit_scale, logit_bias):
    vmem = pl.BlockSpec(memory_space=pltpu.VMEM)
    smem = pl.BlockSpec(memory_space=pltpu.SMEM)
    hbm = pl.BlockSpec(memory_space=pl.ANY)
    msg = D + HID + 256
    scratch = [
        pltpu.VMEM((ROWS, D), BF16),
        pltpu.VMEM((ROWS, 1), F32),
        pltpu.VMEM((ROWS, HID), F32),
        pltpu.VMEM((ROWS, HID), BF16),
        pltpu.VMEM((TOKS, HID), BF16),
        pltpu.VMEM((TOKS, HID), BF16),
        pltpu.VMEM((D + 16, ROWS), BF16),
        pltpu.VMEM((D + 16, HID), BF16),
        pltpu.VMEM((HID, D), BF16),
        pltpu.VMEM((IMGS, D), F32),
        pltpu.VMEM((IMGS, D), F32),
        pltpu.VMEM((IMGS, HID), F32),
        pltpu.VMEM((IMGS, HID), F32),
        pltpu.VMEM((16, HALF), F32),
        pltpu.VMEM((1, HID), F32),
        pltpu.VMEM((8, TOKS), F32),
        pltpu.VMEM((CHUNKS, TOKS), F32),
        pltpu.VMEM((CHUNKS, TOKS), F32),
        pltpu.VMEM((256, 128), F32),
        pltpu.VMEM((256, HALF), F32),
        pltpu.VMEM((2, 8, 16, HALF), BF16),
        pltpu.VMEM((GROUPS, 8, 16, 384), BF16),
        pltpu.VMEM((2, 8, 16, msg), BF16),
        pltpu.VMEM((CHUNKS, 4, 2, 192, TOKS), BF16),
        pltpu.VMEM((CHUNKS, 192, TOKS), BF16),
        pltpu.VMEM((CHUNKS, 192, TOKS), BF16),
        pltpu.VMEM((CHUNKS, 2, 192, TOKS), BF16),
        pltpu.VMEM((CHUNKS, 2, 192, TOKS), BF16),
        pltpu.VMEM((CHUNKS, 192, TOKS), BF16),
        pltpu.VMEM((PAIR_FIRST, 4, 192, TOKS), BF16),
        pltpu.VMEM((3, 4, 2, 2, 96, 256), BF16),
        pltpu.VMEM((3, 4, 2, 96, 256), BF16),
        pltpu.VMEM((3, 4, 2, 96, 256), BF16),
        pltpu.VMEM((3, 96, 256), BF16),
        pltpu.VMEM((3, 96, 256), BF16),
        pltpu.VMEM((3, 2, 96, 256), BF16),
        pltpu.VMEM((3, 2, 96, 256), BF16),
        pltpu.VMEM((3, 96, 256), BF16),
        pltpu.VMEM((192, ROWS), BF16),
        pltpu.VMEM((96, HID), BF16),
        pltpu.VMEM((96, HID), BF16),
        pltpu.VMEM((IMGS, D), BF16),
        pltpu.SemaphoreType.DMA((CHUNKS,)),
        pltpu.SemaphoreType.DMA((7,)),
        pltpu.SemaphoreType.DMA((8,)),
        pltpu.SemaphoreType.DMA((9,)),
        pltpu.SemaphoreType.DMA((GROUPS, 8)),
        pltpu.SemaphoreType.DMA((GROUPS, 8)),
        pltpu.SemaphoreType.DMA((8,)),
        pltpu.SemaphoreType.DMA((9,)),
        pltpu.SemaphoreType.DMA((CHUNKS, 7)),
        pltpu.SemaphoreType.DMA((CHUNKS, 7)),
        pltpu.SemaphoreType.DMA((3, 6)),
        pltpu.SemaphoreType.DMA((3, 6)),
        pltpu.SemaphoreType.DMA((CHUNKS + 3,)),
    ]
    shapes = (
        jax.ShapeDtypeStruct((D // 8, ROWS), BF16),
        jax.ShapeDtypeStruct((D // 16, HID), BF16),
        jax.ShapeDtypeStruct((D // 16, HID), BF16),
        jax.ShapeDtypeStruct((IMGS, D), BF16),
    )
    results = pl.pallas_call(
        kernel,
        out_shape=shapes,
        in_specs=[hbm, hbm, hbm, vmem, smem, smem, smem],
        out_specs=(hbm, hbm, hbm, hbm),
        scratch_shapes=scratch,
        compiler_params=pltpu.CompilerParams(
            collective_id=0, has_side_effects=True, vmem_limit_bytes=61 * 2**20
        ),
        cost_estimate=pl.CostEstimate(
            flops=6 * ROWS * D * HID, bytes_accessed=14 * 2**20, transcendentals=2 * ROWS * HID
        ),
    )(tokens, w_in, w_out, text_emb, labels, logit_scale, logit_bias)
    token_t, w_in_grad, w_out_t, text_grad = pl.pallas_call(
        hand_out,
        out_shape=shapes,
        in_specs=[vmem, vmem, vmem, vmem],
        out_specs=(vmem, vmem, vmem, vmem),
        compiler_params=pltpu.CompilerParams(vmem_limit_bytes=61 * 2**20),
        cost_estimate=pl.CostEstimate(flops=0, bytes_accessed=2 * 2**20, transcendentals=0),
    )(*results)
    return token_t.T, w_in_grad, w_out_t.T, text_grad


def solution(mesh):
    in_specs = (
        P("dp", None),
        P(None, "tensor"),
        P("tensor", None),
        P("dp", None),
        P("dp"),
        P(),
        P(),
    )
    out_specs = (P("dp", "tensor"), P("dp", "tensor"), P("tensor", "dp"), P("dp", None))
    return jax.shard_map(body, mesh=mesh, in_specs=in_specs, out_specs=out_specs, check_vma=False)
```

```python
import math

import jax
import jax.numpy as jnp
from jax import lax
from jax.experimental import pallas as pl
from jax.experimental.pallas import tpu as pltpu
from jax.sharding import PartitionSpec as P

F32 = jnp.float32
BF16 = jnp.bfloat16

D = 1536
HALF = D // 2
HID = 768
ROWS = 2048
TOKS = 256
IMGS = 8
LOSS_SCALE = 64.0
EPS = 1e-06
GELU_A = math.sqrt(2.0 / math.pi)
GELU_B = 0.044715

CHUNKS = 8
GROUPS = 2
PER = CHUNKS // GROUPS
PAIR_FIRST = 3

NN = (((1,), (0,)), ((), ()))
NT = (((1,), (1,)), ((), ()))
TN = (((0,), (0,)), ((), ()))


def dot(a, b, dims=NN):
    return lax.dot_general(a, b, dims, preferred_element_type=F32)


def kernel(
    tokens_hbm, w_in_hbm, w_out_hbm, text_hbm, labels_hbm, scale_ref, bias_ref,
    out_hbm, win_hbm, wout_hbm, tgrad_hbm,
    tok, inv, hpre, hs, cur, nxt, tok_t, w_in, w_out,
    tmean, mlp_out, pooled, pgs, egs, csum, sums, inv_t, shift_t, eg_t, tdir,
    texts, ebuf, msgs,
    q, ra, rb, sa, sb, yr, yq,
    g, gc, gx, gra, grb, gsa, gsb, gyr,
    out, win, wout, tgrad, text_ref, labels_ref,
    tok_sem, w_sem,
    text_ss, text_rs, emb_ss, emb_rs, msg_ss, msg_rs,
    q_ss, q_rs, g_ss, g_rs, out_sem,
):
    dp = lax.axis_index("dp")
    tp = lax.axis_index("tensor")
    yh, local = dp // 8, dp % 8
    x, core = local // 2, dp % 2
    z, y = tp // 2, tp % 2

    def mesh_z(step):
        return (dp, ((z + step) % 4) * 2 + y)

    def mesh_x(step):
        return (yh * 8 + ((x + step) % 4) * 2 + core, tp)

    y_pair = (dp, z * 2 + (1 - y))
    core_pair = (dp - core + (1 - core), tp)
    y_far = ((1 - yh) * 8 + local, tp)

    def remote(src, dst, ssem, rsem, dev):
        return pltpu.make_async_remote_copy(
            src_ref=src, dst_ref=dst, send_sem=ssem, recv_sem=rsem,
            device_id=dev, device_id_type=pl.DeviceIdType.MESH,
        )

    def tok_copy(c):
        rows = pl.ds(c * TOKS, TOKS)
        return pltpu.make_async_copy(tokens_hbm.at[rows], tok.at[rows], tok_sem.at[c])

    def w_in_copy(k):
        feats = pl.ds(k * 256, 256)
        return pltpu.make_async_copy(w_in_hbm.at[feats], w_in.at[feats], w_sem.at[k])

    w_out_copy = pltpu.make_async_copy(w_out_hbm, w_out, w_sem.at[6])
    text_copy = pltpu.make_async_copy(text_hbm, text_ref, w_sem.at[7])
    labels_copy = pltpu.make_async_copy(labels_hbm, labels_ref, w_sem.at[8])
    text_copy.start()
    tok_copy(0).start()
    for k in range(6):
        w_in_copy(k).start()
    tok_copy(1).start()
    labels_copy.start()

    barrier = pltpu.get_barrier_semaphore()

    def greet(dev):
        pl.semaphore_signal(barrier, inc=1, device_id=dev, device_id_type=pl.DeviceIdType.MESH)

    greet(y_far)
    greet(core_pair)
    for k in range(1, 4):
        greet(mesh_x(k))
    for k in range(1, 8):
        greet((dp, (tp + k) % 8))

    mine, far = yh * 4 + x, (1 - yh) * 4 + x
    text_copy.wait()
    text_vals = text_ref[...].astype(F32)
    text_inv = lax.rsqrt(jnp.sum(text_vals * text_vals, axis=1, keepdims=True) + EPS)
    text_nrm = text_vals * text_inv
    texts[core, mine] = jnp.concatenate([text_nrm[:, :HALF], text_nrm[:, HALF:]], axis=0).astype(BF16)
    tmean[...] = jnp.zeros_like(tmean)
    mlp_out[...] = jnp.zeros_like(mlp_out)
    pooled[...] = jnp.zeros_like(pooled)

    def gather_far(buf, ss, rs):
        return remote(buf.at[core, mine], buf.at[core, mine], ss.at[0], rs.at[mine], y_far)

    def gather_x(buf, slot, k, ss, rs, first):
        block = buf.at[core, slot]
        return remote(block, block, ss.at[first + k], rs.at[slot], mesh_x(k))

    def gather_core(buf, ss, rs):
        return remote(buf.at[core], buf.at[core], ss.at[7], rs.at[8], core_pair)

    def gather_first(buf, ss, rs):
        gather_far(buf, ss, rs).start()
        for k in range(1, 4):
            gather_x(buf, mine, k, ss, rs, 0).start()

    def gather_relay(buf, ss, rs):
        gather_x(buf, far, 1, ss, rs, 3).wait_recv()
        for k in range(1, 4):
            gather_x(buf, far, k, ss, rs, 3).start()

    def gather_pass(buf, ss, rs):
        for k in range(1, 4):
            for side in range(2):
                gather_x(buf, side * 4 + (x + k) % 4, k, ss, rs, 0).wait_recv()
        gather_core(buf, ss, rs).start()

    def gather_rest(buf, ss, rs):
        remote(buf.at[1 - core], buf.at[1 - core], ss.at[7], rs.at[8], core_pair).wait_recv()

    def gather_sent(buf, ss, rs):
        gather_far(buf, ss, rs).wait_send()
        for k in range(1, 4):
            gather_x(buf, mine, k, ss, rs, 0).wait_send()
            gather_x(buf, far, k, ss, rs, 3).wait_send()
        gather_core(buf, ss, rs).wait_send()

    def split(vals):
        top = vals.astype(BF16).astype(F32)
        return jnp.concatenate(
            [top, vals - top, jnp.zeros((14,) + vals.shape[1:], F32)], axis=0
        ).astype(BF16)

    def chunk_rows(c):
        return pl.ds(pl.multiple_of(c * TOKS, TOKS), TOKS)

    def forward(c):
        accs = [
            dot(tok[chunk_rows(c), :], w_in[0:D, j * 256:(j + 1) * 256]) for j in range(3)
        ]
        means, scales, shifts = [], [], []
        acc = jnp.zeros((8, D), F32)
        for b in range(TOKS // 16):
            rows = pl.ds(pl.multiple_of(c * TOKS + b * 16, 16), 16)
            vals = tok[rows, :].astype(F32)
            mean = jnp.sum(vals, axis=1, keepdims=True) * (1.0 / D)
            center = vals - mean
            var = jnp.sum(center * center, axis=1, keepdims=True) * (1.0 / D)
            scale = lax.rsqrt(var + EPS)
            shift = mean * scale
            inv[rows, :] = scale
            means.append(mean)
            scales.append(scale)
            shifts.append(shift)
            acc = acc + (vals[:8] + vals[8:])
        tok_t[0:D, chunk_rows(c)] = tok[chunk_rows(c), :].T
        lane = lax.broadcasted_iota(jnp.int32, (TOKS, 128), 1)
        trio = jnp.where(lane == 0, jnp.concatenate(scales, 0), jnp.concatenate(shifts, 0))
        trio = jnp.where(lane == 2, jnp.concatenate(means, 0), trio).T
        inv_t[pl.ds(c, 1), :] = trio[0:1, :]
        shift_t[pl.ds(c, 1), :] = trio[1:2, :]
        tok_t[D:D + 16, chunk_rows(c)] = split(trio[2:3, :])
        tmean[pl.ds(c, 1), :] = jnp.sum(acc, axis=0, keepdims=True) * (1.0 / TOKS)
        for j in range(3):
            cols = slice(j * 256, (j + 1) * 256)
            cs = csum[:, cols]
            acc = jnp.zeros((8, 256), F32)
            for b in range(TOKS // 16):
                rows = pl.ds(pl.multiple_of(c * TOKS + b * 16, 16), 16)
                h = accs[j][b * 16:(b + 1) * 16] * scales[b] - shifts[b] * cs
                hpre[rows, cols] = h
                t = jnp.tanh(h * (GELU_A + (GELU_A * GELU_B) * (h * h)))
                act = h + h * t
                acc = acc + (act[:8] + act[8:])
            pooled[pl.ds(c, 1), cols] = jnp.sum(acc, axis=0, keepdims=True) * (0.5 / TOKS)

    def emb_copy(n, k):
        return remote(
            ebuf.at[n, tp], ebuf.at[n, tp], emb_ss.at[n, k], emb_rs.at[n, tp], (dp, (tp + k) % 8)
        )

    def exchange_start(n):
        part = dot(pooled[...].astype(BF16), w_out[...])
        own = jnp.where(n == 0, part[:PER], part[PER:])
        ebuf[n, tp] = jnp.concatenate(
            [own[:, k * 384:(k + 1) * 384] for k in range(4)], axis=0
        ).astype(BF16)

        @pl.loop(1, 8)
        def _(k):
            emb_copy(n, k).start()

    def exchange_wait(n):
        @pl.loop(1, 8)
        def _(k):
            src = (tp + k) % 8
            remote(
                ebuf.at[n, src], ebuf.at[n, src], emb_ss.at[n, k], emb_rs.at[n, src], (dp, src)
            ).wait_recv()

    def both(sums):
        total = sums[:IMGS] + sums[IMGS:]
        return jnp.concatenate([total, total], axis=0)

    def loss(n):
        scale = scale_ref[0]
        tm = tmean[...]
        own = ebuf[n, 0].astype(F32)
        for k in range(1, 8):
            own = own + ebuf[n, k].astype(F32)
        own = jnp.concatenate([own[k * PER:(k + 1) * PER] for k in range(4)], axis=1)
        image = lax.broadcasted_iota(jnp.int32, (IMGS, D), 0)
        mlp = jnp.where(image // PER == n, jnp.concatenate([own, own], axis=0), mlp_out[...])
        mlp_out[...] = mlp
        full = tm + mlp
        emb = jnp.concatenate([full[:, :HALF], full[:, HALF:]], axis=0)
        emb_inv = lax.rsqrt(both(jnp.sum(emb * emb, axis=1, keepdims=True)) + EPS)
        image_bf = (emb * emb_inv).astype(BF16)
        text_all = texts[...].reshape(256, HALF)
        prod = dot(image_bf, text_all, NT)
        logits = scale * (prod[:IMGS] + pltpu.roll(prod[IMGS:], 256 - IMGS, 1)) + bias_ref[0]
        lane = lax.broadcasted_iota(jnp.int32, (IMGS, 256), 1)
        row = lax.broadcasted_iota(jnp.int32, (IMGS, 256), 0)
        valid = (lane % 16) < 8
        slot = lane // 16
        text_id = ((slot // 4) % 2 * 8 + slot % 4 * 2 + slot // 8) * 8 + lane % 16
        label = jnp.zeros((IMGS, 256), jnp.int32)
        for k in range(IMGS):
            label = jnp.where(row == k, labels_ref[k], label)
        signs = jnp.where(label == text_id, 1.0, -1.0)
        grad = -signs * jax.nn.sigmoid(-signs * logits) * LOSS_SCALE
        grad = jnp.where(valid, grad, 0.0)
        grad = jnp.concatenate([grad, pltpu.roll(grad, IMGS, 1)], axis=0).astype(BF16)
        image_dir = scale * dot(grad, text_all)
        emb_grad = emb_inv * image_dir - (emb_inv * emb_inv * emb_inv) * emb * both(
            jnp.sum(emb * image_dir, axis=1, keepdims=True)
        )
        eg_bf = emb_grad.astype(BF16)
        pgs[...] = (
            dot(eg_bf[:IMGS], w_out[:, :HALF], NT) + dot(eg_bf[IMGS:], w_out[:, HALF:], NT)
        ) * (1.0 / TOKS)
        egs[...] = emb_grad * (1.0 / TOKS)
        msgs[core, mine, :, 0:HALF] = image_bf
        msgs[core, mine, :, HALF:D] = eg_bf
        pooled_f = pooled[...]
        msgs[core, mine, :, D:D + HID] = jnp.concatenate([pooled_f, pooled_f], axis=0).astype(BF16)
        msgs[core, mine, :, D + HID:D + HID + 256] = grad

    def hidden_rows(c):
        half_pg = 0.5 * pgs[pl.ds(c, 1), :]
        second = []
        for b in range(TOKS // 16):
            rows = pl.ds(pl.multiple_of(c * TOKS + b * 16, 16), 16)
            h = hpre[rows, :]
            h2 = h * h
            t = jnp.tanh(h * (GELU_A + (GELU_A * GELU_B) * h2))
            slope = (1.0 + t) + h * (1.0 - t * t) * (GELU_A + (3.0 * GELU_A * GELU_B) * h2)
            grad_bf = (slope * half_pg * inv[rows, :]).astype(BF16)
            hs[rows, :] = grad_bf
            nxt[b * 16:(b + 1) * 16, :] = grad_bf
            p2 = grad_bf.astype(F32) * h
            s2 = p2[:, 0:128]
            for i in range(1, HID // 128):
                s2 = s2 + p2[:, i * 128:(i + 1) * 128]
            second.append(s2)
        m2 = jnp.sum(jnp.concatenate(second, axis=0).T, axis=0, keepdims=True) * (1.0 / D)
        sums[0:1, :] = inv_t[pl.ds(c, 1), :] * m2
        sums[1:2, :] = shift_t[pl.ds(c, 1), :] * m2

    def feature_rows(c):
        rows = chunk_rows(c)
        full = dot(w_in[...], cur[...], NT)
        slope = sums[0:1, :]
        shift = (full[D:D + 1] + full[D + 1:D + 2]) * (1.0 / D) - sums[1:2, :]
        for k in range(8):
            feats = slice(k * 192, (k + 1) * 192)
            block = full[feats] - tok_t[feats, rows].astype(F32) * slope - shift
            q[c, k // 2, k % 2] = block.astype(BF16)

    zp, zn, zo = (z + 1) % 4, (z + 3) % 4, (z + 2) % 4
    up, down = mesh_z(1), mesh_z(3)
    lo, hi = pl.ds(0, 96), pl.ds(96, 96)

    def add_into(dst, a, b):
        dst[...] = (a[...].astype(F32) + b[...].astype(F32)).astype(BF16)

    def pair_copy(c):
        return remote(q.at[c, :, 1 - y], yq.at[c // 2], q_ss.at[c, 0], q_rs.at[c, 0], y_pair)

    def pair_ring1(c):
        return (
            remote(q.at[c, zo, y, lo], ra.at[c, lo], q_ss.at[c, 1], q_rs.at[c, 1], up),
            remote(q.at[c, zo, y, hi], rb.at[c, lo], q_ss.at[c, 2], q_rs.at[c, 2], down),
            remote(q.at[c, zp, y, hi], sa.at[c, 0, hi], q_ss.at[c, 3], q_rs.at[c, 3], up),
            remote(q.at[c, zn, y, lo], sb.at[c, 0, lo], q_ss.at[c, 4], q_rs.at[c, 4], down),
        )

    def pair_ring2(c):
        return (
            remote(q.at[c, zp, y, lo], sa.at[c, 0, lo], q_ss.at[c, 5], q_rs.at[c, 5], up),
            remote(q.at[c, zn, y, hi], sb.at[c, 0, hi], q_ss.at[c, 6], q_rs.at[c, 6], down),
        )

    def ring1(c):
        return (
            remote(q.at[c, zo, 0], ra.at[c], q_ss.at[c, 1], q_rs.at[c, 1], up),
            remote(q.at[c, zo, 1], rb.at[c], q_ss.at[c, 2], q_rs.at[c, 2], down),
            remote(q.at[c, zp, 1], sa.at[c, 1], q_ss.at[c, 3], q_rs.at[c, 3], up),
            remote(q.at[c, zn, 0], sb.at[c, 0], q_ss.at[c, 4], q_rs.at[c, 4], down),
        )

    def ring2(c):
        return (
            remote(q.at[c, zp, 0], sa.at[c, 0], q_ss.at[c, 5], q_rs.at[c, 5], up),
            remote(q.at[c, zn, 1], sb.at[c, 1], q_ss.at[c, 6], q_rs.at[c, 6], down),
        )

    def ring_pair(c):
        return remote(q.at[c, z, 1 - y], yr.at[c], q_ss.at[c, 0], q_rs.at[c, 0], y_pair)

    def start(copies):
        for copy in copies:
            copy.start()

    def pair_b(c):
        pair_copy(c).wait_recv()

        @pl.loop(0, 4)
        def _(zb):
            blk = q.at[c, zb, y]
            add_into(blk, blk, yq.at[c // 2, zb])

        start(pair_ring1(c))

    def ring_b(c):
        first, second = ring1(c)[:2]
        first.wait_recv()
        add_into(q.at[c, zp, 0], q.at[c, zp, 0], ra.at[c])
        second.wait_recv()
        add_into(q.at[c, zn, 1], q.at[c, zn, 1], rb.at[c])
        start(ring2(c))

    def pair_c(c):
        first, second = pair_ring1(c)[:2]
        first.wait_recv()
        add_into(q.at[c, zp, y, lo], q.at[c, zp, y, lo], ra.at[c, lo])
        second.wait_recv()
        add_into(q.at[c, zn, y, hi], q.at[c, zn, y, hi], rb.at[c, lo])
        start(pair_ring2(c))

    def ring_c(c):
        for copy in ring1(c)[2:] + ring2(c):
            copy.wait_recv()

        @pl.loop(0, 2)
        def _(half):
            blk = q.at[c, z, half]
            blk[...] = (
                blk[...].astype(F32) + sa[c, half].astype(F32) + sb[c, half].astype(F32)
            ).astype(BF16)

        ring_pair(c).start()

    def out_copy(c):
        rows = chunk_rows(c)
        return pltpu.make_async_copy(out.at[:, rows], out_hbm.at[:, rows], out_sem.at[c])

    def finish(c, total):
        lane = lax.broadcasted_iota(jnp.int32, (192, 128), 1)
        col = jnp.sum(jnp.where(lane == c, eg_t[0:192, :], 0.0), axis=1, keepdims=True)
        out[:, chunk_rows(c)] = (total + col).astype(BF16)
        out_copy(c).start()

    def pair_d(c):
        for copy in pair_ring1(c)[2:] + pair_ring2(c):
            copy.wait_recv()
        finish(c, q[c, z, y].astype(F32) + sa[c, 0].astype(F32) + sb[c, 0].astype(F32))

    def ring_d(c):
        ring_pair(c).wait_recv()
        finish(c, q[c, z, y].astype(F32) + yr[c].astype(F32))

    xp, xn, xo = (x + 1) % 4, (x + 3) % 4, (x + 2) % 4
    right, left = mesh_x(1), mesh_x(3)

    def core_copy(j):
        return remote(g.at[j, :, :, 1 - core], gc.at[j], g_ss.at[j, 0], g_rs.at[j, 0], core_pair)

    def g1(j):
        return (
            remote(gx.at[j, xo, 0], gra.at[j], g_ss.at[j, 1], g_rs.at[j, 1], right),
            remote(gx.at[j, xo, 1], grb.at[j], g_ss.at[j, 2], g_rs.at[j, 2], left),
        )

    def g2(j):
        return (
            remote(gx.at[j, xp], gsa.at[j], g_ss.at[j, 3], g_rs.at[j, 3], right),
            remote(gx.at[j, xn], gsb.at[j], g_ss.at[j, 4], g_rs.at[j, 4], left),
        )

    def g3(j):
        return remote(gx.at[j, x, 1 - yh], gyr.at[j], g_ss.at[j, 5], g_rs.at[j, 5], y_far)

    def weight_a(j):
        cols = pl.ds(pl.multiple_of(j * 256, 256), 256)
        full = dot(tok_t[...], hs[:, cols])
        lift = full[D:D + 1] + full[D + 1:D + 2]
        g[j] = (full[:D] - lift).astype(BF16).reshape(4, 2, 2, 96, 256)
        core_copy(j).start()

    def weight_b(j):
        core_copy(j).wait_recv()

        @pl.loop(0, 8)
        def _(k):
            xb, yb = k // 2, k % 2
            i, m = yb * 2 + xb // 2, xb % 2
            add_into(gx.at[j, xb, yb], g.at[j, i, m, core], gc.at[j, i, m])

        start(g1(j))

    def weight_c(j):
        first, second = g1(j)
        first.wait_recv()
        add_into(gx.at[j, xp, 0], gx.at[j, xp, 0], gra.at[j])
        second.wait_recv()
        add_into(gx.at[j, xn, 1], gx.at[j, xn, 1], grb.at[j])
        start(g2(j))

    def weight_d(j):
        for copy in g2(j):
            copy.wait_recv()
        for half in range(2):
            blk = gx.at[j, x, half]
            blk[...] = (
                blk[...].astype(F32) + gsa[j, half].astype(F32) + gsb[j, half].astype(F32)
            ).astype(BF16)
        g3(j).start()

    def weight_e():
        for j in range(3):
            g3(j).wait_recv()
            win[:, j * 256:(j + 1) * 256] = (
                gx[j, x, yh].astype(F32) + gyr[j].astype(F32)
            ).astype(BF16)
        small_out(win, win_hbm, 0).start()

    def small_out(src, dst, k):
        return pltpu.make_async_copy(src, dst, out_sem.at[CHUNKS + k])

    def gathered():
        gather_rest(msgs, msg_ss, msg_rs)
        all_msgs = msgs[...].reshape(256, D + HID + 256)
        tdir[...] = dot(all_msgs[:, D + HID:], all_msgs[:, :HALF], TN)
        text_dir = scale_ref[0] * tdir[pl.ds(pl.multiple_of((core * 8 + mine) * 16, 16), 16), :]
        text_dir = jnp.concatenate([text_dir[:IMGS], text_dir[IMGS:]], axis=1)
        vals = text_ref[...].astype(F32)
        t_inv = lax.rsqrt(jnp.sum(vals * vals, axis=1, keepdims=True) + EPS)
        tgrad[...] = (
            t_inv * text_dir
            - (t_inv * t_inv * t_inv) * vals * jnp.sum(vals * text_dir, axis=1, keepdims=True)
        ).astype(BF16)
        small_out(tgrad, tgrad_hbm, 1).start()
        feat = lax.broadcasted_iota(jnp.int32, (HALF, 128), 0)
        col = lax.broadcasted_iota(jnp.int32, (HALF, 128), 1)
        pick = jnp.where(feat == col + local * 96, 1.0, 0.0).astype(BF16)
        emb_cols = dot(all_msgs[:, HALF:D], pick)
        slot_row = lax.broadcasted_iota(jnp.int32, (256, 128), 0)
        emb_cols = jnp.where((slot_row // 8) % 2 == yh, emb_cols, 0.0).astype(BF16)
        wout[...] = dot(emb_cols, all_msgs[:, D:D + HID], TN)[:96].astype(BF16)
        small_out(wout, wout_hbm, 2).start()

    def own_columns():
        cols = egs[pl.ds(pl.multiple_of((z // 2) * 8, 8), 8),
                   pl.ds(pl.multiple_of((z % 2) * 384, 128), 384)]
        cols = jnp.where(y == 0, cols[:, :192], cols[:, 192:])
        square = jnp.concatenate([cols, jnp.zeros((8, 64), F32)], axis=1)
        square = jnp.concatenate([square, jnp.zeros((120, 256), F32)], axis=0)
        eg_t[...] = square.T

    cs = jnp.zeros((16, HID), F32)
    for k in range(6):
        w_in_copy(k).wait()
        cs = cs + dot(jnp.full((16, 256), 1.0, BF16), w_in[k * 256:(k + 1) * 256, :])
    cs = cs[0:1]

    @pl.loop(2, CHUNKS)
    def _(c):
        tok_copy(c).start()

    w_out_copy.start()
    csum[...] = cs
    w_in[D:D + 16, :] = split(cs)
    pl.semaphore_wait(barrier, 12)
    gather_first(texts, text_ss, text_rs)

    def is_pair(c):
        return (c % 2 == 1) & (c < 6)

    def forward_loop(first, last):
        @pl.loop(first, last)
        def _(c):
            tok_copy(c).wait()
            forward(c)

    @pl.loop(0, 3)
    def _(stage):
        @pl.when(stage < 2)
        def _():
            @pl.loop(5 * stage, 4 + 4 * stage)
            def _(c):
                tok_copy(c).wait()
                forward(c)

                @pl.when(c == 5)
                def _():
                    ring_b(0)

            @pl.when(stage == 0)
            def _():
                w_out_copy.wait()
                labels_copy.wait()

            exchange_start(stage)

        @pl.when(stage == 0)
        def _():
            gather_relay(texts, text_ss, text_rs)
            forward_loop(4, 5)
            gather_pass(texts, text_ss, text_rs)

        @pl.when(stage != 1)
        def _():
            n = stage // 2
            exchange_wait(n)

            @pl.when(n == 0)
            def _():
                gather_rest(texts, text_ss, text_rs)

            loss(n)

            @pl.when(n == 1)
            def _():
                gather_first(msgs, msg_ss, msg_rs)
                pair_b(1)
                ring_b(2)

            hidden_rows(n * PER)

        @pl.loop(2 * stage, 2 * stage + 2 + 2 * (stage // 2))
        def _(c):
            cur[...] = nxt[...]
            feature_rows(c)

            @pl.when(is_pair(c))
            def _():
                pair_copy(c).start()

            @pl.when(jnp.logical_not(is_pair(c)))
            def _():
                start(ring1(c))

            hidden_rows(c + 1 - (c % 4) // 3)

            @pl.when(c == 2)
            def _():
                ring_c(0)

            @pl.when(c == 5)
            def _():
                pair_c(1)

            @pl.when(c == 6)
            def _():
                ring_c(2)
                gather_relay(msgs, msg_ss, msg_rs)

            @pl.when(c == 7)
            def _():
                ring_b(4)

    own_columns()

    @pl.loop(0, 3)
    def _(j):
        weight_a(j)

        @pl.when(j == 0)
        def _():
            ring_b(6)
            gather_pass(msgs, msg_ss, msg_rs)

        @pl.when(j == 1)
        def _():
            pair_b(3)
            weight_b(0)

        @pl.when(j == 2)
        def _():
            ring_b(7)
            ring_c(4)

    weight_b(1)
    weight_c(0)
    pair_c(3)
    weight_b(2)
    ring_d(0)
    pair_d(1)
    gathered()
    pair_b(5)
    ring_c(6)
    weight_c(1)
    weight_d(0)
    weight_c(2)
    ring_d(2)
    pair_c(5)
    ring_c(7)
    weight_d(1)
    pair_d(3)
    weight_d(2)
    ring_d(4)
    ring_d(6)
    weight_e()
    pair_d(5)
    ring_d(7)

    @pl.loop(0, CHUNKS)
    def _(c):
        out_copy(c).wait()

        @pl.when(is_pair(c))
        def _():
            for copy in (pair_copy(c),) + pair_ring1(c) + pair_ring2(c):
                copy.wait_send()

        @pl.when(jnp.logical_not(is_pair(c)))
        def _():
            for copy in (ring_pair(c),) + ring1(c) + ring2(c):
                copy.wait_send()

    @pl.loop(0, 3)
    def _(j):
        for copy in (core_copy(j), g3(j)) + g1(j) + g2(j):
            copy.wait_send()

    @pl.loop(1, 8)
    def _(k):
        for n in range(GROUPS):
            emb_copy(n, k).wait_send()

    gather_sent(texts, text_ss, text_rs)
    gather_sent(msgs, msg_ss, msg_rs)
    small_out(win, win_hbm, 0).wait()
    small_out(tgrad, tgrad_hbm, 1).wait()
    small_out(wout, wout_hbm, 2).wait()


def hand_out(a, b, c, d, a_out, b_out, c_out, d_out):
    a_out[...] = a[...]
    b_out[...] = b[...]
    c_out[...] = c[...]
    d_out[...] = d[...]


def body(tokens, w_in, w_out, text_emb, labels, logit_scale, logit_bias):
    vmem = pl.BlockSpec(memory_space=pltpu.VMEM)
    hbm = pl.BlockSpec(memory_space=pl.ANY)
    msg = D + HID + 256
    scratch = [
        pltpu.VMEM((ROWS, D), BF16),
        pltpu.VMEM((ROWS, 1), F32),
        pltpu.VMEM((ROWS, HID), F32),
        pltpu.VMEM((ROWS, HID), BF16),
        pltpu.VMEM((TOKS, HID), BF16),
        pltpu.VMEM((TOKS, HID), BF16),
        pltpu.VMEM((D + 16, ROWS), BF16),
        pltpu.VMEM((D + 16, HID), BF16),
        pltpu.VMEM((HID, D), BF16),
        pltpu.VMEM((IMGS, D), F32),
        pltpu.VMEM((IMGS, D), F32),
        pltpu.VMEM((IMGS, HID), F32),
        pltpu.VMEM((IMGS, HID), F32),
        pltpu.VMEM((16, HALF), F32),
        pltpu.VMEM((1, HID), F32),
        pltpu.VMEM((8, TOKS), F32),
        pltpu.VMEM((CHUNKS, TOKS), F32),
        pltpu.VMEM((CHUNKS, TOKS), F32),
        pltpu.VMEM((256, 128), F32),
        pltpu.VMEM((256, HALF), F32),
        pltpu.VMEM((2, 8, 16, HALF), BF16),
        pltpu.VMEM((GROUPS, 8, 16, 384), BF16),
        pltpu.VMEM((2, 8, 16, msg), BF16),
        pltpu.VMEM((CHUNKS, 4, 2, 192, TOKS), BF16),
        pltpu.VMEM((CHUNKS, 192, TOKS), BF16),
        pltpu.VMEM((CHUNKS, 192, TOKS), BF16),
        pltpu.VMEM((CHUNKS, 2, 192, TOKS), BF16),
        pltpu.VMEM((CHUNKS, 2, 192, TOKS), BF16),
        pltpu.VMEM((CHUNKS, 192, TOKS), BF16),
        pltpu.VMEM((PAIR_FIRST, 4, 192, TOKS), BF16),
        pltpu.VMEM((3, 4, 2, 2, 96, 256), BF16),
        pltpu.VMEM((3, 4, 2, 96, 256), BF16),
        pltpu.VMEM((3, 4, 2, 96, 256), BF16),
        pltpu.VMEM((3, 96, 256), BF16),
        pltpu.VMEM((3, 96, 256), BF16),
        pltpu.VMEM((3, 2, 96, 256), BF16),
        pltpu.VMEM((3, 2, 96, 256), BF16),
        pltpu.VMEM((3, 96, 256), BF16),
        pltpu.VMEM((192, ROWS), BF16),
        pltpu.VMEM((96, HID), BF16),
        pltpu.VMEM((96, HID), BF16),
        pltpu.VMEM((IMGS, D), BF16),
        pltpu.VMEM((IMGS, D), BF16),
        pltpu.SMEM((IMGS,), jnp.int32),
        pltpu.SemaphoreType.DMA((CHUNKS,)),
        pltpu.SemaphoreType.DMA((9,)),
        pltpu.SemaphoreType.DMA((8,)),
        pltpu.SemaphoreType.DMA((9,)),
        pltpu.SemaphoreType.DMA((GROUPS, 8)),
        pltpu.SemaphoreType.DMA((GROUPS, 8)),
        pltpu.SemaphoreType.DMA((8,)),
        pltpu.SemaphoreType.DMA((9,)),
        pltpu.SemaphoreType.DMA((CHUNKS, 7)),
        pltpu.SemaphoreType.DMA((CHUNKS, 7)),
        pltpu.SemaphoreType.DMA((3, 6)),
        pltpu.SemaphoreType.DMA((3, 6)),
        pltpu.SemaphoreType.DMA((CHUNKS + 3,)),
    ]
    shapes = (
        jax.ShapeDtypeStruct((D // 8, ROWS), BF16),
        jax.ShapeDtypeStruct((D // 16, HID), BF16),
        jax.ShapeDtypeStruct((D // 16, HID), BF16),
        jax.ShapeDtypeStruct((IMGS, D), BF16),
    )
    results = pl.pallas_call(
        kernel,
        out_shape=shapes,
        in_specs=[hbm] * 5 + [pl.BlockSpec(memory_space=pltpu.SMEM)] * 2,
        out_specs=(hbm, hbm, hbm, hbm),
        scratch_shapes=scratch,
        compiler_params=pltpu.CompilerParams(
            collective_id=0, has_side_effects=True, vmem_limit_bytes=61 * 2**20
        ),
        cost_estimate=pl.CostEstimate(
            flops=6 * ROWS * D * HID, bytes_accessed=14 * 2**20, transcendentals=2 * ROWS * HID
        ),
    )(tokens, w_in, w_out, text_emb, labels, logit_scale, logit_bias)
    token_t, w_in_grad, w_out_t, text_grad = pl.pallas_call(
        hand_out,
        out_shape=shapes,
        in_specs=[vmem, vmem, vmem, vmem],
        out_specs=(vmem, vmem, vmem, vmem),
        compiler_params=pltpu.CompilerParams(vmem_limit_bytes=61 * 2**20),
        cost_estimate=pl.CostEstimate(flops=0, bytes_accessed=2 * 2**20, transcendentals=0),
    )(*results)
    return token_t.T, w_in_grad, w_out_t.T, text_grad


def solution(mesh):
    in_specs = (
        P("dp", None),
        P(None, "tensor"),
        P("tensor", None),
        P("dp", None),
        P("dp"),
        P(),
        P(),
    )
    out_specs = (P("dp", "tensor"), P("dp", "tensor"), P("tensor", "dp"), P("dp", None))
    return jax.shard_map(body, mesh=mesh, in_specs=in_specs, out_specs=out_specs, check_vma=False)
```
